32 devices in a mesh: segment: 4 (over x, core), seq: 4 (over z), tp: 2 (over y).
Axes of the slice: x: 2, y: 2, z: 4, core: 2. Of those that a mesh axis runs over, the one named last changes fastest.
Arguments:
- pairs: bfloat16 [4, 1024, 2, 2048], P('segment', ('seq', 'tp')), may hold values from -4 to 4
- queries: bfloat16 [4, 1536, 2048], P('segment', None, ('seq', 'tp')), may hold values from -24 to 24
- upstream: bfloat16 [4, 1536, 2048], P('segment', None, ('seq', 'tp')), may hold values from -6 to 6
Outputs:
- context: bfloat16 [4, 1536, 2048], P('segment', None, ('seq', 'tp'))
- grad_query: bfloat16 [4, 1536, 2048], P('segment', None, ('seq', 'tp'))
- grad_pairs: bfloat16 [4, 1024, 2, 2048], P('segment', ('seq', 'tp'))
The draws below stay inside these ranges and needn't reach their ends.
All inputs are finite; a program needn't handle non-finite values.
Results may differ from the reference program's by a relative error of at most 0.011.
Values may be sent and summed in bfloat16 or wider, within the bound.
No kernel may reach another device: no remote copies, remote signals or barrier semaphores. Data moves between devices by JAX's collectives and lax.ppermute only.
A program may use at most 128 MiB of HBM per device.

```python
import jax
import jax.numpy as jnp
from jax import lax

HEAD = 128
HH = 2048
S_ENC = 1024
T_DEC = 1536
SECTIONS = 4


def draw_pairs(key, part):
    key = jax.random.fold_in(key, 3)
    shape = (SECTIONS, S_ENC, 2, HH)
    base = jnp.clip(jax.random.normal(key, shape, jnp.float32), -4.0, 4.0)
    return base.astype(jnp.bfloat16)


def draw_queries(key, part):
    key = jax.random.fold_in(key, 5)
    shape = (SECTIONS, T_DEC, HH)
    base = jnp.clip(jax.random.normal(key, shape, jnp.float32), -4.0, 4.0)
    return base.astype(jnp.bfloat16)


def levels(key, dims, shards, smallest, top_value):
    def one(dim, parts):
        heights = jax.random.uniform(jax.random.fold_in(jax.random.fold_in(key, 6), dim), (parts,), jnp.float32, smallest / len(shards), top_value / len(shards))
        return jnp.repeat(jnp.exp(heights), dims[dim] // parts).reshape((-1,) + (1,) * (len(dims) - dim - 1))

    gain = one(*shards[0])
    for cut in shards[1:]:
        gain = gain * one(*cut)
    return gain


def bell_draw(rng, shape, width, limit, pieces=(), dtype=jnp.bfloat16):
    entries = width * jax.random.normal(rng, shape, jnp.float32)
    if pieces:
        entries = entries * levels(rng, shape, pieces, -0.22, 0.18)
    return jnp.clip(entries, -limit, limit).astype(dtype)


def setup_inputs(seed: int = 0) -> dict:
    splits = jax.random.split(jax.random.key(seed), 4)
    return {
        "pairs": draw_pairs(jax.random.fold_in(splits[3], 71), 0),
        "queries": draw_queries(jax.random.fold_in(splits[3], 71), 0),
        "upstream": bell_draw(splits[2], (SECTIONS, T_DEC, HH), 1.0, 6.0, ((0, 4), (2, 8))),
    }


def one_head(inputs):
    query_head, key_head, value_head, grad_head = inputs
    factor = HEAD ** -0.5
    scores = jnp.dot(query_head, key_head.T, preferred_element_type=jnp.float32) * factor
    row_max = jnp.max(scores, axis=1, keepdims=True)
    raised = jnp.exp(scores - row_max)
    weights = raised / jnp.sum(raised, axis=1, keepdims=True)
    weights_low = weights.astype(jnp.bfloat16)
    full_context = jnp.dot(weights_low, value_head, preferred_element_type=jnp.float32)
    row_dot = jnp.sum(grad_head.astype(jnp.float32) * full_context, axis=1, keepdims=True)
    grad_weights = jnp.dot(grad_head, value_head.T, preferred_element_type=jnp.float32)
    grad_scores = (weights * (grad_weights - row_dot) * factor).astype(jnp.bfloat16)
    grad_q = jnp.dot(grad_scores, key_head, preferred_element_type=jnp.float32).astype(jnp.bfloat16)
    grad_k = jnp.dot(grad_scores.T, query_head, preferred_element_type=jnp.float32).astype(jnp.bfloat16)
    grad_v = jnp.dot(weights_low.T, grad_head, preferred_element_type=jnp.float32).astype(jnp.bfloat16)
    return full_context.astype(jnp.bfloat16), grad_q, grad_k, grad_v


def by_head(array, sections, rows, num_heads):
    return array.reshape(sections, rows, num_heads, HEAD).transpose(0, 2, 1, 3).reshape(sections * num_heads, rows, HEAD)


def from_heads(array, sections, rows, num_heads):
    return array.reshape(sections, num_heads, rows, HEAD).transpose(0, 2, 1, 3).reshape(sections, rows, num_heads * HEAD)


def reference(pairs, queries, upstream):
    sections = queries.shape[0]
    num_heads = HH // HEAD
    rolled = jnp.roll(pairs, 1, axis=0)
    query_all = by_head(queries, sections, T_DEC, num_heads)
    grad_all = by_head(upstream, sections, T_DEC, num_heads)
    key_all = by_head(rolled[:, :, 0, :], sections, S_ENC, num_heads)
    value_all = by_head(rolled[:, :, 1, :], sections, S_ENC, num_heads)
    context, grad_query, grad_keys, grad_values = lax.map(one_head, (query_all, key_all, value_all, grad_all))
    context = from_heads(context, sections, T_DEC, num_heads)
    grad_query = from_heads(grad_query, sections, T_DEC, num_heads)
    grad_keys = from_heads(grad_keys, sections, S_ENC, num_heads)
    grad_values = from_heads(grad_values, sections, S_ENC, num_heads)
    grad_pairs = jnp.roll(jnp.stack([grad_keys, grad_values], axis=2), -1, axis=0)
    return context, grad_query, grad_pairs
```

```python
import jax
import jax.numpy as jnp
from jax import lax
from jax.sharding import PartitionSpec as P

HEAD = 128
AXES = ("segment", "seq", "tp")


def offsets():
    seq_count = lax.axis_size("seq")
    tp_count = lax.axis_size("tp")
    pairs = [(dz, dy) for dz in range(seq_count) for dy in range(tp_count)]
    middle = seq_count / 2
    return sorted(pairs, key=lambda o: (abs(o[0] - middle), -o[1]))


def group_at(offset):
    seq_count = lax.axis_size("seq")
    tp_count = lax.axis_size("tp")
    z = lax.rem(lax.axis_index("seq") + offset[0], seq_count)
    y = lax.rem(lax.axis_index("tp") + offset[1], tp_count)
    return z * tp_count + y


def route(offset, back):
    segments, seq_count, tp_count = (lax.axis_size(a) for a in AXES)
    hops = []
    for s in range(segments):
        for z in range(seq_count):
            for y in range(tp_count):
                source = (s * seq_count + z) * tp_count + y
                s_to = (s + 1) % segments
                z_to = (z + offset[0]) % seq_count
                y_to = (y + offset[1]) % tp_count
                target = (s_to * seq_count + z_to) * tp_count + y_to
                hops.append((target, source) if back else (source, target))
    return hops


def attend(head_pairs, query_rows, grad_rows):
    enc_len = head_pairs.shape[0]
    local = head_pairs.shape[2]
    num_heads = local // HEAD
    dec_len = query_rows.shape[0]
    block = min(512, dec_len)
    count = dec_len // block
    factor = HEAD ** (-0.5)
    keys_all = head_pairs[:, 0, :].reshape(enc_len, num_heads, HEAD)
    values_all = head_pairs[:, 1, :].reshape(enc_len, num_heads, HEAD)
    query_blocks = query_rows.reshape(count, block, num_heads, HEAD)
    grad_blocks = grad_rows.reshape(count, block, num_heads, HEAD)

    def step(carry, inputs):
        grad_keys, grad_values = carry
        query_block, grad_block = inputs
        scores = (
            jnp.einsum("bhd,shd->hbs", query_block, keys_all, preferred_element_type=jnp.float32)
            * factor
        )
        row_max = jnp.max(scores, axis=2, keepdims=True)
        raised = jnp.exp(scores - row_max)
        weights = raised / jnp.sum(raised, axis=2, keepdims=True)
        weights_low = weights.astype(jnp.bfloat16)
        full_context = jnp.einsum(
            "hbs,shd->bhd", weights_low, values_all, preferred_element_type=jnp.float32
        )
        row_dot = jnp.sum(grad_block.astype(jnp.float32) * full_context, axis=2)
        grad_weights = jnp.einsum(
            "bhd,shd->hbs", grad_block, values_all, preferred_element_type=jnp.float32
        )
        grad_scores = (weights * (grad_weights - row_dot.T[:, :, None]) * factor).astype(
            jnp.bfloat16
        )
        grad_q = jnp.einsum(
            "hbs,shd->bhd", grad_scores, keys_all, preferred_element_type=jnp.float32
        )
        grad_keys = grad_keys + jnp.einsum(
            "hbs,bhd->shd", grad_scores, query_block, preferred_element_type=jnp.float32
        )
        grad_values = grad_values + jnp.einsum(
            "hbs,bhd->shd", weights_low, grad_block, preferred_element_type=jnp.float32
        )
        return (
            (grad_keys, grad_values),
            (full_context.astype(jnp.bfloat16), grad_q.astype(jnp.bfloat16)),
        )

    zeros_start = jnp.zeros((enc_len, num_heads, HEAD), jnp.float32)
    (grad_keys, grad_values), (context, grad_query) = lax.scan(
        step, (zeros_start, zeros_start), (query_blocks, grad_blocks)
    )
    grad_pairs = (
        jnp.stack([grad_keys, grad_values], axis=1).astype(jnp.bfloat16).reshape(enc_len, 2, local)
    )
    return (context.reshape(dec_len, local), grad_query.reshape(dec_len, local), grad_pairs)


def shards(pairs, queries, upstream):
    groups = lax.axis_size("seq") * lax.axis_size("tp")
    rows, _, width = pairs.shape[1:]
    local = width // groups
    order = offsets()
    by_group = pairs.reshape(rows, 2, groups, local)
    arrived = []
    for offset in order:
        block = lax.dynamic_index_in_dim(by_group, group_at(offset), axis=2, keepdims=False)
        arrived.append(lax.ppermute(block, AXES, route(offset, False)))
    head_pairs = jnp.concatenate(arrived, axis=0)
    context, grad_query, head_grads = attend(head_pairs, queries[0], upstream[0])
    grad_pairs = jnp.zeros((rows, 2, groups, local), pairs.dtype)
    for i, offset in enumerate(order):
        block = lax.ppermute(head_grads[i * rows : (i + 1) * rows], AXES, route(offset, True))
        grad_pairs = lax.dynamic_update_index_in_dim(
            grad_pairs, block, group_at(offset), axis=2
        )
    return (context[None], grad_query[None], grad_pairs.reshape(1, rows, 2, width))


def solution(mesh):
    return jax.shard_map(
        shards,
        mesh=mesh,
        in_specs=(
            P("segment", ("seq", "tp"), None, None),
            P("segment", None, ("seq", "tp")),
            P("segment", None, ("seq", "tp")),
        ),
        out_specs=(
            P("segment", None, ("seq", "tp")),
            P("segment", None, ("seq", "tp")),
            P("segment", ("seq", "tp"), None, None),
        ),
        check_vma=False,
    )
```

```python
import functools

import jax
import jax.numpy as jnp
from jax import lax
from jax.experimental import pallas as pl
from jax.experimental.pallas import tpu as pltpu
from jax.sharding import PartitionSpec as P

HEAD = 128
AXES = ("segment", "seq", "tp")
LOG2E = 1.4426950408889634
MIB = 1 << 20


def offsets():
    seq_count = lax.axis_size("seq")
    tp_count = lax.axis_size("tp")
    pairs = [(dz, dy) for dz in range(seq_count) for dy in range(tp_count)]
    middle = seq_count / 2
    return sorted(pairs, key=lambda o: (abs(o[0] - middle), -o[1]))


def group_at(offset):
    seq_count = lax.axis_size("seq")
    tp_count = lax.axis_size("tp")
    z = lax.rem(lax.axis_index("seq") + offset[0], seq_count)
    y = lax.rem(lax.axis_index("tp") + offset[1], tp_count)
    return z * tp_count + y


def route(offset, back):
    segments, seq_count, tp_count = (lax.axis_size(a) for a in AXES)
    hops = []
    for s in range(segments):
        for z in range(seq_count):
            for y in range(tp_count):
                source = (s * seq_count + z) * tp_count + y
                s_to = (s + 1) % segments
                z_to = (z + offset[0]) % seq_count
                y_to = (y + offset[1]) % tp_count
                target = (s_to * seq_count + z_to) * tp_count + y_to
                hops.append((target, source) if back else (source, target))
    return hops


def pack(pairs, order, heads):
    _, rows, _, width = pairs.shape
    local = heads * HEAD

    def kernel(pairs_ref, *refs):
        outs, sem = refs[:-1], refs[-1]
        copies = []
        for i, offset in enumerate(order):
            base = group_at(offset) * local
            for h in range(heads):
                column = pl.multiple_of(base + h * HEAD, HEAD)
                copy = pltpu.make_async_copy(
                    pairs_ref.at[0, :, :, pl.ds(column, HEAD)], outs[i].at[h], sem.at[i, h]
                )
                copy.start()
                copies.append(copy)
        for copy in copies:
            copy.wait()

    return pl.pallas_call(
        kernel,
        out_shape=[jax.ShapeDtypeStruct((heads, rows, 2, HEAD), pairs.dtype)] * len(order),
        in_specs=[pl.BlockSpec(memory_space=pl.ANY)],
        out_specs=[pl.BlockSpec(memory_space=pl.ANY)] * len(order),
        scratch_shapes=[pltpu.SemaphoreType.DMA((len(order), heads))],
        name="pack",
    )(pairs)


def unpack(blocks, order, width):
    heads, rows, _, _ = blocks[0].shape
    local = heads * HEAD

    def kernel(*refs):
        ins, out, sem = refs[: len(order)], refs[len(order)], refs[-1]
        copies = []
        for i, offset in enumerate(order):
            base = group_at(offset) * local
            for h in range(heads):
                column = pl.multiple_of(base + h * HEAD, HEAD)
                copy = pltpu.make_async_copy(
                    ins[i].at[h], out.at[0, :, :, pl.ds(column, HEAD)], sem.at[i, h]
                )
                copy.start()
                copies.append(copy)
        for copy in copies:
            copy.wait()

    return pl.pallas_call(
        kernel,
        out_shape=jax.ShapeDtypeStruct((1, rows, 2, width), blocks[0].dtype),
        in_specs=[pl.BlockSpec(memory_space=pl.ANY)] * len(order),
        out_specs=pl.BlockSpec(memory_space=pl.ANY),
        scratch_shapes=[pltpu.SemaphoreType.DMA((len(order), heads))],
        name="unpack",
    )(*blocks)


def dot(a, b, contract=((1,), (0,))):
    return lax.dot_general(a, b, (contract, ((), ())), preferred_element_type=jnp.float32)


NT = ((1,), (1,))


def splitter(rows):
    to = lax.broadcasted_iota(jnp.int32, (2 * rows, 2 * rows), 0)
    source = lax.broadcasted_iota(jnp.int32, (2 * rows, 2 * rows), 1)
    wanted = jnp.where(to < rows, 2 * to, 2 * (to - rows) + 1)
    return jnp.where(source == wanted, 1.0, 0.0).astype(jnp.bfloat16)


def joiner(rows):
    to = lax.broadcasted_iota(jnp.int32, (2 * rows, 2 * rows), 0)
    source = lax.broadcasted_iota(jnp.int32, (2 * rows, 2 * rows), 1)
    wanted = jnp.where(source < rows, 2 * source, 2 * (source - rows) + 1)
    return jnp.where(to == wanted, 1.0, 0.0).astype(jnp.bfloat16)


def attend_kernel(count, steps, sub, *refs):
    chunks = refs[:count]
    q_ref, g_ref, ctx_ref, gq_ref = refs[count : count + 4]
    outs = refs[count + 4 : 2 * count + 4]
    k_ref, v_ref, kt_ref, vt_ref, gk_ref, gv_ref = refs[2 * count + 4 :]
    rows = chunks[0].shape[1] // 2
    factor = HEAD**-0.5
    step = pl.program_id(1)

    @pl.when(step == 0)
    def _():
        split = splitter(rows)
        for i in range(count):
            both = dot(split, chunks[i][0])
            here = slice(i * rows, (i + 1) * rows)
            k_ref[here, :] = both[:rows].astype(jnp.bfloat16)
            v_ref[here, :] = both[rows:].astype(jnp.bfloat16)
            kt_ref[:, here] = both[:rows].T.astype(jnp.bfloat16)
            vt_ref[:HEAD, here] = both[rows:].T.astype(jnp.bfloat16)
        vt_ref[HEAD:, :] = jnp.ones((vt_ref.shape[0] - HEAD, vt_ref.shape[1]), jnp.bfloat16)
        gk_ref[...] = jnp.zeros_like(gk_ref)
        gv_ref[...] = jnp.zeros_like(gv_ref)

    for j in range(q_ref.shape[1] // sub):
        here = slice(j * sub, (j + 1) * sub)
        qt = q_ref[0, here, :].astype(jnp.float32).T
        gt = g_ref[0, here, :].astype(jnp.float32).T
        scores = dot(k_ref[...], qt.astype(jnp.bfloat16))
        top = jnp.max(scores, axis=0, keepdims=True)
        raised = jnp.exp2((scores - top) * (factor * LOG2E))
        raised_low = raised.astype(jnp.bfloat16)
        summed = dot(vt_ref[...], raised_low)
        scale = 1.0 / summed[HEAD : HEAD + 1, :]
        context = summed[:HEAD, :] * scale
        row_dot = jnp.sum(gt * context, axis=0, keepdims=True)
        grad_weights = dot(v_ref[...], gt.astype(jnp.bfloat16))
        grad_scores = (raised * (grad_weights - row_dot)).astype(jnp.bfloat16)
        ctx_ref[0, here, :] = context.T.astype(jnp.bfloat16)
        grad_q = dot(kt_ref[...], grad_scores) * (scale * factor)
        gq_ref[0, here, :] = grad_q.T.astype(jnp.bfloat16)
        gk_ref[...] += dot(grad_scores, (qt * (scale * factor)).astype(jnp.bfloat16), NT)
        gv_ref[...] += dot(raised_low, (gt * scale).astype(jnp.bfloat16), NT)

    @pl.when(step == steps - 1)
    def _():
        join = joiner(rows)
        for i in range(count):
            here = slice(i * rows, (i + 1) * rows)
            both = jnp.concatenate([gk_ref[here, :], gv_ref[here, :]], axis=0)
            outs[i][0] = dot(join, both.astype(jnp.bfloat16)).astype(jnp.bfloat16)


def attend(chunks, queries, upstream):
    heads, pair_rows, _ = chunks[0].shape
    count = len(chunks)
    enc_len = count * pair_rows // 2
    dec_len = queries.shape[1]
    block = 512 if dec_len % 512 == 0 else dec_len
    sub = 256 if block % 256 == 0 else block
    steps = dec_len // block
    chunk_spec = pl.BlockSpec((1, pair_rows, HEAD), lambda h, i: (h, 0, 0))
    row_spec = pl.BlockSpec((1, block, HEAD), lambda h, i: (0, i, h))
    rows_shape = jax.ShapeDtypeStruct(queries.shape, queries.dtype)
    results = pl.pallas_call(
        functools.partial(attend_kernel, count, steps, sub),
        grid=(heads, steps),
        out_shape=[rows_shape, rows_shape]
        + [jax.ShapeDtypeStruct(c.shape, c.dtype) for c in chunks],
        in_specs=[chunk_spec] * count + [row_spec] * 2,
        out_specs=[row_spec] * 2 + [chunk_spec] * count,
        scratch_shapes=[
            pltpu.VMEM((enc_len, HEAD), jnp.bfloat16),
            pltpu.VMEM((enc_len, HEAD), jnp.bfloat16),
            pltpu.VMEM((HEAD, enc_len), jnp.bfloat16),
            pltpu.VMEM((HEAD + 16, enc_len), jnp.bfloat16),
            pltpu.VMEM((enc_len, HEAD), jnp.float32),
            pltpu.VMEM((enc_len, HEAD), jnp.float32),
        ],
        compiler_params=pltpu.CompilerParams(vmem_limit_bytes=48 * MIB),
        cost_estimate=pl.CostEstimate(
            flops=heads * 12 * enc_len * dec_len * HEAD,
            bytes_accessed=heads * HEAD * (8 * enc_len + 8 * dec_len),
            transcendentals=heads * enc_len * dec_len,
        ),
        name="attend",
    )(*chunks, queries, upstream)
    return results[0], results[1], results[2:]


def shards(pairs, queries, upstream):
    _, rows, _, width = pairs.shape
    heads = queries.shape[2] // HEAD
    order = offsets()
    arrived = []
    for offset, block in zip(order, pack(pairs, order, heads)):
        block = block.reshape(heads, 2 * rows, HEAD)
        arrived.append(lax.ppermute(block, AXES, route(offset, False)))
    context, grad_query, grads = attend(arrived, queries, upstream)
    returned = []
    for offset, block in zip(order, grads):
        block = lax.ppermute(block, AXES, route(offset, True))
        returned.append(block.reshape(heads, rows, 2, HEAD))
    return context, grad_query, unpack(returned, order, width)


def solution(mesh):
    return jax.shard_map(
        shards,
        mesh=mesh,
        in_specs=(
            P("segment", ("seq", "tp"), None, None),
            P("segment", None, ("seq", "tp")),
            P("segment", None, ("seq", "tp")),
        ),
        out_specs=(
            P("segment", None, ("seq", "tp")),
            P("segment", None, ("seq", "tp")),
            P("segment", ("seq", "tp"), None, None),
        ),
        check_vma=False,
    )
```

```python
import functools

import jax
import jax.numpy as jnp
from jax import lax
from jax.experimental import pallas as pl
from jax.experimental.pallas import tpu as pltpu
from jax.sharding import PartitionSpec as P

HEAD = 128
AXES = ("segment", "seq", "tp")
LOG2E = 1.4426950408889634
MIB = 1 << 20


def offsets():
    seq_count = lax.axis_size("seq")
    tp_count = lax.axis_size("tp")
    pairs = [(dz, dy) for dz in range(seq_count) for dy in range(tp_count)]
    middle = seq_count / 2
    return sorted(pairs, key=lambda o: (abs(o[0] - middle), -o[1]))


def group_at(offset):
    seq_count = lax.axis_size("seq")
    tp_count = lax.axis_size("tp")
    z = lax.rem(lax.axis_index("seq") + offset[0], seq_count)
    y = lax.rem(lax.axis_index("tp") + offset[1], tp_count)
    return z * tp_count + y


def route(offset, back):
    segments, seq_count, tp_count = (lax.axis_size(a) for a in AXES)
    hops = []
    for s in range(segments):
        for z in range(seq_count):
            for y in range(tp_count):
                source = (s * seq_count + z) * tp_count + y
                s_to = (s + 1) % segments
                z_to = (z + offset[0]) % seq_count
                y_to = (y + offset[1]) % tp_count
                target = (s_to * seq_count + z_to) * tp_count + y_to
                hops.append((target, source) if back else (source, target))
    return hops


def pack(pairs, order, heads):
    _, rows, _, width = pairs.shape
    local = heads * HEAD

    def kernel(pairs_ref, *outs):
        for i, offset in enumerate(order):
            base = group_at(offset) * local
            for h in range(heads):
                column = pl.multiple_of(base + h * HEAD, HEAD)
                outs[i][h] = pairs_ref[0, :, :, pl.ds(column, HEAD)]

    return pl.pallas_call(
        kernel,
        out_shape=[jax.ShapeDtypeStruct((heads, rows, 2, HEAD), pairs.dtype)] * len(order),
        in_specs=[pl.BlockSpec(memory_space=pltpu.VMEM)],
        out_specs=[pl.BlockSpec(memory_space=pltpu.VMEM)] * len(order),
        compiler_params=pltpu.CompilerParams(vmem_limit_bytes=32 * MIB),
        name="pack",
    )(pairs)


def unpack(blocks, order, width):
    heads, rows, _, _ = blocks[0].shape
    local = heads * HEAD

    def kernel(*refs):
        ins, out = refs[: len(order)], refs[len(order)]
        for i, offset in enumerate(order):
            base = group_at(offset) * local
            for h in range(heads):
                column = pl.multiple_of(base + h * HEAD, HEAD)
                out[0, :, :, pl.ds(column, HEAD)] = ins[i][h]

    return pl.pallas_call(
        kernel,
        out_shape=jax.ShapeDtypeStruct((1, rows, 2, width), blocks[0].dtype),
        in_specs=[pl.BlockSpec(memory_space=pltpu.VMEM)] * len(order),
        out_specs=pl.BlockSpec(memory_space=pltpu.VMEM),
        compiler_params=pltpu.CompilerParams(vmem_limit_bytes=32 * MIB),
        name="unpack",
    )(*blocks)


def dot(a, b, contract=((1,), (0,))):
    return lax.dot_general(a, b, (contract, ((), ())), preferred_element_type=jnp.float32)


NT = ((1,), (1,))


def splitter(rows):
    to = lax.broadcasted_iota(jnp.int32, (2 * rows, 2 * rows), 0)
    source = lax.broadcasted_iota(jnp.int32, (2 * rows, 2 * rows), 1)
    wanted = jnp.where(to < rows, 2 * to, 2 * (to - rows) + 1)
    return jnp.where(source == wanted, 1.0, 0.0).astype(jnp.bfloat16)


def joiner(rows):
    to = lax.broadcasted_iota(jnp.int32, (2 * rows, 2 * rows), 0)
    source = lax.broadcasted_iota(jnp.int32, (2 * rows, 2 * rows), 1)
    wanted = jnp.where(source < rows, 2 * source, 2 * (source - rows) + 1)
    return jnp.where(to == wanted, 1.0, 0.0).astype(jnp.bfloat16)


def attend_kernel(count, steps, sub, *refs):
    chunks = refs[:count]
    q_ref, g_ref, ctx_ref, gq_ref = refs[count : count + 4]
    outs = refs[count + 4 : 2 * count + 4]
    k_ref, v_ref, kt_ref, vt_ref, gk_ref, gv_ref = refs[2 * count + 4 :]
    rows = chunks[0].shape[1] // 2
    factor = HEAD**-0.5
    step = pl.program_id(1)

    @pl.when(step == 0)
    def _():
        split = splitter(rows)
        for i in range(count):
            both = dot(split, chunks[i][0])
            here = slice(i * rows, (i + 1) * rows)
            k_ref[here, :] = both[:rows].astype(jnp.bfloat16)
            v_ref[here, :] = both[rows:].astype(jnp.bfloat16)
            kt_ref[:, here] = both[:rows].T.astype(jnp.bfloat16)
            vt_ref[:HEAD, here] = both[rows:].T.astype(jnp.bfloat16)
        vt_ref[HEAD:, :] = jnp.ones((vt_ref.shape[0] - HEAD, vt_ref.shape[1]), jnp.bfloat16)
        gk_ref[...] = jnp.zeros_like(gk_ref)
        gv_ref[...] = jnp.zeros_like(gv_ref)

    for j in range(q_ref.shape[1] // sub):
        here = slice(j * sub, (j + 1) * sub)
        qt = q_ref[0, here, :].astype(jnp.float32).T
        gt = g_ref[0, here, :].astype(jnp.float32).T
        scores = dot(k_ref[...], qt.astype(jnp.bfloat16))
        top = jnp.max(scores, axis=0, keepdims=True)
        raised = jnp.exp2((scores - top) * (factor * LOG2E))
        raised_low = raised.astype(jnp.bfloat16)
        summed = dot(vt_ref[...], raised_low)
        scale = 1.0 / summed[HEAD : HEAD + 1, :]
        context = summed[:HEAD, :] * scale
        row_dot = jnp.sum(gt * context, axis=0, keepdims=True)
        grad_weights = dot(v_ref[...], gt.astype(jnp.bfloat16))
        grad_scores = (raised * (grad_weights - row_dot)).astype(jnp.bfloat16)
        ctx_ref[0, here, :] = context.T.astype(jnp.bfloat16)
        grad_q = dot(kt_ref[...], grad_scores) * (scale * factor)
        gq_ref[0, here, :] = grad_q.T.astype(jnp.bfloat16)
        gk_ref[...] += dot(grad_scores, (qt * (scale * factor)).astype(jnp.bfloat16), NT)
        gv_ref[...] += dot(raised_low, (gt * scale).astype(jnp.bfloat16), NT)

    @pl.when(step == steps - 1)
    def _():
        join = joiner(rows)
        for i in range(count):
            here = slice(i * rows, (i + 1) * rows)
            both = jnp.concatenate([gk_ref[here, :], gv_ref[here, :]], axis=0)
            outs[i][0] = dot(join, both.astype(jnp.bfloat16)).astype(jnp.bfloat16)


def attend(chunks, queries, upstream):
    heads, pair_rows, _ = chunks[0].shape
    count = len(chunks)
    enc_len = count * pair_rows // 2
    dec_len = queries.shape[1]
    block = 512 if dec_len % 512 == 0 else dec_len
    sub = 256 if block % 256 == 0 else block
    steps = dec_len // block
    chunk_spec = pl.BlockSpec((1, pair_rows, HEAD), lambda h, i: (h, 0, 0))
    row_spec = pl.BlockSpec((1, block, HEAD), lambda h, i: (0, i, h))
    rows_shape = jax.ShapeDtypeStruct(queries.shape, queries.dtype)
    results = pl.pallas_call(
        functools.partial(attend_kernel, count, steps, sub),
        grid=(heads, steps),
        out_shape=[rows_shape, rows_shape]
        + [jax.ShapeDtypeStruct(c.shape, c.dtype) for c in chunks],
        in_specs=[chunk_spec] * count + [row_spec] * 2,
        out_specs=[row_spec] * 2 + [chunk_spec] * count,
        scratch_shapes=[
            pltpu.VMEM((enc_len, HEAD), jnp.bfloat16),
            pltpu.VMEM((enc_len, HEAD), jnp.bfloat16),
            pltpu.VMEM((HEAD, enc_len), jnp.bfloat16),
            pltpu.VMEM((HEAD + 16, enc_len), jnp.bfloat16),
            pltpu.VMEM((enc_len, HEAD), jnp.float32),
            pltpu.VMEM((enc_len, HEAD), jnp.float32),
        ],
        compiler_params=pltpu.CompilerParams(vmem_limit_bytes=48 * MIB),
        cost_estimate=pl.CostEstimate(
            flops=heads * 12 * enc_len * dec_len * HEAD,
            bytes_accessed=heads * HEAD * (8 * enc_len + 8 * dec_len),
            transcendentals=heads * enc_len * dec_len,
        ),
        name="attend",
    )(*chunks, queries, upstream)
    return results[0], results[1], results[2:]


def shards(pairs, queries, upstream):
    _, rows, _, width = pairs.shape
    heads = queries.shape[2] // HEAD
    order = offsets()
    arrived = []
    for offset, block in zip(order, pack(pairs, order, heads)):
        block = block.reshape(heads, 2 * rows, HEAD)
        arrived.append(lax.ppermute(block, AXES, route(offset, False)))
    context, grad_query, grads = attend(arrived, queries, upstream)
    returned = []
    for offset, block in zip(order, grads):
        block = lax.ppermute(block, AXES, route(offset, True))
        returned.append(block.reshape(heads, rows, 2, HEAD))
    return context, grad_query, unpack(returned, order, width)


def solution(mesh):
    return jax.shard_map(
        shards,
        mesh=mesh,
        in_specs=(
            P("segment", ("seq", "tp"), None, None),
            P("segment", None, ("seq", "tp")),
            P("segment", None, ("seq", "tp")),
        ),
        out_specs=(
            P("segment", None, ("seq", "tp")),
            P("segment", None, ("seq", "tp")),
            P("segment", ("seq", "tp"), None, None),
        ),
        check_vma=False,
    )
```

```python
import functools

import jax
import jax.numpy as jnp
from jax import lax
from jax.experimental import pallas as pl
from jax.experimental.pallas import tpu as pltpu
from jax.sharding import PartitionSpec as P

HEAD = 128
AXES = ("segment", "seq", "tp")
FACTOR = HEAD**-0.5
EXPONENT = FACTOR * 1.4426950408889634
MIB = 1 << 20
NT = ((1,), (1,))
ANY = pl.BlockSpec(memory_space=pl.ANY)
VMEM = pl.BlockSpec(memory_space=pltpu.VMEM)


def offsets():
    seq_count = lax.axis_size("seq")
    tp_count = lax.axis_size("tp")
    near = [(0, dy) for dy in reversed(range(tp_count))]
    order = [(dz, dy) for dz in range(1, seq_count) for dy in reversed(range(tp_count))]
    order.sort(key=lambda o: -abs(o[0] - seq_count / 2))
    for i, offset in enumerate(near):
        order.insert(3 + 2 * i, offset)
    return order


def group_at(offset):
    seq_count = lax.axis_size("seq")
    tp_count = lax.axis_size("tp")
    z = lax.rem(lax.axis_index("seq") + offset[0], seq_count)
    y = lax.rem(lax.axis_index("tp") + offset[1], tp_count)
    return z * tp_count + y


def route(offset, back):
    segments, seq_count, tp_count = (lax.axis_size(a) for a in AXES)
    hops = []
    for s in range(segments):
        for z in range(seq_count):
            for y in range(tp_count):
                source = (s * seq_count + z) * tp_count + y
                s_to = (s + 1) % segments
                z_to = (z + offset[0]) % seq_count
                y_to = (y + offset[1]) % tp_count
                target = (s_to * seq_count + z_to) * tp_count + y_to
                hops.append((target, source) if back else (source, target))
    return hops


def params(enc_len):
    return pltpu.CompilerParams(vmem_limit_bytes=(12 + enc_len * 36 // 4096) * MIB)


def pack(pairs, order, heads):
    _, rows, _, width = pairs.shape
    local = heads * HEAD

    def kernel(pairs_ref, *outs):
        @pl.loop(0, rows // 16)
        def _(r):
            here = pl.ds(pl.multiple_of(r * 16, 16), 16)
            for i, offset in enumerate(order):
                base = group_at(offset) * local
                for h in range(heads):
                    column = pl.multiple_of(base + h * HEAD, HEAD)
                    outs[i][h, here] = pairs_ref[0, here, :, pl.ds(column, HEAD)]

    return pl.pallas_call(
        kernel,
        out_shape=[jax.ShapeDtypeStruct((heads, rows, 2, HEAD), pairs.dtype)] * len(order),
        in_specs=[VMEM],
        out_specs=[VMEM] * len(order),
        compiler_params=pltpu.CompilerParams(vmem_limit_bytes=24 * MIB),
        name="pack",
    )(pairs)


def unpack(blocks, order, width):
    heads, rows, _, _ = blocks[0].shape
    local = heads * HEAD

    def kernel(*refs):
        ins, out = refs[: len(order)], refs[len(order)]

        @pl.loop(0, rows // 16)
        def _(r):
            here = pl.ds(pl.multiple_of(r * 16, 16), 16)
            for i, offset in enumerate(order):
                base = group_at(offset) * local
                for h in range(heads):
                    column = pl.multiple_of(base + h * HEAD, HEAD)
                    out[0, here, :, pl.ds(column, HEAD)] = ins[i][h, here]

    return pl.pallas_call(
        kernel,
        out_shape=jax.ShapeDtypeStruct((1, rows, 2, width), blocks[0].dtype),
        in_specs=[VMEM] * len(order),
        out_specs=VMEM,
        compiler_params=pltpu.CompilerParams(vmem_limit_bytes=24 * MIB),
        name="unpack",
    )(*blocks)


def turned(rows):
    _, tokens, local = rows.shape
    heads = local // HEAD
    tile = 256 if tokens % 256 == 0 else tokens

    def kernel(rows_ref, out_ref):
        for h in range(heads):
            for j in range(tokens // tile):
                here = slice(j * tile, (j + 1) * tile)
                block = rows_ref[0, here, h * HEAD : (h + 1) * HEAD]
                out_ref[h, :, here] = block.astype(jnp.float32).T.astype(rows.dtype)

    return pl.pallas_call(
        kernel,
        out_shape=jax.ShapeDtypeStruct((heads, HEAD, tokens), rows.dtype),
        in_specs=[VMEM],
        out_specs=VMEM,
        compiler_params=pltpu.CompilerParams(vmem_limit_bytes=16 * MIB),
        name="turned",
    )(rows)


def dot(a, b, contract=((1,), (0,))):
    return lax.dot_general(a, b, (contract, ((), ())), preferred_element_type=jnp.float32)


def shuffle(rows, join):
    to = lax.broadcasted_iota(jnp.int32, (2 * rows, 2 * rows), 1 if join else 0)
    source = lax.broadcasted_iota(jnp.int32, (2 * rows, 2 * rows), 0 if join else 1)
    wanted = jnp.where(to < rows, 2 * to, 2 * (to - rows) + 1)
    return jnp.where(source == wanted, 1.0, 0.0).astype(jnp.bfloat16)


def split_chunks(chunks, h, rows, k_ref=None, v_ref=None, kt_ref=None, vt_ref=None):
    split = shuffle(rows, False)
    for i, chunk in enumerate(chunks):
        both = dot(split, chunk[h])
        here = slice(i * rows, (i + 1) * rows)
        keys, values = both[:rows], both[rows:]
        if k_ref is not None:
            k_ref[h, here, :] = keys.astype(jnp.bfloat16)
        if v_ref is not None:
            v_ref[h, here, :] = values.astype(jnp.bfloat16)
        if kt_ref is not None:
            kt_ref[h, :, here] = keys.T.astype(jnp.bfloat16)
        if vt_ref is not None:
            vt_ref[h, :HEAD, here] = values.T.astype(jnp.bfloat16)
    if vt_ref is not None:
        tail = (vt_ref.shape[1] - HEAD, vt_ref.shape[2])
        vt_ref[h, HEAD:, :] = jnp.ones(tail, jnp.bfloat16)


def join_chunks(outs, h, rows, gk_ref, gv_ref):
    join = shuffle(rows, True)
    for i, out in enumerate(outs):
        here = slice(i * rows, (i + 1) * rows)
        both = jnp.concatenate([gk_ref[h, here, :], gv_ref[h, here, :]], axis=0)
        out[h] = dot(join, both.astype(jnp.bfloat16)).astype(jnp.bfloat16)


def raise_scores(keys, qt, values_t, before):
    scores = dot(keys, qt)
    top = jnp.max(scores, axis=0, keepdims=True)
    if before is not None:
        top = jnp.maximum(top, before[0])
    raised = jnp.exp2((scores - top) * EXPONENT)
    low = raised.astype(jnp.bfloat16)
    summed = dot(values_t, low)
    total, context = summed[HEAD : HEAD + 1], summed[:HEAD]
    if before is not None:
        shrink = jnp.exp2((before[0] - top) * EXPONENT)
        total = total + before[1] * shrink
        context = context + before[2] * shrink
    return raised, low, top, total, context


def forward_kernel(count, first, tile, *refs):
    chunks, refs = refs[:count], refs[count:]
    qt_ref, refs = refs[0], refs[1:]
    if not first:
        stats_in, context_in, refs = refs[0], refs[1], refs[2:]
    stats_ref, context_ref, low_ref, k_ref, vt_ref = refs
    heads, pair_rows, _ = chunks[0].shape
    for h in range(heads):
        split_chunks(chunks, h, pair_rows // 2, k_ref=k_ref, vt_ref=vt_ref)

    @pl.loop(0, qt_ref.shape[2] // tile)
    def _(j):
        here = pl.ds(pl.multiple_of(j * tile, tile), tile)
        for h in range(heads):
            before = None
            if not first:
                before = (stats_in[h, 0:1, here], stats_in[h, 1:2, here], context_in[h, :, here])
            _, low, top, total, context = raise_scores(
                k_ref[h], qt_ref[h, :, here], vt_ref[h], before
            )
            low_ref[h, :, here] = low
            stats_ref[h, 0:1, here] = top
            stats_ref[h, 1:2, here] = total
            context_ref[h, :, here] = context


def gradients(raised, low, shrunk, stats, h, here, refs):
    qt_ref, gt_ref, v_ref, kt_ref, gk_ref, gv_ref = refs
    scale, row_dot = stats
    qt = qt_ref[h, :, here].astype(jnp.float32)
    gt = gt_ref[h, :, here]
    grad_weights = dot(v_ref[h], gt)
    grad_scores = (raised * (grad_weights - row_dot)).astype(jnp.bfloat16)
    scale = scale if shrunk is None else scale * shrunk
    grad_q = dot(kt_ref[h], grad_scores) * (scale * FACTOR)
    gk_ref[h] += dot(grad_scores, (qt * (scale * FACTOR)).astype(jnp.bfloat16), NT)
    gv_ref[h] += dot(low, (gt.astype(jnp.float32) * scale).astype(jnp.bfloat16), NT)
    return grad_q


def turn_kernel(count, tile, *refs):
    chunks, refs = refs[:count], refs[count:]
    qt_ref, gt_ref, stats_in, context_in = refs[:4]
    stats_ref, context_ref, grad_q_ref = refs[4:7]
    outs, refs = refs[7 : 7 + count], refs[7 + count :]
    k_ref, v_ref, kt_ref, vt_ref, gk_ref, gv_ref = refs
    heads, pair_rows, _ = chunks[0].shape
    rows = pair_rows // 2
    for h in range(heads):
        split_chunks(chunks, h, rows, k_ref, v_ref, kt_ref, vt_ref)
    gk_ref[...] = jnp.zeros_like(gk_ref)
    gv_ref[...] = jnp.zeros_like(gv_ref)

    @pl.loop(0, qt_ref.shape[2] // tile)
    def _(j):
        here = pl.ds(pl.multiple_of(j * tile, tile), tile)
        for h in range(heads):
            before = (stats_in[h, 0:1, here], stats_in[h, 1:2, here], context_in[h, :, here])
            raised, low, top, total, context = raise_scores(
                k_ref[h], qt_ref[h, :, here], vt_ref[h], before
            )
            scale = 1.0 / total
            context = context * scale
            row_dot = jnp.sum(
                gt_ref[h, :, here].astype(jnp.float32) * context, axis=0, keepdims=True
            )
            context_ref[h, :, here] = context
            stats_ref[h, 0:1, here] = top
            stats_ref[h, 1:2, here] = scale
            stats_ref[h, 2:3, here] = row_dot
            grad_q_ref[h, :, here] = gradients(
                raised,
                low,
                None,
                (scale, row_dot),
                h,
                here,
                (qt_ref, gt_ref, v_ref, kt_ref, gk_ref, gv_ref),
            )

    for h in range(heads):
        join_chunks(outs, h, rows, gk_ref, gv_ref)


def backward_kernel(back, count, ready, last, tile, *refs):
    chunks, refs = refs[back : back + count], refs[back + count :]
    qt_ref, gt_ref, low_ref, stats_then, stats_ref, grad_q_in = refs[:6]
    refs = refs[6:]
    if ready:
        ready_ref, refs = refs[0], refs[1:]
    if ready or last:
        rows_ref, refs = refs[0], refs[1:]
    if not last:
        grad_q_ref, refs = refs[0], refs[1:]
    outs, refs = refs[:count], refs[count:]
    v_ref, kt_ref, gk_ref, gv_ref = refs
    heads, pair_rows, _ = chunks[0].shape
    rows = pair_rows // 2
    for h in range(heads):
        split_chunks(chunks, h, rows, v_ref=v_ref, kt_ref=kt_ref)
    gk_ref[...] = jnp.zeros_like(gk_ref)
    gv_ref[...] = jnp.zeros_like(gv_ref)

    @pl.loop(0, qt_ref.shape[2] // tile)
    def _(j):
        here = pl.ds(pl.multiple_of(j * tile, tile), tile)
        for h in range(heads):
            columns = slice(h * HEAD, (h + 1) * HEAD)
            low = low_ref[h, :, here]
            top, scale, row_dot = (stats_ref[h, i : i + 1, here] for i in range(3))
            shrunk = jnp.exp2((stats_then[h, 0:1, here] - top) * EXPONENT)
            grad_q = grad_q_in[h, :, here] + gradients(
                low.astype(jnp.float32),
                low,
                shrunk,
                (scale, row_dot),
                h,
                here,
                (qt_ref, gt_ref, v_ref, kt_ref, gk_ref, gv_ref),
            )
            if last:
                rows_ref[0, here, columns] = grad_q.T.astype(rows_ref.dtype)
            else:
                grad_q_ref[h, :, here] = grad_q
            if ready:
                rows_ref[0, here, columns] = ready_ref[h, :, here].T.astype(rows_ref.dtype)

    for h in range(heads):
        join_chunks(outs, h, rows, gk_ref, gv_ref)


def cost(heads, rows, tokens, matmuls):
    return pl.CostEstimate(
        flops=2 * matmuls * heads * rows * tokens * HEAD,
        bytes_accessed=heads * (rows + tokens) * HEAD * 8,
        transcendentals=heads * rows * tokens,
    )


def attend(arrived, queries, upstream, send_back):
    heads, pair_rows, _ = arrived[0].shape
    rows = pair_rows // 2
    enc_len = len(arrived) * rows
    tokens = queries.shape[1]
    tile = 256 if tokens % 256 == 0 else tokens
    qt, gt = turned(queries), turned(upstream)
    stats_shape = jax.ShapeDtypeStruct((heads, 8, tokens), jnp.float32)
    wide_shape = jax.ShapeDtypeStruct((heads, HEAD, tokens), jnp.float32)
    rows_shape = jax.ShapeDtypeStruct(queries.shape, queries.dtype)
    compiler_params = params(enc_len)
    turn_at = len(arrived) - len(arrived) // 4
    half = (turn_at + 1) // 2

    def natural(count):
        return pltpu.VMEM((heads, count * rows, HEAD), jnp.bfloat16)

    def across(count, extra=0):
        return pltpu.VMEM((heads, HEAD + extra, count * rows), jnp.bfloat16)

    def sums(count):
        return pltpu.VMEM((heads, count * rows, HEAD), jnp.float32)

    def shapes_of(group):
        return [jax.ShapeDtypeStruct(c.shape, c.dtype) for c in group]

    state, parts = [], []
    for begin, end in ((0, half), (half, turn_at)):
        group, count = arrived[begin:end], end - begin
        low_shape = jax.ShapeDtypeStruct((heads, count * rows, tokens), jnp.bfloat16)
        stats, context, low = pl.pallas_call(
            functools.partial(forward_kernel, count, not state, tile),
            out_shape=[stats_shape, wide_shape, low_shape],
            in_specs=[VMEM] * (count + 1 + len(state)),
            out_specs=[VMEM] * 3,
            scratch_shapes=[natural(count), across(count, 16)],
            compiler_params=compiler_params,
            cost_estimate=cost(heads, count * rows, tokens, 2),
            name="forward",
        )(*group, qt, *state)
        state = [stats, context]
        parts.insert(0, (begin, count, low, stats))

    group, count = arrived[turn_at:], len(arrived) - turn_at
    final, context, grad_q, *grads = pl.pallas_call(
        functools.partial(turn_kernel, count, tile),
        out_shape=[stats_shape, wide_shape, wide_shape] + shapes_of(group),
        in_specs=[VMEM] * (count + 4),
        out_specs=[VMEM] * (count + 3),
        scratch_shapes=[natural(count), natural(count), across(count), across(count, 16)]
        + [sums(count)] * 2,
        compiler_params=compiler_params,
        cost_estimate=cost(heads, count * rows, tokens, 6),
        name="turn",
    )(*group, qt, gt, *state)
    returned = [send_back(turn_at, grads)]

    for i, (begin, count, low, then) in enumerate(parts):
        group = arrived[begin : begin + count]
        ready, last = i == 0, i == len(parts) - 1
        back = returned[i - 1] if i >= 1 else []
        extra = [rows_shape] * (ready or last) + [wide_shape] * (not last)
        outs = pl.pallas_call(
            functools.partial(backward_kernel, len(back), count, ready, last, tile),
            out_shape=extra + shapes_of(group),
            in_specs=[ANY] * len(back) + [VMEM] * (count + 6 + ready),
            out_specs=[VMEM] * (len(extra) + count),
            scratch_shapes=[natural(count), across(count)] + [sums(count)] * 2,
            compiler_params=compiler_params,
            cost_estimate=cost(heads, count * rows, tokens, 4),
            name="backward",
        )(*back, *group, qt, gt, low, then, final, grad_q, *([context] if ready else []))
        if ready:
            context_rows = outs[0]
        if last:
            grad_query = outs[0]
        else:
            grad_q = outs[len(extra) - 1]
        returned.append(send_back(begin, outs[len(extra) :]))
    return context_rows, grad_query, returned


def shards(pairs, queries, upstream):
    _, rows, _, width = pairs.shape
    heads = queries.shape[2] // HEAD
    order = offsets()
    arrived = []
    for offset, block in zip(order, pack(pairs, order, heads)):
        block = block.reshape(heads, 2 * rows, HEAD)
        arrived.append(lax.ppermute(block, AXES, route(offset, False)))
    homes = []

    def send_back(begin, blocks):
        there = order[begin : begin + len(blocks)]
        homes.extend(there)
        return [lax.ppermute(b, AXES, route(o, True)) for o, b in zip(there, blocks)]

    context, grad_query, parts = attend(arrived, queries, upstream, send_back)
    returned = [b.reshape(heads, rows, 2, HEAD) for part in parts for b in part]
    return context, grad_query, unpack(returned, homes, width)


def solution(mesh):
    return jax.shard_map(
        shards,
        mesh=mesh,
        in_specs=(
            P("segment", ("seq", "tp"), None, None),
            P("segment", None, ("seq", "tp")),
            P("segment", None, ("seq", "tp")),
        ),
        out_specs=(
            P("segment", None, ("seq", "tp")),
            P("segment", None, ("seq", "tp")),
            P("segment", ("seq", "tp"), None, None),
        ),
        check_vma=False,
    )
```

```python
import functools

import jax
import jax.numpy as jnp
from jax import lax
from jax.experimental import pallas as pl
from jax.experimental.pallas import tpu as pltpu
from jax.sharding import PartitionSpec as P

HEAD = 128
AXES = ("segment", "seq", "tp")
FACTOR = HEAD**-0.5
EXPONENT = FACTOR * 1.4426950408889634
MIB = 1 << 20
NT = ((1,), (1,))
ANY = pl.BlockSpec(memory_space=pl.ANY)
VMEM = pl.BlockSpec(memory_space=pltpu.VMEM)


def offsets():
    seq_count = lax.axis_size("seq")
    tp_count = lax.axis_size("tp")
    near = [(0, dy) for dy in reversed(range(tp_count))]
    order = [(dz, dy) for dz in range(1, seq_count) for dy in reversed(range(tp_count))]
    order.sort(key=lambda o: -abs(o[0] - seq_count / 2))
    for i, offset in enumerate(near):
        order.insert(3 + 2 * i, offset)
    return order


def group_at(offset):
    seq_count = lax.axis_size("seq")
    tp_count = lax.axis_size("tp")
    z = lax.rem(lax.axis_index("seq") + offset[0], seq_count)
    y = lax.rem(lax.axis_index("tp") + offset[1], tp_count)
    return z * tp_count + y


def route(offset, back):
    segments, seq_count, tp_count = (lax.axis_size(a) for a in AXES)
    hops = []
    for s in range(segments):
        for z in range(seq_count):
            for y in range(tp_count):
                source = (s * seq_count + z) * tp_count + y
                s_to = (s + 1) % segments
                z_to = (z + offset[0]) % seq_count
                y_to = (y + offset[1]) % tp_count
                target = (s_to * seq_count + z_to) * tp_count + y_to
                hops.append((target, source) if back else (source, target))
    return hops


def params(enc_len):
    return pltpu.CompilerParams(vmem_limit_bytes=(12 + enc_len * 36 // 4096) * MIB)


def pack(pairs, order, heads):
    _, rows, _, width = pairs.shape
    local = heads * HEAD

    def kernel(pairs_ref, *outs):
        @pl.loop(0, rows // 16)
        def _(r):
            here = pl.ds(pl.multiple_of(r * 16, 16), 16)
            for i, offset in enumerate(order):
                base = group_at(offset) * local
                for h in range(heads):
                    column = pl.multiple_of(base + h * HEAD, HEAD)
                    outs[i][h, here] = pairs_ref[0, here, :, pl.ds(column, HEAD)]

    return pl.pallas_call(
        kernel,
        out_shape=[jax.ShapeDtypeStruct((heads, rows, 2, HEAD), pairs.dtype)] * len(order),
        in_specs=[VMEM],
        out_specs=[VMEM] * len(order),
        compiler_params=pltpu.CompilerParams(vmem_limit_bytes=24 * MIB),
        name="pack",
    )(pairs)


def unpack(blocks, order, width):
    heads, rows, _, _ = blocks[0].shape
    local = heads * HEAD

    def kernel(*refs):
        ins, out = refs[: len(order)], refs[len(order)]

        @pl.loop(0, rows // 16)
        def _(r):
            here = pl.ds(pl.multiple_of(r * 16, 16), 16)
            for i, offset in enumerate(order):
                base = group_at(offset) * local
                for h in range(heads):
                    column = pl.multiple_of(base + h * HEAD, HEAD)
                    out[0, here, :, pl.ds(column, HEAD)] = ins[i][h, here]

    return pl.pallas_call(
        kernel,
        out_shape=jax.ShapeDtypeStruct((1, rows, 2, width), blocks[0].dtype),
        in_specs=[VMEM] * len(order),
        out_specs=VMEM,
        compiler_params=pltpu.CompilerParams(vmem_limit_bytes=24 * MIB),
        name="unpack",
    )(*blocks)


def turned(rows):
    _, tokens, local = rows.shape
    heads = local // HEAD
    tile = 256 if tokens % 256 == 0 else tokens

    def kernel(rows_ref, out_ref):
        for h in range(heads):
            for j in range(tokens // tile):
                here = slice(j * tile, (j + 1) * tile)
                block = rows_ref[0, here, h * HEAD : (h + 1) * HEAD]
                out_ref[h, :, here] = block.astype(jnp.float32).T.astype(rows.dtype)

    return pl.pallas_call(
        kernel,
        out_shape=jax.ShapeDtypeStruct((heads, HEAD, tokens), rows.dtype),
        in_specs=[VMEM],
        out_specs=VMEM,
        compiler_params=pltpu.CompilerParams(vmem_limit_bytes=16 * MIB),
        name="turned",
    )(rows)


def tiles(count):
    def run(body):
        if count <= 2:
            for j in range(count):
                body(j)
        else:
            pl.loop(0, count)(body)

    return run


def tokens_of(j, tile):
    return pl.ds(j * tile if isinstance(j, int) else pl.multiple_of(j * tile, tile), tile)


def tile_of(rows, tokens):
    for parts in range(1, tokens // 256 + 1):
        if tokens % (256 * parts) == 0 and rows * (tokens // parts) * 4 <= 5 * MIB // 4:
            return tokens // parts
    return 256 if tokens % 256 == 0 else tokens


def dot(a, b, contract=((1,), (0,))):
    return lax.dot_general(a, b, (contract, ((), ())), preferred_element_type=jnp.float32)


def shuffle(rows, join):
    to = lax.broadcasted_iota(jnp.int32, (2 * rows, 2 * rows), 1 if join else 0)
    source = lax.broadcasted_iota(jnp.int32, (2 * rows, 2 * rows), 0 if join else 1)
    wanted = jnp.where(to < rows, 2 * to, 2 * (to - rows) + 1)
    return jnp.where(source == wanted, 1.0, 0.0).astype(jnp.bfloat16)


def split_chunks(chunks, h, rows, k_ref=None, v_ref=None, kt_ref=None, vt_ref=None):
    split = shuffle(rows, False)
    for i, chunk in enumerate(chunks):
        both = dot(split, chunk[h])
        here = slice(i * rows, (i + 1) * rows)
        keys, values = both[:rows], both[rows:]
        if k_ref is not None:
            k_ref[h, here, :] = keys.astype(jnp.bfloat16)
        if v_ref is not None:
            v_ref[h, here, :] = values.astype(jnp.bfloat16)
        if kt_ref is not None:
            kt_ref[h, :, here] = keys.T.astype(jnp.bfloat16)
        if vt_ref is not None:
            vt_ref[h, :HEAD, here] = values.T.astype(jnp.bfloat16)
    if vt_ref is not None:
        tail = (vt_ref.shape[1] - HEAD, vt_ref.shape[2])
        vt_ref[h, HEAD:, :] = jnp.ones(tail, jnp.bfloat16)


def join_chunks(outs, h, rows, gk_ref, gv_ref):
    join = shuffle(rows, True)
    for i, out in enumerate(outs):
        here = slice(i * rows, (i + 1) * rows)
        both = jnp.concatenate([gk_ref[h, here, :], gv_ref[h, here, :]], axis=0)
        out[h] = dot(join, both.astype(jnp.bfloat16)).astype(jnp.bfloat16)


def raise_scores(keys, qt, values_t, before):
    scores = dot(keys, qt)
    top = jnp.max(scores, axis=0, keepdims=True)
    if before is not None:
        top = jnp.maximum(top, before[0])
    raised = jnp.exp2((scores - top) * EXPONENT)
    low = raised.astype(jnp.bfloat16)
    summed = dot(values_t, low)
    total, context = summed[HEAD : HEAD + 1], summed[:HEAD]
    if before is not None:
        shrink = jnp.exp2((before[0] - top) * EXPONENT)
        total = total + before[1] * shrink
        context = context + before[2] * shrink
    return raised, low, top, total, context


def forward_kernel(count, first, tile, *refs):
    chunks, refs = refs[:count], refs[count:]
    qt_ref, refs = refs[0], refs[1:]
    if not first:
        stats_in, context_in, refs = refs[0], refs[1], refs[2:]
    stats_ref, context_ref, low_ref, k_ref, vt_ref = refs
    heads, pair_rows, _ = chunks[0].shape
    for h in range(heads):
        split_chunks(chunks, h, pair_rows // 2, k_ref=k_ref, vt_ref=vt_ref)

    @tiles(qt_ref.shape[2] // tile)
    def _(j):
        here = tokens_of(j, tile)
        for h in range(heads):
            before = None
            if not first:
                before = (stats_in[h, 0:1, here], stats_in[h, 1:2, here], context_in[h, :, here])
            _, low, top, total, context = raise_scores(
                k_ref[h], qt_ref[h, :, here], vt_ref[h], before
            )
            low_ref[h, :, here] = low
            stats_ref[h, 0:1, here] = top
            stats_ref[h, 1:2, here] = total
            context_ref[h, :, here] = context


def gradients(raised, low, shrunk, stats, h, here, refs):
    qt_ref, gt_ref, v_ref, kt_ref, gk_ref, gv_ref = refs
    scale, row_dot = stats
    qt = qt_ref[h, :, here].astype(jnp.float32)
    gt = gt_ref[h, :, here]
    grad_weights = dot(v_ref[h], gt)
    grad_scores = (raised * (grad_weights - row_dot)).astype(jnp.bfloat16)
    scale = scale if shrunk is None else scale * shrunk
    grad_q = dot(kt_ref[h], grad_scores) * (scale * FACTOR)
    gk_ref[h] += dot(grad_scores, (qt * (scale * FACTOR)).astype(jnp.bfloat16), NT)
    gv_ref[h] += dot(low, (gt.astype(jnp.float32) * scale).astype(jnp.bfloat16), NT)
    return grad_q


def turn_kernel(count, tile, *refs):
    chunks, refs = refs[:count], refs[count:]
    qt_ref, gt_ref, stats_in, context_in = refs[:4]
    stats_ref, context_ref, grad_q_ref = refs[4:7]
    outs, refs = refs[7 : 7 + count], refs[7 + count :]
    k_ref, v_ref, kt_ref, vt_ref, gk_ref, gv_ref = refs
    heads, pair_rows, _ = chunks[0].shape
    rows = pair_rows // 2
    for h in range(heads):
        split_chunks(chunks, h, rows, k_ref, v_ref, kt_ref, vt_ref)
    gk_ref[...] = jnp.zeros_like(gk_ref)
    gv_ref[...] = jnp.zeros_like(gv_ref)

    @tiles(qt_ref.shape[2] // tile)
    def _(j):
        here = tokens_of(j, tile)
        for h in range(heads):
            before = (stats_in[h, 0:1, here], stats_in[h, 1:2, here], context_in[h, :, here])
            raised, low, top, total, context = raise_scores(
                k_ref[h], qt_ref[h, :, here], vt_ref[h], before
            )
            scale = 1.0 / total
            context = context * scale
            row_dot = jnp.sum(
                gt_ref[h, :, here].astype(jnp.float32) * context, axis=0, keepdims=True
            )
            context_ref[h, :, here] = context
            stats_ref[h, 0:1, here] = top
            stats_ref[h, 1:2, here] = scale
            stats_ref[h, 2:3, here] = row_dot
            grad_q_ref[h, :, here] = gradients(
                raised,
                low,
                None,
                (scale, row_dot),
                h,
                here,
                (qt_ref, gt_ref, v_ref, kt_ref, gk_ref, gv_ref),
            )

    for h in range(heads):
        join_chunks(outs, h, rows, gk_ref, gv_ref)


def backward_kernel(back, count, ready, last, tile, *refs):
    chunks, refs = refs[back : back + count], refs[back + count :]
    qt_ref, gt_ref, low_ref, stats_then, stats_ref, grad_q_in = refs[:6]
    refs = refs[6:]
    if ready:
        ready_ref, refs = refs[0], refs[1:]
    if ready or last:
        rows_ref, refs = refs[0], refs[1:]
    if not last:
        grad_q_ref, refs = refs[0], refs[1:]
    outs, refs = refs[:count], refs[count:]
    v_ref, kt_ref, gk_ref, gv_ref = refs
    heads, pair_rows, _ = chunks[0].shape
    rows = pair_rows // 2
    for h in range(heads):
        split_chunks(chunks, h, rows, v_ref=v_ref, kt_ref=kt_ref)
    gk_ref[...] = jnp.zeros_like(gk_ref)
    gv_ref[...] = jnp.zeros_like(gv_ref)

    @tiles(qt_ref.shape[2] // tile)
    def _(j):
        here = tokens_of(j, tile)
        for h in range(heads):
            columns = slice(h * HEAD, (h + 1) * HEAD)
            low = low_ref[h, :, here]
            top, scale, row_dot = (stats_ref[h, i : i + 1, here] for i in range(3))
            shrunk = jnp.exp2((stats_then[h, 0:1, here] - top) * EXPONENT)
            grad_q = grad_q_in[h, :, here] + gradients(
                low.astype(jnp.float32),
                low,
                shrunk,
                (scale, row_dot),
                h,
                here,
                (qt_ref, gt_ref, v_ref, kt_ref, gk_ref, gv_ref),
            )
            if last:
                rows_ref[0, here, columns] = grad_q.T.astype(rows_ref.dtype)
            else:
                grad_q_ref[h, :, here] = grad_q
            if ready:
                rows_ref[0, here, columns] = ready_ref[h, :, here].T.astype(rows_ref.dtype)

    for h in range(heads):
        join_chunks(outs, h, rows, gk_ref, gv_ref)


def cost(heads, rows, tokens, matmuls):
    return pl.CostEstimate(
        flops=2 * matmuls * heads * rows * tokens * HEAD,
        bytes_accessed=heads * (rows + tokens) * HEAD * 8,
        transcendentals=heads * rows * tokens,
    )


def attend(arrived, queries, upstream, send_back):
    heads, pair_rows, _ = arrived[0].shape
    rows = pair_rows // 2
    enc_len = len(arrived) * rows
    tokens = queries.shape[1]
    qt, gt = turned(queries), turned(upstream)
    stats_shape = jax.ShapeDtypeStruct((heads, 8, tokens), jnp.float32)
    wide_shape = jax.ShapeDtypeStruct((heads, HEAD, tokens), jnp.float32)
    rows_shape = jax.ShapeDtypeStruct(queries.shape, queries.dtype)
    compiler_params = params(enc_len)
    turn_at = len(arrived) - len(arrived) // 4
    half = (turn_at + 1) // 2

    def natural(count):
        return pltpu.VMEM((heads, count * rows, HEAD), jnp.bfloat16)

    def across(count, extra=0):
        return pltpu.VMEM((heads, HEAD + extra, count * rows), jnp.bfloat16)

    def sums(count):
        return pltpu.VMEM((heads, count * rows, HEAD), jnp.float32)

    def shapes_of(group):
        return [jax.ShapeDtypeStruct(c.shape, c.dtype) for c in group]

    state, parts = [], []
    for begin, end in ((0, half), (half, turn_at)):
        group, count = arrived[begin:end], end - begin
        low_shape = jax.ShapeDtypeStruct((heads, count * rows, tokens), jnp.bfloat16)
        stats, context, low = pl.pallas_call(
            functools.partial(forward_kernel, count, not state, tile_of(count * rows, tokens)),
            out_shape=[stats_shape, wide_shape, low_shape],
            in_specs=[VMEM] * (count + 1 + len(state)),
            out_specs=[VMEM] * 3,
            scratch_shapes=[natural(count), across(count, 16)],
            compiler_params=compiler_params,
            cost_estimate=cost(heads, count * rows, tokens, 2),
            name="forward",
        )(*group, qt, *state)
        state = [stats, context]
        parts.insert(0, (begin, count, low, stats))

    group, count = arrived[turn_at:], len(arrived) - turn_at
    final, context, grad_q, *grads = pl.pallas_call(
        functools.partial(turn_kernel, count, tile_of(count * rows, tokens)),
        out_shape=[stats_shape, wide_shape, wide_shape] + shapes_of(group),
        in_specs=[VMEM] * (count + 4),
        out_specs=[VMEM] * (count + 3),
        scratch_shapes=[natural(count), natural(count), across(count), across(count, 16)]
        + [sums(count)] * 2,
        compiler_params=compiler_params,
        cost_estimate=cost(heads, count * rows, tokens, 6),
        name="turn",
    )(*group, qt, gt, *state)
    returned = [send_back(turn_at, grads)]

    for i, (begin, count, low, then) in enumerate(parts):
        group = arrived[begin : begin + count]
        ready, last = i == 0, i == len(parts) - 1
        back = returned[i - 1] if i >= 1 else []
        extra = [rows_shape] * (ready or last) + [wide_shape] * (not last)
        outs = pl.pallas_call(
            functools.partial(
                backward_kernel, len(back), count, ready, last, tile_of(count * rows, tokens)
            ),
            out_shape=extra + shapes_of(group),
            in_specs=[ANY] * len(back) + [VMEM] * (count + 6 + ready),
            out_specs=[VMEM] * (len(extra) + count),
            scratch_shapes=[natural(count), across(count)] + [sums(count)] * 2,
            compiler_params=compiler_params,
            cost_estimate=cost(heads, count * rows, tokens, 4),
            name="backward",
        )(*back, *group, qt, gt, low, then, final, grad_q, *([context] if ready else []))
        if ready:
            context_rows = outs[0]
        if last:
            grad_query = outs[0]
        else:
            grad_q = outs[len(extra) - 1]
        returned.append(send_back(begin, outs[len(extra) :]))
    return context_rows, grad_query, returned


def shards(pairs, queries, upstream):
    _, rows, _, width = pairs.shape
    heads = queries.shape[2] // HEAD
    order = offsets()
    arrived = []
    for offset, block in zip(order, pack(pairs, order, heads)):
        block = block.reshape(heads, 2 * rows, HEAD)
        arrived.append(lax.ppermute(block, AXES, route(offset, False)))
    homes = []

    def send_back(begin, blocks):
        there = order[begin : begin + len(blocks)]
        homes.extend(there)
        return [lax.ppermute(b, AXES, route(o, True)) for o, b in zip(there, blocks)]

    context, grad_query, parts = attend(arrived, queries, upstream, send_back)
    returned = [b.reshape(heads, rows, 2, HEAD) for part in parts for b in part]
    return context, grad_query, unpack(returned, homes, width)


def solution(mesh):
    return jax.shard_map(
        shards,
        mesh=mesh,
        in_specs=(
            P("segment", ("seq", "tp"), None, None),
            P("segment", None, ("seq", "tp")),
            P("segment", None, ("seq", "tp")),
        ),
        out_specs=(
            P("segment", None, ("seq", "tp")),
            P("segment", None, ("seq", "tp")),
            P("segment", ("seq", "tp"), None, None),
        ),
        check_vma=False,
    )
```

```python
import functools

import jax
import jax.numpy as jnp
from jax import lax
from jax.experimental import pallas as pl
from jax.experimental.pallas import tpu as pltpu
from jax.sharding import PartitionSpec as P

HEAD = 128
AXES = ("segment", "seq", "tp")
FACTOR = HEAD**-0.5
EXPONENT = FACTOR * 1.4426950408889634
MIB = 1 << 20
NT = ((1,), (1,))
ANY = pl.BlockSpec(memory_space=pl.ANY)
VMEM = pl.BlockSpec(memory_space=pltpu.VMEM)


def offsets():
    seq_count = lax.axis_size("seq")
    tp_count = lax.axis_size("tp")
    near = [(0, dy) for dy in reversed(range(tp_count))]
    order = [(dz, dy) for dz in range(1, seq_count) for dy in reversed(range(tp_count))]
    order.sort(key=lambda o: abs(o[0] - seq_count / 2))
    last = len(order) - 1
    for i, offset in enumerate(near):
        order.insert(last + 2 * i, offset)
    return order


def group_at(offset):
    seq_count = lax.axis_size("seq")
    tp_count = lax.axis_size("tp")
    z = lax.rem(lax.axis_index("seq") + offset[0], seq_count)
    y = lax.rem(lax.axis_index("tp") + offset[1], tp_count)
    return z * tp_count + y


def route(offset, back):
    segments, seq_count, tp_count = (lax.axis_size(a) for a in AXES)
    hops = []
    for s in range(segments):
        for z in range(seq_count):
            for y in range(tp_count):
                source = (s * seq_count + z) * tp_count + y
                s_to = (s + 1) % segments
                z_to = (z + offset[0]) % seq_count
                y_to = (y + offset[1]) % tp_count
                target = (s_to * seq_count + z_to) * tp_count + y_to
                hops.append((target, source) if back else (source, target))
    return hops


def params(enc_len):
    return pltpu.CompilerParams(vmem_limit_bytes=(12 + enc_len * 36 // 4096) * MIB)


def pack(pairs, order, heads):
    _, rows, _, width = pairs.shape
    local = heads * HEAD

    def kernel(pairs_ref, *outs):
        @pl.loop(0, rows // 16)
        def _(r):
            here = pl.ds(pl.multiple_of(r * 16, 16), 16)
            for i, offset in enumerate(order):
                base = group_at(offset) * local
                for h in range(heads):
                    column = pl.multiple_of(base + h * HEAD, HEAD)
                    outs[i][h, here] = pairs_ref[0, here, :, pl.ds(column, HEAD)]

    return pl.pallas_call(
        kernel,
        out_shape=[jax.ShapeDtypeStruct((heads, rows, 2, HEAD), pairs.dtype)] * len(order),
        in_specs=[VMEM],
        out_specs=[VMEM] * len(order),
        compiler_params=pltpu.CompilerParams(vmem_limit_bytes=24 * MIB),
        name="pack",
    )(pairs)


def unpack(blocks, order, width):
    heads, rows, _, _ = blocks[0].shape
    local = heads * HEAD

    def kernel(*refs):
        ins, out = refs[: len(order)], refs[len(order)]

        @pl.loop(0, rows // 16)
        def _(r):
            here = pl.ds(pl.multiple_of(r * 16, 16), 16)
            for i, offset in enumerate(order):
                base = group_at(offset) * local
                for h in range(heads):
                    column = pl.multiple_of(base + h * HEAD, HEAD)
                    out[0, here, :, pl.ds(column, HEAD)] = ins[i][h, here]

    return pl.pallas_call(
        kernel,
        out_shape=jax.ShapeDtypeStruct((1, rows, 2, width), blocks[0].dtype),
        in_specs=[VMEM] * len(order),
        out_specs=VMEM,
        compiler_params=pltpu.CompilerParams(vmem_limit_bytes=24 * MIB),
        name="unpack",
    )(*blocks)


def turned(rows):
    _, tokens, local = rows.shape
    heads = local // HEAD
    tile = 256 if tokens % 256 == 0 else tokens

    def kernel(rows_ref, out_ref):
        for h in range(heads):
            for j in range(tokens // tile):
                here = slice(j * tile, (j + 1) * tile)
                block = rows_ref[0, here, h * HEAD : (h + 1) * HEAD]
                out_ref[h, :, here] = block.astype(jnp.float32).T.astype(rows.dtype)

    return pl.pallas_call(
        kernel,
        out_shape=jax.ShapeDtypeStruct((heads, HEAD, tokens), rows.dtype),
        in_specs=[VMEM],
        out_specs=VMEM,
        compiler_params=pltpu.CompilerParams(vmem_limit_bytes=16 * MIB),
        name="turned",
    )(rows)


def tiles(count):
    def run(body):
        if count <= 2:
            for j in range(count):
                body(j)
        else:
            pl.loop(0, count)(body)

    return run


def tokens_of(j, tile):
    return pl.ds(j * tile if isinstance(j, int) else pl.multiple_of(j * tile, tile), tile)


def tile_of(rows, tokens):
    for parts in range(1, tokens // 256 + 1):
        if tokens % (256 * parts) == 0 and rows * (tokens // parts) * 4 <= 5 * MIB // 4:
            return tokens // parts
    return 256 if tokens % 256 == 0 else tokens


def dot(a, b, contract=((1,), (0,))):
    return lax.dot_general(a, b, (contract, ((), ())), preferred_element_type=jnp.float32)


def shuffle(rows, join):
    to = lax.broadcasted_iota(jnp.int32, (2 * rows, 2 * rows), 1 if join else 0)
    source = lax.broadcasted_iota(jnp.int32, (2 * rows, 2 * rows), 0 if join else 1)
    wanted = jnp.where(to < rows, 2 * to, 2 * (to - rows) + 1)
    return jnp.where(source == wanted, 1.0, 0.0).astype(jnp.bfloat16)


def split_chunks(chunks, h, rows, k_ref=None, v_ref=None, kt_ref=None, vt_ref=None):
    split = shuffle(rows, False)
    for i, chunk in enumerate(chunks):
        both = dot(split, chunk[h])
        here = slice(i * rows, (i + 1) * rows)
        keys, values = both[:rows], both[rows:]
        if k_ref is not None:
            k_ref[h, here, :] = keys.astype(jnp.bfloat16)
        if v_ref is not None:
            v_ref[h, here, :] = values.astype(jnp.bfloat16)
        if kt_ref is not None:
            kt_ref[h, :, here] = keys.T.astype(jnp.bfloat16)
        if vt_ref is not None:
            vt_ref[h, :HEAD, here] = values.T.astype(jnp.bfloat16)
    if vt_ref is not None:
        tail = (vt_ref.shape[1] - HEAD, vt_ref.shape[2])
        vt_ref[h, HEAD:, :] = jnp.ones(tail, jnp.bfloat16)


def join_chunks(outs, h, rows, gk_ref, gv_ref):
    join = shuffle(rows, True)
    for i, out in enumerate(outs):
        here = slice(i * rows, (i + 1) * rows)
        both = jnp.concatenate([gk_ref[h, here, :], gv_ref[h, here, :]], axis=0)
        out[h] = dot(join, both.astype(jnp.bfloat16)).astype(jnp.bfloat16)


def raise_scores(keys, qt, values_t, before):
    scores = dot(keys, qt)
    top = jnp.max(scores, axis=0, keepdims=True)
    if before is not None:
        top = jnp.maximum(top, before[0])
    raised = jnp.exp2((scores - top) * EXPONENT)
    low = raised.astype(jnp.bfloat16)
    summed = dot(values_t, low)
    total, context = summed[HEAD : HEAD + 1], summed[:HEAD]
    if before is not None:
        shrink = jnp.exp2((before[0] - top) * EXPONENT)
        total = total + before[1] * shrink
        context = context + before[2] * shrink
    return low, top, total, context


def forward_kernel(count, first, tile, *refs):
    chunks, refs = refs[:count], refs[count:]
    qt_ref, refs = refs[0], refs[1:]
    if not first:
        stats_in, context_in, refs = refs[0], refs[1], refs[2:]
    stats_ref, context_ref, low_ref, k_ref, vt_ref = refs
    heads, pair_rows, _ = chunks[0].shape
    for h in range(heads):
        split_chunks(chunks, h, pair_rows // 2, k_ref=k_ref, vt_ref=vt_ref)

    @tiles(qt_ref.shape[2] // tile)
    def _(j):
        here = tokens_of(j, tile)
        for h in range(heads):
            before = None
            if not first:
                before = (stats_in[h, 0:1, here], stats_in[h, 1:2, here], context_in[h, :, here])
            low, top, total, context = raise_scores(
                k_ref[h], qt_ref[h, :, here], vt_ref[h], before
            )
            low_ref[h, :, here] = low
            stats_ref[h, 0:1, here] = top
            stats_ref[h, 1:2, here] = total
            context_ref[h, :, here] = context


def gradients(low, scale, row_dot, h, here, refs):
    qt_ref, gt_ref, v_ref, kt_ref, gk_ref, gv_ref = refs
    qt = qt_ref[h, :, here].astype(jnp.float32)
    gt = gt_ref[h, :, here]
    grad_weights = dot(v_ref[h], gt)
    grad_scores = (low.astype(jnp.float32) * (grad_weights - row_dot)).astype(jnp.bfloat16)
    grad_q = dot(kt_ref[h], grad_scores) * (scale * FACTOR)
    gk_ref[h] += dot(grad_scores, (qt * (scale * FACTOR)).astype(jnp.bfloat16), NT)
    gv_ref[h] += dot(low, (gt.astype(jnp.float32) * scale).astype(jnp.bfloat16), NT)
    return grad_q


def turn_kernel(count, others, tile, *refs):
    chunks, refs = refs[:count], refs[count:]
    far_chunks, refs = refs[:others], refs[others:]
    qt_ref, gt_ref, stats_in, context_in, far_low_ref, far_stats = refs[:6]
    stats_ref, context_ref, low_ref, grad_q_ref = refs[6:10]
    outs, refs = refs[10 : 10 + others], refs[10 + others :]
    k_ref, vt_ref, v_ref, kt_ref, gk_ref, gv_ref = refs
    heads, pair_rows, _ = chunks[0].shape
    rows = pair_rows // 2
    for h in range(heads):
        split_chunks(chunks, h, rows, k_ref=k_ref, vt_ref=vt_ref)
        split_chunks(far_chunks, h, rows, v_ref=v_ref, kt_ref=kt_ref)
    gk_ref[...] = jnp.zeros_like(gk_ref)
    gv_ref[...] = jnp.zeros_like(gv_ref)

    @tiles(qt_ref.shape[2] // tile)
    def _(j):
        here = tokens_of(j, tile)
        for h in range(heads):
            before = (stats_in[h, 0:1, here], stats_in[h, 1:2, here], context_in[h, :, here])
            low, top, total, context = raise_scores(
                k_ref[h], qt_ref[h, :, here], vt_ref[h], before
            )
            scale = 1.0 / total
            context = context * scale
            row_dot = jnp.sum(
                gt_ref[h, :, here].astype(jnp.float32) * context, axis=0, keepdims=True
            )
            low_ref[h, :, here] = low
            context_ref[h, :, here] = context
            stats_ref[h, 0:1, here] = top
            stats_ref[h, 1:2, here] = scale
            stats_ref[h, 2:3, here] = row_dot
            shrunk = jnp.exp2((far_stats[h, 0:1, here] - top) * EXPONENT)
            grad_q_ref[h, :, here] = gradients(
                far_low_ref[h, :, here],
                scale * shrunk,
                row_dot,
                h,
                here,
                (qt_ref, gt_ref, v_ref, kt_ref, gk_ref, gv_ref),
            )

    for h in range(heads):
        join_chunks(outs, h, rows, gk_ref, gv_ref)


def backward_kernel(back, count, first, tile, *refs):
    chunks, refs = refs[back : back + count], refs[back + count :]
    qt_ref, gt_ref, low_ref, stats_then, stats_ref, grad_q_in = refs[:6]
    if first:
        ready_ref, rows_ref, grad_q_ref, refs = refs[6], refs[7], refs[8], refs[9:]
    else:
        rows_ref, refs = refs[6], refs[7:]
    outs, refs = refs[:count], refs[count:]
    v_ref, kt_ref, gk_ref, gv_ref = refs
    heads, pair_rows, _ = chunks[0].shape
    rows = pair_rows // 2
    for h in range(heads):
        split_chunks(chunks, h, rows, v_ref=v_ref, kt_ref=kt_ref)
    gk_ref[...] = jnp.zeros_like(gk_ref)
    gv_ref[...] = jnp.zeros_like(gv_ref)

    @tiles(qt_ref.shape[2] // tile)
    def _(j):
        here = tokens_of(j, tile)
        for h in range(heads):
            columns = slice(h * HEAD, (h + 1) * HEAD)
            top, scale, row_dot = (stats_ref[h, i : i + 1, here] for i in range(3))
            shrunk = jnp.exp2((stats_then[h, 0:1, here] - top) * EXPONENT)
            grad_q = grad_q_in[h, :, here] + gradients(
                low_ref[h, :, here],
                scale * shrunk,
                row_dot,
                h,
                here,
                (qt_ref, gt_ref, v_ref, kt_ref, gk_ref, gv_ref),
            )
            if first:
                grad_q_ref[h, :, here] = grad_q
                grad_q = ready_ref[h, :, here]
            rows_ref[0, here, columns] = grad_q.T.astype(rows_ref.dtype)

    for h in range(heads):
        join_chunks(outs, h, rows, gk_ref, gv_ref)


def cost(heads, rows, tokens, matmuls):
    return pl.CostEstimate(
        flops=2 * matmuls * heads * rows * tokens * HEAD,
        bytes_accessed=heads * (rows + tokens) * HEAD * 8,
        transcendentals=heads * rows * tokens,
    )


def attend(arrived, queries, upstream, send_back):
    heads, pair_rows, _ = arrived[0].shape
    rows = pair_rows // 2
    enc_len = len(arrived) * rows
    tokens = queries.shape[1]
    qt, gt = turned(queries), turned(upstream)
    stats_shape = jax.ShapeDtypeStruct((heads, 8, tokens), jnp.float32)
    wide_shape = jax.ShapeDtypeStruct((heads, HEAD, tokens), jnp.float32)
    rows_shape = jax.ShapeDtypeStruct(queries.shape, queries.dtype)
    compiler_params = params(enc_len)
    quarter = max(1, len(arrived) // 4)
    cuts = [0, quarter, len(arrived) - quarter, len(arrived)]

    def natural(count):
        return pltpu.VMEM((heads, count * rows, HEAD), jnp.bfloat16)

    def across(count, extra=0):
        return pltpu.VMEM((heads, HEAD + extra, count * rows), jnp.bfloat16)

    def sums(count):
        return pltpu.VMEM((heads, count * rows, HEAD), jnp.float32)

    def low_of(count):
        return jax.ShapeDtypeStruct((heads, count * rows, tokens), jnp.bfloat16)

    def shapes_of(group):
        return [jax.ShapeDtypeStruct(c.shape, c.dtype) for c in group]

    state, kept = [], []
    for begin, end in zip(cuts[:2], cuts[1:3]):
        group, count = arrived[begin:end], end - begin
        stats, context, low = pl.pallas_call(
            functools.partial(forward_kernel, count, not state, tile_of(count * rows, tokens)),
            out_shape=[stats_shape, wide_shape, low_of(count)],
            in_specs=[VMEM] * (count + 1 + len(state)),
            out_specs=[VMEM] * 3,
            scratch_shapes=[natural(count), across(count, 16)],
            compiler_params=compiler_params,
            cost_estimate=cost(heads, count * rows, tokens, 2),
            name="forward",
        )(*group, qt, *state)
        state = [stats, context]
        kept.append((low, stats))

    far, group = arrived[: cuts[1]], arrived[cuts[2] :]
    others, count = len(far), len(group)
    final, context, low, grad_q, *grads = pl.pallas_call(
        functools.partial(turn_kernel, count, others, tile_of(count * rows, tokens)),
        out_shape=[stats_shape, wide_shape, low_of(count), wide_shape] + shapes_of(far),
        in_specs=[VMEM] * (count + others + 6),
        out_specs=[VMEM] * (others + 4),
        scratch_shapes=[natural(count), across(count, 16), natural(others), across(others)]
        + [sums(others)] * 2,
        compiler_params=compiler_params,
        cost_estimate=cost(heads, count * rows, tokens, 6),
        name="turn",
    )(*group, *far, qt, gt, *state, *kept[0])
    kept.append((low, final))
    returned = [send_back(0, grads)]

    for i, (begin, end) in enumerate(zip(cuts[1:3], cuts[2:])):
        group, count = arrived[begin:end], end - begin
        first = i == 0
        back = [] if first else returned[0]
        shapes = [rows_shape, wide_shape] if first else [rows_shape]
        outs = pl.pallas_call(
            functools.partial(
                backward_kernel, len(back), count, first, tile_of(count * rows, tokens)
            ),
            out_shape=shapes + shapes_of(group),
            in_specs=[ANY] * len(back) + [VMEM] * (count + 6 + first),
            out_specs=[VMEM] * (len(shapes) + count),
            scratch_shapes=[natural(count), across(count)] + [sums(count)] * 2,
            compiler_params=compiler_params,
            cost_estimate=cost(heads, count * rows, tokens, 4),
            name="backward",
        )(*back, *group, qt, gt, *kept[i + 1], final, grad_q, *([context] if first else []))
        if first:
            context_rows, grad_q = outs[:2]
        else:
            grad_query = outs[0]
        returned.append(send_back(begin, outs[len(shapes) :]))
    return context_rows, grad_query, returned


def shards(pairs, queries, upstream):
    _, rows, _, width = pairs.shape
    heads = queries.shape[2] // HEAD
    order = offsets()
    arrived = []
    for offset, block in zip(order, pack(pairs, order, heads)):
        block = block.reshape(heads, 2 * rows, HEAD)
        arrived.append(lax.ppermute(block, AXES, route(offset, False)))
    homes = []

    def send_back(begin, blocks):
        there = order[begin : begin + len(blocks)]
        homes.extend(there)
        return [lax.ppermute(b, AXES, route(o, True)) for o, b in zip(there, blocks)]

    context, grad_query, parts = attend(arrived, queries, upstream, send_back)
    returned = [b.reshape(heads, rows, 2, HEAD) for part in parts for b in part]
    return context, grad_query, unpack(returned, homes, width)


def solution(mesh):
    return jax.shard_map(
        shards,
        mesh=mesh,
        in_specs=(
            P("segment", ("seq", "tp"), None, None),
            P("segment", None, ("seq", "tp")),
            P("segment", None, ("seq", "tp")),
        ),
        out_specs=(
            P("segment", None, ("seq", "tp")),
            P("segment", None, ("seq", "tp")),
            P("segment", ("seq", "tp"), None, None),
        ),
        check_vma=False,
    )
```

```python
import functools

import jax
import jax.numpy as jnp
from jax import lax
from jax.experimental import pallas as pl
from jax.experimental.pallas import tpu as pltpu
from jax.sharding import PartitionSpec as P

HEAD = 128
AXES = ("segment", "seq", "tp")
FACTOR = HEAD**-0.5
EXPONENT = FACTOR * 1.4426950408889634
MIB = 1 << 20
NT = ((1,), (1,))
ANY = pl.BlockSpec(memory_space=pl.ANY)
VMEM = pl.BlockSpec(memory_space=pltpu.VMEM)


def offsets():
    seq_count = lax.axis_size("seq")
    tp_count = lax.axis_size("tp")
    near = [(0, dy) for dy in reversed(range(tp_count))]
    far = [(dz, dy) for dz in range(1, seq_count) for dy in reversed(range(tp_count))]
    far.sort(key=lambda o: -abs(o[0] - seq_count / 2))
    quarter = max(1, (len(near) + len(far)) // 4)
    half = 2 * quarter - 1
    return far[:1] + near[:1] + far[1:half] + far[-quarter:] + far[half:-quarter] + near[1:]


def group_at(offset):
    seq_count = lax.axis_size("seq")
    tp_count = lax.axis_size("tp")
    z = lax.rem(lax.axis_index("seq") + offset[0], seq_count)
    y = lax.rem(lax.axis_index("tp") + offset[1], tp_count)
    return z * tp_count + y


def route(offset, back):
    segments, seq_count, tp_count = (lax.axis_size(a) for a in AXES)
    hops = []
    for s in range(segments):
        for z in range(seq_count):
            for y in range(tp_count):
                source = (s * seq_count + z) * tp_count + y
                s_to = (s + 1) % segments
                z_to = (z + offset[0]) % seq_count
                y_to = (y + offset[1]) % tp_count
                target = (s_to * seq_count + z_to) * tp_count + y_to
                hops.append((target, source) if back else (source, target))
    return hops


def params(enc_len):
    return pltpu.CompilerParams(vmem_limit_bytes=(12 + enc_len * 36 // 4096) * MIB)


def pack(pairs, order, heads):
    _, rows, _, width = pairs.shape
    local = heads * HEAD

    def kernel(pairs_ref, *outs):
        @pl.loop(0, rows // 16)
        def _(r):
            here = pl.ds(pl.multiple_of(r * 16, 16), 16)
            for i, offset in enumerate(order):
                base = group_at(offset) * local
                for h in range(heads):
                    column = pl.multiple_of(base + h * HEAD, HEAD)
                    outs[i][h, here] = pairs_ref[0, here, :, pl.ds(column, HEAD)]

    return pl.pallas_call(
        kernel,
        out_shape=[jax.ShapeDtypeStruct((heads, rows, 2, HEAD), pairs.dtype)] * len(order),
        in_specs=[VMEM],
        out_specs=[VMEM] * len(order),
        compiler_params=pltpu.CompilerParams(vmem_limit_bytes=24 * MIB),
        name="pack",
    )(pairs)


def unpack(blocks, order, width):
    heads, rows, _, _ = blocks[0].shape
    local = heads * HEAD

    def kernel(*refs):
        ins, out = refs[: len(order)], refs[len(order)]

        @pl.loop(0, rows // 16)
        def _(r):
            here = pl.ds(pl.multiple_of(r * 16, 16), 16)
            for i, offset in enumerate(order):
                base = group_at(offset) * local
                for h in range(heads):
                    column = pl.multiple_of(base + h * HEAD, HEAD)
                    out[0, here, :, pl.ds(column, HEAD)] = ins[i][h, here]

    return pl.pallas_call(
        kernel,
        out_shape=jax.ShapeDtypeStruct((1, rows, 2, width), blocks[0].dtype),
        in_specs=[VMEM] * len(order),
        out_specs=VMEM,
        compiler_params=pltpu.CompilerParams(vmem_limit_bytes=24 * MIB),
        name="unpack",
    )(*blocks)


def turned(rows):
    _, tokens, local = rows.shape
    heads = local // HEAD
    tile = 256 if tokens % 256 == 0 else tokens

    def kernel(rows_ref, out_ref):
        for h in range(heads):
            for j in range(tokens // tile):
                here = slice(j * tile, (j + 1) * tile)
                block = rows_ref[0, here, h * HEAD : (h + 1) * HEAD]
                out_ref[h, :, here] = block.astype(jnp.float32).T.astype(rows.dtype)

    return pl.pallas_call(
        kernel,
        out_shape=jax.ShapeDtypeStruct((heads, HEAD, tokens), rows.dtype),
        in_specs=[VMEM],
        out_specs=VMEM,
        compiler_params=pltpu.CompilerParams(vmem_limit_bytes=16 * MIB),
        name="turned",
    )(rows)


def tiles(count):
    def run(body):
        if count <= 2:
            for j in range(count):
                body(j)
        else:
            pl.loop(0, count)(body)

    return run


def tokens_of(j, tile):
    return pl.ds(j * tile if isinstance(j, int) else pl.multiple_of(j * tile, tile), tile)


def tile_of(rows, tokens):
    for parts in range(1, tokens // 256 + 1):
        if tokens % (256 * parts) == 0 and rows * (tokens // parts) * 4 <= 5 * MIB // 4:
            return tokens // parts
    return 256 if tokens % 256 == 0 else tokens


def dot(a, b, contract=((1,), (0,))):
    return lax.dot_general(a, b, (contract, ((), ())), preferred_element_type=jnp.float32)


def shuffle(rows, join):
    to = lax.broadcasted_iota(jnp.int32, (2 * rows, 2 * rows), 1 if join else 0)
    source = lax.broadcasted_iota(jnp.int32, (2 * rows, 2 * rows), 0 if join else 1)
    wanted = jnp.where(to < rows, 2 * to, 2 * (to - rows) + 1)
    return jnp.where(source == wanted, 1.0, 0.0).astype(jnp.bfloat16)


def split_chunks(chunks, h, rows, k_ref=None, v_ref=None, kt_ref=None, vt_ref=None):
    split = shuffle(rows, False)
    for i, chunk in enumerate(chunks):
        both = dot(split, chunk[h])
        here = slice(i * rows, (i + 1) * rows)
        keys, values = both[:rows], both[rows:]
        if k_ref is not None:
            k_ref[h, here, :] = keys.astype(jnp.bfloat16)
        if v_ref is not None:
            v_ref[h, here, :] = values.astype(jnp.bfloat16)
        if kt_ref is not None:
            kt_ref[h, :, here] = keys.T.astype(jnp.bfloat16)
        if vt_ref is not None:
            vt_ref[h, :HEAD, here] = values.T.astype(jnp.bfloat16)
    if vt_ref is not None:
        tail = (vt_ref.shape[1] - HEAD, vt_ref.shape[2])
        vt_ref[h, HEAD:, :] = jnp.ones(tail, jnp.bfloat16)


def join_chunks(outs, h, rows, gk_ref, gv_ref):
    join = shuffle(rows, True)
    for i, out in enumerate(outs):
        here = slice(i * rows, (i + 1) * rows)
        both = jnp.concatenate([gk_ref[h, here, :], gv_ref[h, here, :]], axis=0)
        out[h] = dot(join, both.astype(jnp.bfloat16)).astype(jnp.bfloat16)


def raise_scores(keys, qt, values_t, before):
    scores = dot(keys, qt)
    top = jnp.max(scores, axis=0, keepdims=True)
    if before is not None:
        top = jnp.maximum(top, before[0])
    raised = jnp.exp2((scores - top) * EXPONENT)
    low = raised.astype(jnp.bfloat16)
    summed = dot(values_t, low)
    total, context = summed[HEAD : HEAD + 1], summed[:HEAD]
    if before is not None:
        shrink = jnp.exp2((before[0] - top) * EXPONENT)
        total = total + before[1] * shrink
        context = context + before[2] * shrink
    return low, top, total, context


def forward_kernel(count, first, tile, *refs):
    chunks, refs = refs[:count], refs[count:]
    qt_ref, refs = refs[0], refs[1:]
    if not first:
        stats_in, context_in, refs = refs[0], refs[1], refs[2:]
    stats_ref, context_ref, low_ref, k_ref, vt_ref = refs
    heads, pair_rows, _ = chunks[0].shape
    for h in range(heads):
        split_chunks(chunks, h, pair_rows // 2, k_ref=k_ref, vt_ref=vt_ref)

    @tiles(qt_ref.shape[2] // tile)
    def _(j):
        here = tokens_of(j, tile)
        for h in range(heads):
            before = None
            if not first:
                before = (stats_in[h, 0:1, here], stats_in[h, 1:2, here], context_in[h, :, here])
            low, top, total, context = raise_scores(
                k_ref[h], qt_ref[h, :, here], vt_ref[h], before
            )
            low_ref[h, :, here] = low
            stats_ref[h, 0:1, here] = top
            stats_ref[h, 1:2, here] = total
            context_ref[h, :, here] = context


def gradients(low, scale, row_dot, h, here, refs):
    qt_ref, gt_ref, v_ref, kt_ref, gk_ref, gv_ref = refs
    qt = qt_ref[h, :, here].astype(jnp.float32)
    gt = gt_ref[h, :, here]
    grad_weights = dot(v_ref[h], gt)
    grad_scores = (low.astype(jnp.float32) * (grad_weights - row_dot)).astype(jnp.bfloat16)
    grad_q = dot(kt_ref[h], grad_scores) * (scale * FACTOR)
    gk_ref[h] += dot(grad_scores, (qt * (scale * FACTOR)).astype(jnp.bfloat16), NT)
    gv_ref[h] += dot(low, (gt.astype(jnp.float32) * scale).astype(jnp.bfloat16), NT)
    return grad_q


def turn_kernel(count, others, tile, *refs):
    chunks, refs = refs[:count], refs[count:]
    far_chunks, refs = refs[:others], refs[others:]
    qt_ref, gt_ref, stats_in, context_in, far_low_ref, far_stats = refs[:6]
    stats_ref, context_ref, low_ref, grad_q_ref = refs[6:10]
    outs, refs = refs[10 : 10 + others], refs[10 + others :]
    k_ref, vt_ref, v_ref, kt_ref, gk_ref, gv_ref = refs
    heads, pair_rows, _ = chunks[0].shape
    rows = pair_rows // 2
    for h in range(heads):
        split_chunks(chunks, h, rows, k_ref=k_ref, vt_ref=vt_ref)
        split_chunks(far_chunks, h, rows, v_ref=v_ref, kt_ref=kt_ref)
    gk_ref[...] = jnp.zeros_like(gk_ref)
    gv_ref[...] = jnp.zeros_like(gv_ref)

    @tiles(qt_ref.shape[2] // tile)
    def _(j):
        here = tokens_of(j, tile)
        for h in range(heads):
            before = (stats_in[h, 0:1, here], stats_in[h, 1:2, here], context_in[h, :, here])
            low, top, total, context = raise_scores(
                k_ref[h], qt_ref[h, :, here], vt_ref[h], before
            )
            scale = 1.0 / total
            context = context * scale
            row_dot = jnp.sum(
                gt_ref[h, :, here].astype(jnp.float32) * context, axis=0, keepdims=True
            )
            low_ref[h, :, here] = low
            context_ref[h, :, here] = context
            stats_ref[h, 0:1, here] = top
            stats_ref[h, 1:2, here] = scale
            stats_ref[h, 2:3, here] = row_dot
            shrunk = jnp.exp2((far_stats[h, 0:1, here] - top) * EXPONENT)
            grad_q_ref[h, :, here] = gradients(
                far_low_ref[h, :, here],
                scale * shrunk,
                row_dot,
                h,
                here,
                (qt_ref, gt_ref, v_ref, kt_ref, gk_ref, gv_ref),
            )

    for h in range(heads):
        join_chunks(outs, h, rows, gk_ref, gv_ref)


def backward_kernel(back, counts, first, tile, *refs):
    refs = refs[back:]
    groups = []
    for count in counts:
        groups.append((refs[:count], refs[count], refs[count + 1]))
        refs = refs[count + 2 :]
    qt_ref, gt_ref, stats_ref, grad_q_in = refs[:4]
    if first:
        ready_ref, rows_ref, grad_q_ref, refs = refs[4], refs[5], refs[6], refs[7:]
    else:
        rows_ref, refs = refs[4], refs[5:]
    outs, refs = refs[: sum(counts)], refs[sum(counts) :]
    scratch = [refs[i : i + 4] for i in range(0, len(refs), 4)]
    heads, pair_rows, _ = groups[0][0][0].shape
    rows = pair_rows // 2
    for (chunks, _, _), (v_ref, kt_ref, gk_ref, gv_ref) in zip(groups, scratch):
        for h in range(heads):
            split_chunks(chunks, h, rows, v_ref=v_ref, kt_ref=kt_ref)
        gk_ref[...] = jnp.zeros_like(gk_ref)
        gv_ref[...] = jnp.zeros_like(gv_ref)

    @tiles(qt_ref.shape[2] // tile)
    def _(j):
        here = tokens_of(j, tile)
        for h in range(heads):
            columns = slice(h * HEAD, (h + 1) * HEAD)
            top, scale, row_dot = (stats_ref[h, i : i + 1, here] for i in range(3))
            grad_q = grad_q_in[h, :, here]
            for (_, low_ref, then_ref), own in zip(groups, scratch):
                shrunk = jnp.exp2((then_ref[h, 0:1, here] - top) * EXPONENT)
                grad_q = grad_q + gradients(
                    low_ref[h, :, here], scale * shrunk, row_dot, h, here, (qt_ref, gt_ref, *own)
                )
            if first:
                grad_q_ref[h, :, here] = grad_q
                grad_q = ready_ref[h, :, here]
            rows_ref[0, here, columns] = grad_q.T.astype(rows_ref.dtype)

    for count, (_, _, gk_ref, gv_ref) in zip(counts, scratch):
        for h in range(heads):
            join_chunks(outs[:count], h, rows, gk_ref, gv_ref)
        outs = outs[count:]


def cost(heads, rows, tokens, matmuls):
    return pl.CostEstimate(
        flops=2 * matmuls * heads * rows * tokens * HEAD,
        bytes_accessed=heads * (rows + tokens) * HEAD * 8,
        transcendentals=heads * rows * tokens,
    )


def attend(arrived, queries, upstream, send_back):
    heads, pair_rows, _ = arrived[0].shape
    rows = pair_rows // 2
    enc_len = len(arrived) * rows
    tokens = queries.shape[1]
    qt, gt = turned(queries), turned(upstream)
    stats_shape = jax.ShapeDtypeStruct((heads, 8, tokens), jnp.float32)
    wide_shape = jax.ShapeDtypeStruct((heads, HEAD, tokens), jnp.float32)
    rows_shape = jax.ShapeDtypeStruct(queries.shape, queries.dtype)
    compiler_params = params(enc_len)
    quarter = max(1, len(arrived) // 4)
    cuts = [0, quarter, 2 * quarter, 3 * quarter, len(arrived)]
    groups = [arrived[a:b] for a, b in zip(cuts[:-1], cuts[1:])]

    def natural(count):
        return pltpu.VMEM((heads, count * rows, HEAD), jnp.bfloat16)

    def across(count, extra=0):
        return pltpu.VMEM((heads, HEAD + extra, count * rows), jnp.bfloat16)

    def sums(count):
        return pltpu.VMEM((heads, count * rows, HEAD), jnp.float32)

    def low_of(count):
        return jax.ShapeDtypeStruct((heads, count * rows, tokens), jnp.bfloat16)

    def shapes_of(group):
        return [jax.ShapeDtypeStruct(c.shape, c.dtype) for c in group]

    state, kept = [], []
    for group in groups[:-1]:
        count = len(group)
        stats, context, low = pl.pallas_call(
            functools.partial(forward_kernel, count, not state, tile_of(count * rows, tokens)),
            out_shape=[stats_shape, wide_shape, low_of(count)],
            in_specs=[VMEM] * (count + 1 + len(state)),
            out_specs=[VMEM] * 3,
            scratch_shapes=[natural(count), across(count, 16)],
            compiler_params=compiler_params,
            cost_estimate=cost(heads, count * rows, tokens, 2),
            name="forward",
        )(*group, qt, *state)
        state = [stats, context]
        kept.append((low, stats))

    far, group = groups[-2], groups[-1]
    others, count = len(far), len(group)
    final, context, low, grad_q, *grads = pl.pallas_call(
        functools.partial(turn_kernel, count, others, tile_of(count * rows, tokens)),
        out_shape=[stats_shape, wide_shape, low_of(count), wide_shape] + shapes_of(far),
        in_specs=[VMEM] * (count + others + 6),
        out_specs=[VMEM] * (others + 4),
        scratch_shapes=[natural(count), across(count, 16), natural(others), across(others)]
        + [sums(others)] * 2,
        compiler_params=compiler_params,
        cost_estimate=cost(heads, count * rows, tokens, 6),
        name="turn",
    )(*group, *far, qt, gt, *state, *kept[-1])
    kept.append((low, final))
    returned = [send_back(cuts[-3], grads)]

    for first, part in ((True, [1, 3]), (False, [0])):
        counts = [len(groups[i]) for i in part]
        back = [] if first else returned[0]
        operands = []
        for i in part:
            operands += [*groups[i], *kept[i]]
        shapes = [rows_shape, wide_shape] if first else [rows_shape]
        outs = pl.pallas_call(
            functools.partial(
                backward_kernel, len(back), counts, first, tile_of(max(counts) * rows, tokens)
            ),
            out_shape=shapes + shapes_of(sum((groups[i] for i in part), [])),
            in_specs=[ANY] * len(back) + [VMEM] * (len(operands) + 4 + first),
            out_specs=[VMEM] * (len(shapes) + sum(counts)),
            scratch_shapes=[
                shape
                for count in counts
                for shape in (natural(count), across(count), sums(count), sums(count))
            ],
            compiler_params=compiler_params,
            cost_estimate=cost(heads, sum(counts) * rows, tokens, 4),
            name="backward",
        )(*back, *operands, qt, gt, final, grad_q, *([context] if first else []))
        if first:
            context_rows, grad_q = outs[:2]
        else:
            grad_query = outs[0]
        blocks = list(outs[len(shapes) :])
        for i in part:
            returned.append(send_back(cuts[i], blocks[: len(groups[i])]))
            blocks = blocks[len(groups[i]) :]
    return context_rows, grad_query, returned


def shards(pairs, queries, upstream):
    _, rows, _, width = pairs.shape
    heads = queries.shape[2] // HEAD
    order = offsets()
    arrived = []
    for offset, block in zip(order, pack(pairs, order, heads)):
        block = block.reshape(heads, 2 * rows, HEAD)
        arrived.append(lax.ppermute(block, AXES, route(offset, False)))
    homes = []

    def send_back(begin, blocks):
        there = order[begin : begin + len(blocks)]
        homes.extend(there)
        return [lax.ppermute(b, AXES, route(o, True)) for o, b in zip(there, blocks)]

    context, grad_query, parts = attend(arrived, queries, upstream, send_back)
    returned = [b.reshape(heads, rows, 2, HEAD) for part in parts for b in part]
    return context, grad_query, unpack(returned, homes, width)


def solution(mesh):
    return jax.shard_map(
        shards,
        mesh=mesh,
        in_specs=(
            P("segment", ("seq", "tp"), None, None),
            P("segment", None, ("seq", "tp")),
            P("segment", None, ("seq", "tp")),
        ),
        out_specs=(
            P("segment", None, ("seq", "tp")),
            P("segment", None, ("seq", "tp")),
            P("segment", ("seq", "tp"), None, None),
        ),
        check_vma=False,
    )
```

```python
import functools

import jax
import jax.numpy as jnp
from jax import lax
from jax.experimental import pallas as pl
from jax.experimental.pallas import tpu as pltpu
from jax.sharding import PartitionSpec as P

HEAD = 128
AXES = ("segment", "seq", "tp")
FACTOR = HEAD**-0.5
EXPONENT = FACTOR * 1.4426950408889634
MIB = 1 << 20
NT = ((1,), (1,))
ANY = pl.BlockSpec(memory_space=pl.ANY)
HBM = pl.BlockSpec(memory_space=pltpu.HBM)
VMEM = pl.BlockSpec(memory_space=pltpu.VMEM)


def offsets():
    seq_count = lax.axis_size("seq")
    tp_count = lax.axis_size("tp")
    near = [(0, dy) for dy in reversed(range(tp_count))]
    far = [(dz, dy) for dz in range(1, seq_count) for dy in reversed(range(tp_count))]
    far.sort(key=lambda o: -abs(o[0] - seq_count / 2))
    quarter = max(1, (len(near) + len(far)) // 4)
    return far[:1] + near[:1] + far[1:-quarter] + near[1:] + far[-quarter:]


def group_at(offset):
    seq_count = lax.axis_size("seq")
    tp_count = lax.axis_size("tp")
    z = lax.rem(lax.axis_index("seq") + offset[0], seq_count)
    y = lax.rem(lax.axis_index("tp") + offset[1], tp_count)
    return z * tp_count + y


def route(offset, back):
    segments, seq_count, tp_count = (lax.axis_size(a) for a in AXES)
    hops = []
    for s in range(segments):
        for z in range(seq_count):
            for y in range(tp_count):
                source = (s * seq_count + z) * tp_count + y
                s_to = (s + 1) % segments
                z_to = (z + offset[0]) % seq_count
                y_to = (y + offset[1]) % tp_count
                target = (s_to * seq_count + z_to) * tp_count + y_to
                hops.append((target, source) if back else (source, target))
    return hops


def params(enc_len):
    return pltpu.CompilerParams(vmem_limit_bytes=(12 + enc_len * 36 // 4096) * MIB)


def pack(pairs, pieces):
    _, rows, _, width = pairs.shape
    groups = lax.axis_size("seq") * lax.axis_size("tp")
    local = width // groups

    def kernel(pairs_ref, *outs):
        @pl.loop(0, rows // 16)
        def _(r):
            here = pl.ds(pl.multiple_of(r * 16, 16), 16)
            for out, (offset, head, count) in zip(outs, pieces):
                base = group_at(offset) * local + head * HEAD
                for h in range(count):
                    column = pl.multiple_of(base + h * HEAD, HEAD)
                    out[h, here] = pairs_ref[0, here, :, pl.ds(column, HEAD)]

    return pl.pallas_call(
        kernel,
        out_shape=[
            jax.ShapeDtypeStruct((count, rows, 2, HEAD), pairs.dtype) for _, _, count in pieces
        ],
        in_specs=[VMEM],
        out_specs=[VMEM] * len(pieces),
        compiler_params=pltpu.CompilerParams(vmem_limit_bytes=24 * MIB),
        name="pack",
    )(pairs)


def unpack(blocks, pieces, width):
    _, rows, _, _ = blocks[0].shape
    groups = lax.axis_size("seq") * lax.axis_size("tp")
    local = width // groups
    parts = 4 if rows % 64 == 0 else 1
    size = rows // parts

    def kernel(*refs):
        ins, out, held, sem = refs[: len(pieces)], refs[len(pieces)], refs[-2], refs[-1]

        def store(r):
            here = pl.ds(pl.multiple_of(r * size, size), size)
            return pltpu.make_async_copy(held.at[here], out.at[0, here], sem.at[r])

        @pl.loop(0, parts)
        def _(r):
            here = pl.ds(pl.multiple_of(r * size, size), size)
            for block, (offset, head, count) in zip(ins, pieces):
                base = group_at(offset) * local + head * HEAD
                for h in range(count):
                    column = pl.multiple_of(base + h * HEAD, HEAD)
                    held[here, :, pl.ds(column, HEAD)] = block[h, here]
            store(r).start()

        for r in range(parts):
            store(r).wait()

    return pl.pallas_call(
        kernel,
        out_shape=jax.ShapeDtypeStruct((1, rows, 2, width), blocks[0].dtype),
        in_specs=[VMEM] * len(pieces),
        out_specs=HBM,
        scratch_shapes=[
            pltpu.VMEM((rows, 2, width), blocks[0].dtype),
            pltpu.SemaphoreType.DMA((parts,)),
        ],
        compiler_params=pltpu.CompilerParams(vmem_limit_bytes=24 * MIB),
        name="unpack",
    )(*blocks)


def turned(rows):
    _, tokens, local = rows.shape
    heads = local // HEAD
    tile = 256 if tokens % 256 == 0 else tokens

    def kernel(rows_ref, out_ref):
        for h in range(heads):
            for j in range(tokens // tile):
                here = slice(j * tile, (j + 1) * tile)
                block = rows_ref[0, here, h * HEAD : (h + 1) * HEAD]
                out_ref[h, :, here] = block.astype(jnp.float32).T.astype(rows.dtype)

    return pl.pallas_call(
        kernel,
        out_shape=jax.ShapeDtypeStruct((heads, HEAD, tokens), rows.dtype),
        in_specs=[VMEM],
        out_specs=VMEM,
        compiler_params=pltpu.CompilerParams(vmem_limit_bytes=16 * MIB),
        name="turned",
    )(rows)


def tiles(count):
    def run(body):
        if count <= 2:
            for j in range(count):
                body(j)
        else:
            pl.loop(0, count)(body)

    return run


def tokens_of(j, tile):
    return pl.ds(j * tile if isinstance(j, int) else pl.multiple_of(j * tile, tile), tile)


def tile_of(rows, tokens):
    for parts in range(1, tokens // 256 + 1):
        if tokens % (256 * parts) == 0 and rows * (tokens // parts) * 4 <= 5 * MIB // 4:
            return tokens // parts
    return 256 if tokens % 256 == 0 else tokens


def dot(a, b, contract=((1,), (0,))):
    return lax.dot_general(a, b, (contract, ((), ())), preferred_element_type=jnp.float32)


def shuffle(rows, join):
    to = lax.broadcasted_iota(jnp.int32, (2 * rows, 2 * rows), 1 if join else 0)
    source = lax.broadcasted_iota(jnp.int32, (2 * rows, 2 * rows), 0 if join else 1)
    wanted = jnp.where(to < rows, 2 * to, 2 * (to - rows) + 1)
    return jnp.where(source == wanted, 1.0, 0.0).astype(jnp.bfloat16)


def split_chunks(chunks, h, rows, k_ref=None, v_ref=None, kt_ref=None, vt_ref=None):
    split = shuffle(rows, False)
    for i, chunk in enumerate(chunks):
        both = dot(split, chunk[h])
        here = slice(i * rows, (i + 1) * rows)
        keys, values = both[:rows], both[rows:]
        if k_ref is not None:
            k_ref[h, here, :] = keys.astype(jnp.bfloat16)
        if v_ref is not None:
            v_ref[h, here, :] = values.astype(jnp.bfloat16)
        if kt_ref is not None:
            kt_ref[h, :, here] = keys.T.astype(jnp.bfloat16)
        if vt_ref is not None:
            vt_ref[h, :HEAD, here] = values.T.astype(jnp.bfloat16)
    if vt_ref is not None:
        tail = (vt_ref.shape[1] - HEAD, vt_ref.shape[2])
        vt_ref[h, HEAD:, :] = jnp.ones(tail, jnp.bfloat16)


def join_chunks(outs, h, rows, gk_ref, gv_ref):
    join = shuffle(rows, True)
    for i, out in enumerate(outs):
        here = slice(i * rows, (i + 1) * rows)
        both = jnp.concatenate([gk_ref[h, here, :], gv_ref[h, here, :]], axis=0)
        out[h] = dot(join, both.astype(jnp.bfloat16)).astype(jnp.bfloat16)


def raise_scores(keys, qt, values_t, before):
    scores = dot(keys, qt)
    top = jnp.max(scores, axis=0, keepdims=True)
    if before is not None:
        top = jnp.maximum(top, before[0])
    raised = jnp.exp2((scores - top) * EXPONENT)
    low = raised.astype(jnp.bfloat16)
    summed = dot(values_t, low)
    total, context = summed[HEAD : HEAD + 1], summed[:HEAD]
    if before is not None:
        shrink = jnp.exp2((before[0] - top) * EXPONENT)
        total = total + before[1] * shrink
        context = context + before[2] * shrink
    return raised, low, top, total, context


def forward_kernel(count, first, tile, *refs):
    chunks, refs = refs[:count], refs[count:]
    qt_ref, refs = refs[0], refs[1:]
    if not first:
        stats_in, context_in, refs = refs[0], refs[1], refs[2:]
    stats_ref, context_ref, low_ref, k_ref, vt_ref = refs
    heads, pair_rows, _ = chunks[0].shape
    for h in range(heads):
        split_chunks(chunks, h, pair_rows // 2, k_ref=k_ref, vt_ref=vt_ref)

    @tiles(qt_ref.shape[2] // tile)
    def _(j):
        here = tokens_of(j, tile)
        for h in range(heads):
            before = None
            if not first:
                before = (stats_in[h, 0:1, here], stats_in[h, 1:2, here], context_in[h, :, here])
            _, low, top, total, context = raise_scores(
                k_ref[h], qt_ref[h, :, here], vt_ref[h], before
            )
            low_ref[h, :, here] = low
            stats_ref[h, 0:1, here] = top
            stats_ref[h, 1:2, here] = total
            context_ref[h, :, here] = context


def gradients(raised, low, scale, row_dot, qt, gt, refs, h):
    v_ref, kt_ref, gk_ref, gv_ref = refs
    grad_weights = dot(v_ref[h], gt)
    grad_scores = (raised * (grad_weights - row_dot)).astype(jnp.bfloat16)
    grad_q = dot(kt_ref[h], grad_scores) * (scale * FACTOR)
    scaled = (qt.astype(jnp.float32) * (scale * FACTOR)).astype(jnp.bfloat16)
    gk_ref[h] += dot(grad_scores, scaled, NT)
    gv_ref[h] += dot(low, (gt.astype(jnp.float32) * scale).astype(jnp.bfloat16), NT)
    return grad_q


def turn_kernel(count, head, tile, *refs):
    chunks, refs = refs[:count], refs[count:]
    qt_ref, gt_ref, stats_in, context_in = refs[:4]
    stats_ref, context_ref, grad_q_ref = refs[4:7]
    outs, refs = refs[7 : 7 + count], refs[7 + count :]
    k_ref, vt_ref, v_ref, kt_ref, gk_ref, gv_ref = refs
    rows = chunks[0].shape[1] // 2
    split_chunks(chunks, 0, rows, k_ref, v_ref, kt_ref, vt_ref)
    gk_ref[...] = jnp.zeros_like(gk_ref)
    gv_ref[...] = jnp.zeros_like(gv_ref)

    @tiles(qt_ref.shape[2] // tile)
    def _(j):
        here = tokens_of(j, tile)
        qt, gt = qt_ref[head, :, here], gt_ref[head, :, here]
        before = (
            stats_in[head, 0:1, here],
            stats_in[head, 1:2, here],
            context_in[head, :, here],
        )
        raised, low, top, total, context = raise_scores(k_ref[0], qt, vt_ref[0], before)
        scale = 1.0 / total
        context = context * scale
        row_dot = jnp.sum(gt.astype(jnp.float32) * context, axis=0, keepdims=True)
        context_ref[0, :, here] = context
        stats_ref[0, 0:1, here] = top
        stats_ref[0, 1:2, here] = scale
        stats_ref[0, 2:3, here] = row_dot
        grad_q_ref[0, :, here] = gradients(
            raised, low, scale, row_dot, qt, gt, (v_ref, kt_ref, gk_ref, gv_ref), 0
        )

    join_chunks(outs, 0, rows, gk_ref, gv_ref)


def backward_kernel(back, counts, heads, first, tile, *refs):
    refs = refs[back:]
    groups = []
    for count in counts:
        groups.append((refs[:count], refs[count], refs[count + 1]))
        refs = refs[count + 2 :]
    qt_ref, gt_ref, refs = refs[0], refs[1], refs[2:]
    final, grads_in, refs = refs[:heads], refs[heads : 2 * heads], refs[2 * heads :]
    if first:
        ready, rows_ref, grads_out, refs = (
            refs[:heads],
            refs[heads],
            refs[heads + 1 : 2 * heads + 1],
            refs[2 * heads + 1 :],
        )
    else:
        rows_ref, refs = refs[0], refs[1:]
    outs, refs = refs[: sum(counts)], refs[sum(counts) :]
    scratch = [refs[i : i + 4] for i in range(0, len(refs), 4)]
    rows = groups[0][0][0].shape[1] // 2
    for (chunks, _, _), (v_ref, kt_ref, gk_ref, gv_ref) in zip(groups, scratch):
        for h in range(heads):
            split_chunks(chunks, h, rows, v_ref=v_ref, kt_ref=kt_ref)
        gk_ref[...] = jnp.zeros_like(gk_ref)
        gv_ref[...] = jnp.zeros_like(gv_ref)

    @tiles(qt_ref.shape[2] // tile)
    def _(j):
        here = tokens_of(j, tile)
        for h in range(heads):
            columns = slice(h * HEAD, (h + 1) * HEAD)
            qt, gt = qt_ref[h, :, here], gt_ref[h, :, here]
            top, scale, row_dot = (final[h][0, i : i + 1, here] for i in range(3))
            grad_q = grads_in[h][0, :, here]
            for (_, low_ref, then_ref), own in zip(groups, scratch):
                shrunk = jnp.exp2((then_ref[h, 0:1, here] - top) * EXPONENT)
                low = low_ref[h, :, here]
                raised = low.astype(jnp.float32)
                grad_q = grad_q + gradients(
                    raised, low, scale * shrunk, row_dot, qt, gt, own, h
                )
            if first:
                grads_out[h][0, :, here] = grad_q
                grad_q = ready[h][0, :, here]
            rows_ref[0, here, columns] = grad_q.T.astype(rows_ref.dtype)

    for count, (_, _, gk_ref, gv_ref) in zip(counts, scratch):
        for h in range(heads):
            join_chunks(outs[:count], h, rows, gk_ref, gv_ref)
        outs = outs[count:]


def cost(heads, rows, tokens, matmuls):
    return pl.CostEstimate(
        flops=2 * matmuls * heads * rows * tokens * HEAD,
        bytes_accessed=heads * (rows + tokens) * HEAD * 8,
        transcendentals=heads * rows * tokens,
    )


def attend(groups, last, queries, upstream, send_back):
    heads, pair_rows, _ = groups[0][0].shape
    rows = pair_rows // 2
    enc_len = (sum(len(g) for g in groups) + len(last[0])) * rows
    tokens = queries.shape[1]
    qt, gt = turned(queries), turned(upstream)
    stats_shape = jax.ShapeDtypeStruct((heads, 8, tokens), jnp.float32)
    wide_shape = jax.ShapeDtypeStruct((heads, HEAD, tokens), jnp.float32)
    stats_one = jax.ShapeDtypeStruct((1, 8, tokens), jnp.float32)
    wide_one = jax.ShapeDtypeStruct((1, HEAD, tokens), jnp.float32)
    rows_shape = jax.ShapeDtypeStruct(queries.shape, queries.dtype)
    compiler_params = params(enc_len)

    def natural(heads, count):
        return pltpu.VMEM((heads, count * rows, HEAD), jnp.bfloat16)

    def across(heads, count, extra=0):
        return pltpu.VMEM((heads, HEAD + extra, count * rows), jnp.bfloat16)

    def sums(heads, count):
        return pltpu.VMEM((heads, count * rows, HEAD), jnp.float32)

    def shapes_of(group):
        return [jax.ShapeDtypeStruct(c.shape, c.dtype) for c in group]

    state, kept = [], []
    for group in groups:
        count = len(group)
        low_shape = jax.ShapeDtypeStruct((heads, count * rows, tokens), jnp.bfloat16)
        stats, context, low = pl.pallas_call(
            functools.partial(forward_kernel, count, not state, tile_of(count * rows, tokens)),
            out_shape=[stats_shape, wide_shape, low_shape],
            in_specs=[VMEM] * (count + 1 + len(state)),
            out_specs=[VMEM] * 3,
            scratch_shapes=[natural(heads, count), across(heads, count, 16)],
            compiler_params=compiler_params,
            cost_estimate=cost(heads, count * rows, tokens, 2),
            name="forward",
        )(*group, qt, *state)
        state = [stats, context]
        kept.append((low, stats))

    final, contexts, grads_q, returned = [], [], [], []
    for h, group in enumerate(last):
        count = len(group)
        stats, context, grad_q, *grads = pl.pallas_call(
            functools.partial(turn_kernel, count, h, tile_of(count * rows, tokens)),
            out_shape=[stats_one, wide_one, wide_one] + shapes_of(group),
            in_specs=[VMEM] * (count + 4),
            out_specs=[VMEM] * (count + 3),
            scratch_shapes=[natural(1, count), across(1, count, 16)]
            + [natural(1, count), across(1, count)]
            + [sums(1, count)] * 2,
            compiler_params=compiler_params,
            cost_estimate=cost(1, count * rows, tokens, 6),
            name="turn",
        )(*group, qt, gt, *state)
        final.append(stats)
        contexts.append(context)
        grads_q.append(grad_q)
        returned.append(send_back(len(groups), h, grads))

    for part in (list(range(1, len(groups))), [0]):
        first = part[0] > 0
        counts = [len(groups[i]) for i in part]
        back = [] if first else sum(returned, [])
        operands = []
        for i in part:
            operands += [*groups[i], *kept[i]]
        operands += [qt, gt, *final, *grads_q, *(contexts if first else [])]
        shapes = [rows_shape] + ([wide_one] * heads if first else [])
        outs = pl.pallas_call(
            functools.partial(
                backward_kernel,
                len(back),
                counts,
                heads,
                first,
                tile_of(max(counts) * rows, tokens),
            ),
            out_shape=shapes + shapes_of(sum((groups[i] for i in part), [])),
            in_specs=[ANY] * len(back) + [VMEM] * len(operands),
            out_specs=[VMEM] * (len(shapes) + sum(counts)),
            scratch_shapes=[
                shape
                for count in counts
                for shape in (
                    natural(heads, count),
                    across(heads, count),
                    sums(heads, count),
                    sums(heads, count),
                )
            ],
            compiler_params=compiler_params,
            cost_estimate=cost(heads, sum(counts) * rows, tokens, 4),
            name="backward",
        )(*back, *operands)
        if first:
            context_rows, grads_q = outs[0], outs[1 : 1 + heads]
        else:
            grad_query = outs[0]
        blocks = list(outs[len(shapes) :])
        for i in part:
            send_back(i, 0, blocks[: len(groups[i])])
            blocks = blocks[len(groups[i]) :]
    return context_rows, grad_query


def shards(pairs, queries, upstream):
    _, rows, _, width = pairs.shape
    heads = queries.shape[2] // HEAD
    order = offsets()
    quarter = max(1, len(order) // 4)
    cuts = [0, quarter, 2 * quarter, len(order) - quarter, len(order)]
    whole = [[(o, 0, heads) for o in order[a:b]] for a, b in zip(cuts[:-2], cuts[1:-1])]
    single = [[(o, h, 1) for o in order[cuts[-2] :]] for h in range(heads)]
    pieces = sum(whole + single, [])
    blocks = []
    for piece, block in zip(pieces, pack(pairs, pieces)):
        block = block.reshape(-1, 2 * rows, HEAD)
        blocks.append(lax.ppermute(block, AXES, route(piece[0], False)))
    arrived = []
    for group in whole + single:
        arrived.append(blocks[: len(group)])
        blocks = blocks[len(group) :]
    homes, returned = [], []

    def send_back(index, head, grads):
        sent = (whole + single)[index + head]
        back = [lax.ppermute(g, AXES, route(p[0], True)) for p, g in zip(sent, grads)]
        homes.extend(sent)
        returned.extend(b.reshape(-1, rows, 2, HEAD) for b in back)
        return back

    context, grad_query = attend(
        arrived[: len(whole)], arrived[len(whole) :], queries, upstream, send_back
    )
    return context, grad_query, unpack(returned, homes, width)


def solution(mesh):
    return jax.shard_map(
        shards,
        mesh=mesh,
        in_specs=(
            P("segment", ("seq", "tp"), None, None),
            P("segment", None, ("seq", "tp")),
            P("segment", None, ("seq", "tp")),
        ),
        out_specs=(
            P("segment", None, ("seq", "tp")),
            P("segment", None, ("seq", "tp")),
            P("segment", ("seq", "tp"), None, None),
        ),
        check_vma=False,
    )
```

```python
import functools

import jax
import jax.numpy as jnp
from jax import lax
from jax.experimental import pallas as pl
from jax.experimental.pallas import tpu as pltpu
from jax.sharding import PartitionSpec as P

HEAD = 128
FACTOR = HEAD**-0.5
EXPONENT = FACTOR * 1.4426950408889634
MIB = 1 << 20
NT = ((1,), (1,))
HBM = pl.BlockSpec(memory_space=pltpu.HBM)
VMEM = pl.BlockSpec(memory_space=pltpu.VMEM)


def passed_along(block, distance):
    count = lax.axis_size("segment")
    return lax.ppermute(block, "segment", [((i - distance) % count, i) for i in range(count)])


def swapped(blocks):
    return lax.all_to_all(blocks, ("seq", "tp"), split_axis=0, concat_axis=0, tiled=True)


def pack(pairs, groups, heads):
    _, rows, _, width = pairs.shape

    def kernel(pairs_ref, *outs):
        @pl.loop(0, rows // 16)
        def _(r):
            here = pl.ds(pl.multiple_of(r * 16, 16), 16)
            for g in range(groups):
                for h, out in enumerate(outs):
                    column = (g * heads + h) * HEAD
                    out[g, here] = pairs_ref[0, here, :, column : column + HEAD]

    return pl.pallas_call(
        kernel,
        out_shape=[jax.ShapeDtypeStruct((groups, rows, 2, HEAD), pairs.dtype)] * heads,
        in_specs=[VMEM],
        out_specs=[VMEM] * heads,
        compiler_params=pltpu.CompilerParams(vmem_limit_bytes=24 * MIB),
        name="pack",
    )(pairs)


def unpack(blocks, width):
    heads = len(blocks)
    groups, rows, _, _ = blocks[0].shape
    parts = 4 if rows % 64 == 0 else 1
    size = rows // parts

    def kernel(*refs):
        ins, out, held, sem = refs[:heads], refs[heads], refs[-2], refs[-1]

        def store(r):
            here = pl.ds(pl.multiple_of(r * size, size), size)
            return pltpu.make_async_copy(held.at[here], out.at[0, here], sem.at[r])

        @pl.loop(0, parts)
        def _(r):
            here = pl.ds(pl.multiple_of(r * size, size), size)
            for g in range(groups):
                for h, block in enumerate(ins):
                    column = (g * heads + h) * HEAD
                    held[here, :, column : column + HEAD] = block[g, here]
            store(r).start()

        for r in range(parts):
            store(r).wait()

    return pl.pallas_call(
        kernel,
        out_shape=jax.ShapeDtypeStruct((1, rows, 2, width), blocks[0].dtype),
        in_specs=[VMEM] * heads,
        out_specs=HBM,
        scratch_shapes=[
            pltpu.VMEM((rows, 2, width), blocks[0].dtype),
            pltpu.SemaphoreType.DMA((parts,)),
        ],
        compiler_params=pltpu.CompilerParams(vmem_limit_bytes=24 * MIB),
        name="unpack",
    )(*blocks)


def turned(arrays, head):
    _, tokens, _ = arrays[0].shape
    tile = 256 if tokens % 256 == 0 else tokens
    columns = slice(head * HEAD, (head + 1) * HEAD)

    def kernel(*refs):
        out = refs[-1]
        for i, ref in enumerate(refs[:-1]):
            for j in range(tokens // tile):
                here = slice(j * tile, (j + 1) * tile)
                block = ref[0, here, columns].astype(jnp.float32)
                out[i, :, here] = block.T.astype(out.dtype)

    return pl.pallas_call(
        kernel,
        out_shape=jax.ShapeDtypeStruct((len(arrays), HEAD, tokens), arrays[0].dtype),
        in_specs=[VMEM] * len(arrays),
        out_specs=VMEM,
        compiler_params=pltpu.CompilerParams(vmem_limit_bytes=16 * MIB),
        name="turned",
    )(*arrays)


def turned_back(per_head):
    count, _, tokens = per_head[0].shape
    heads = len(per_head)
    tile = 256 if tokens % 256 == 0 else tokens

    def kernel(*refs):
        ins, outs = refs[:heads], refs[heads:]
        for i, out in enumerate(outs):
            for h, block in enumerate(ins):
                for j in range(tokens // tile):
                    here = slice(j * tile, (j + 1) * tile)
                    rows = block[i, :, here].astype(jnp.float32).T
                    out[0, here, h * HEAD : (h + 1) * HEAD] = rows.astype(out.dtype)

    shape = jax.ShapeDtypeStruct((1, tokens, heads * HEAD), per_head[0].dtype)
    return pl.pallas_call(
        kernel,
        out_shape=[shape] * count,
        in_specs=[VMEM] * heads,
        out_specs=[VMEM] * count,
        compiler_params=pltpu.CompilerParams(vmem_limit_bytes=16 * MIB),
        name="turned_back",
    )(*per_head)


def tiles(count):
    def run(body):
        if count <= 3:
            for j in range(count):
                body(j)
        else:
            pl.loop(0, count)(body)

    return run


def tokens_of(j, tile):
    return pl.ds(j * tile if isinstance(j, int) else pl.multiple_of(j * tile, tile), tile)


def tile_of(rows, tokens):
    for parts in range(1, tokens // 256 + 1):
        if tokens % (256 * parts) == 0 and rows * (tokens // parts) * 4 <= 2 * MIB:
            return tokens // parts
    return 256 if tokens % 256 == 0 else tokens


def dot(a, b, contract=((1,), (0,))):
    return lax.dot_general(a, b, (contract, ((), ())), preferred_element_type=jnp.float32)


def shuffle(rows, join):
    to = lax.broadcasted_iota(jnp.int32, (2 * rows, 2 * rows), 1 if join else 0)
    source = lax.broadcasted_iota(jnp.int32, (2 * rows, 2 * rows), 0 if join else 1)
    wanted = jnp.where(to < rows, 2 * to, 2 * (to - rows) + 1)
    return jnp.where(source == wanted, 1.0, 0.0).astype(jnp.bfloat16)


def attend_kernel(tile, pairs_ref, tokens_ref, result_ref, grads_ref, *scratch):
    k_ref, v_ref, kt_ref, vt_ref, gk_ref, gv_ref = scratch
    groups, pair_rows, _ = pairs_ref.shape
    rows = pair_rows // 2
    split = shuffle(rows, False)
    for g in range(groups):
        both = dot(split, pairs_ref[g])
        here = slice(g * rows, (g + 1) * rows)
        keys, values = both[:rows], both[rows:]
        k_ref[here, :] = keys.astype(jnp.bfloat16)
        v_ref[here, :] = values.astype(jnp.bfloat16)
        kt_ref[:, here] = keys.T.astype(jnp.bfloat16)
        vt_ref[:HEAD, here] = values.T.astype(jnp.bfloat16)
    vt_ref[HEAD:, :] = jnp.ones((vt_ref.shape[0] - HEAD, vt_ref.shape[1]), jnp.bfloat16)
    gk_ref[...] = jnp.zeros_like(gk_ref)
    gv_ref[...] = jnp.zeros_like(gv_ref)

    @tiles(tokens_ref.shape[2] // tile)
    def _(j):
        here = tokens_of(j, tile)
        qt, gt = tokens_ref[0, :, here], tokens_ref[1, :, here]
        scores = dot(k_ref[...], qt)
        grad_weights = dot(v_ref[...], gt)
        top = jnp.max(scores, axis=0, keepdims=True)
        raised = jnp.exp2((scores - top) * EXPONENT)
        low = raised.astype(jnp.bfloat16)
        summed = dot(vt_ref[...], low)
        scale = 1.0 / summed[HEAD : HEAD + 1]
        context = summed[:HEAD] * scale
        row_dot = jnp.sum(gt.astype(jnp.float32) * context, axis=0, keepdims=True)
        result_ref[0, :, here] = context.astype(jnp.bfloat16)
        grad_scores = (raised * (grad_weights - row_dot)).astype(jnp.bfloat16)
        grad_q = dot(kt_ref[...], grad_scores) * (scale * FACTOR)
        result_ref[1, :, here] = grad_q.astype(jnp.bfloat16)
        scaled = (qt.astype(jnp.float32) * (scale * FACTOR)).astype(jnp.bfloat16)
        gk_ref[...] += dot(grad_scores, scaled, NT)
        gv_ref[...] += dot(low, (gt.astype(jnp.float32) * scale).astype(jnp.bfloat16), NT)

    join = shuffle(rows, True)
    for g in range(groups):
        here = slice(g * rows, (g + 1) * rows)
        both = jnp.concatenate([gk_ref[here, :], gv_ref[here, :]], axis=0)
        grads_ref[g] = dot(join, both.astype(jnp.bfloat16)).astype(jnp.bfloat16)


def attend(pairs, both):
    groups, pair_rows, _ = pairs.shape
    enc_len = groups * pair_rows // 2
    tokens = both.shape[2]
    return pl.pallas_call(
        functools.partial(attend_kernel, tile_of(enc_len, tokens)),
        out_shape=[
            jax.ShapeDtypeStruct(both.shape, both.dtype),
            jax.ShapeDtypeStruct(pairs.shape, pairs.dtype),
        ],
        in_specs=[VMEM] * 2,
        out_specs=[VMEM] * 2,
        scratch_shapes=[
            pltpu.VMEM((enc_len, HEAD), jnp.bfloat16),
            pltpu.VMEM((enc_len, HEAD), jnp.bfloat16),
            pltpu.VMEM((HEAD, enc_len), jnp.bfloat16),
            pltpu.VMEM((HEAD + 16, enc_len), jnp.bfloat16),
            pltpu.VMEM((enc_len, HEAD), jnp.float32),
            pltpu.VMEM((enc_len, HEAD), jnp.float32),
        ],
        compiler_params=pltpu.CompilerParams(vmem_limit_bytes=(16 + enc_len * 32 // 4096) * MIB),
        cost_estimate=pl.CostEstimate(
            flops=12 * enc_len * tokens * HEAD,
            bytes_accessed=HEAD * (8 * enc_len + 8 * tokens),
            transcendentals=enc_len * tokens,
        ),
        name="attend",
    )(pairs, both)


def shards(pairs, queries, upstream):
    _, rows, _, width = pairs.shape
    groups = lax.axis_size("seq") * lax.axis_size("tp")
    heads = queries.shape[2] // HEAD
    arrived = []
    for h, block in enumerate(pack(pairs, groups, heads)):
        both = passed_along(turned([queries, upstream], h), -1)
        arrived.append((swapped(block.reshape(groups, 2 * rows, HEAD)), both))
    results, grads = [], []
    for block, both in arrived:
        result, grad = attend(block, both)
        grads.append(swapped(grad).reshape(groups, rows, 2, HEAD))
        results.append(passed_along(result, 1))
    context, grad_query = turned_back(results)
    return context, grad_query, unpack(grads, width)


def solution(mesh):
    return jax.shard_map(
        shards,
        mesh=mesh,
        in_specs=(
            P("segment", ("seq", "tp"), None, None),
            P("segment", None, ("seq", "tp")),
            P("segment", None, ("seq", "tp")),
        ),
        out_specs=(
            P("segment", None, ("seq", "tp")),
            P("segment", None, ("seq", "tp")),
            P("segment", ("seq", "tp"), None, None),
        ),
        check_vma=False,
    )
```

```python
import functools

import jax
import jax.numpy as jnp
from jax import lax
from jax.experimental import pallas as pl
from jax.experimental.pallas import tpu as pltpu
from jax.sharding import PartitionSpec as P

HEAD = 128
AXES = ("segment", "seq", "tp")
FACTOR = HEAD**-0.5
EXPONENT = FACTOR * 1.4426950408889634
MIB = 1 << 20
NT = ((1,), (1,))
ANY = pl.BlockSpec(memory_space=pl.ANY)
HBM = pl.BlockSpec(memory_space=pltpu.HBM)
VMEM = pl.BlockSpec(memory_space=pltpu.VMEM)


def partner(index, distance, count):
    if count & (count - 1):
        return (index + distance) % count
    return index ^ distance


def offset_groups():
    seq_count = lax.axis_size("seq")
    tp_count = lax.axis_size("tp")
    middle = seq_count // 2
    far = [(dz, dy) for dy in reversed(range(tp_count)) for dz in range(middle, seq_count)]
    near = [(dz, dy) for dy in reversed(range(tp_count)) for dz in reversed(range(middle))]
    f, n = max(1, len(far) // 4), len(near) // 2
    return [far[:f] + near[:n], far[f : 2 * f] + near[n:] + far[2 * f : -f], far[-f:]]


def group_at(offset):
    seq_count = lax.axis_size("seq")
    tp_count = lax.axis_size("tp")
    z = partner(lax.axis_index("seq"), offset[0], seq_count)
    y = partner(lax.axis_index("tp"), offset[1], tp_count)
    return z * tp_count + y


def route(offset, back):
    segments, seq_count, tp_count = (lax.axis_size(a) for a in AXES)
    hops = []
    for s in range(segments):
        for z in range(seq_count):
            for y in range(tp_count):
                source = (s * seq_count + z) * tp_count + y
                s_to = (s + 1) % segments
                z_to = partner(z, offset[0], seq_count)
                y_to = partner(y, offset[1], tp_count)
                target = (s_to * seq_count + z_to) * tp_count + y_to
                hops.append((target, source) if back else (source, target))
    return hops


def params(enc_len):
    return pltpu.CompilerParams(vmem_limit_bytes=(12 + enc_len * 36 // 4096) * MIB)


def pack(pairs, order, heads):
    _, rows, _, width = pairs.shape
    local = heads * HEAD

    def kernel(pairs_ref, *outs):
        @pl.loop(0, rows // 16)
        def _(r):
            here = pl.ds(pl.multiple_of(r * 16, 16), 16)
            for out, offset in zip(outs, order):
                base = group_at(offset) * local
                for h in range(heads):
                    column = pl.multiple_of(base + h * HEAD, HEAD)
                    out[h, here] = pairs_ref[0, here, :, pl.ds(column, HEAD)]

    return pl.pallas_call(
        kernel,
        out_shape=[jax.ShapeDtypeStruct((heads, rows, 2, HEAD), pairs.dtype)] * len(order),
        in_specs=[VMEM],
        out_specs=[VMEM] * len(order),
        compiler_params=pltpu.CompilerParams(vmem_limit_bytes=24 * MIB),
        name="pack",
    )(pairs)


def unpack(blocks, order, width):
    heads, rows, _, _ = blocks[0].shape
    local = heads * HEAD
    parts = 4 if rows % 64 == 0 else 1
    size = rows // parts

    def kernel(*refs):
        ins, out, held, sem = refs[: len(order)], refs[len(order)], refs[-2], refs[-1]

        def store(r):
            here = pl.ds(pl.multiple_of(r * size, size), size)
            return pltpu.make_async_copy(held.at[here], out.at[0, here], sem.at[r])

        @pl.loop(0, parts)
        def _(r):
            here = pl.ds(pl.multiple_of(r * size, size), size)
            for block, offset in zip(ins, order):
                base = group_at(offset) * local
                for h in range(heads):
                    column = pl.multiple_of(base + h * HEAD, HEAD)
                    held[here, :, pl.ds(column, HEAD)] = block[h, here]
            store(r).start()

        for r in range(parts):
            store(r).wait()

    return pl.pallas_call(
        kernel,
        out_shape=jax.ShapeDtypeStruct((1, rows, 2, width), blocks[0].dtype),
        in_specs=[VMEM] * len(order),
        out_specs=HBM,
        scratch_shapes=[
            pltpu.VMEM((rows, 2, width), blocks[0].dtype),
            pltpu.SemaphoreType.DMA((parts,)),
        ],
        compiler_params=pltpu.CompilerParams(vmem_limit_bytes=24 * MIB),
        name="unpack",
    )(*blocks)


def turned(rows):
    _, tokens, local = rows.shape
    heads = local // HEAD
    tile = 256 if tokens % 256 == 0 else tokens

    def kernel(rows_ref, out_ref):
        for h in range(heads):
            for j in range(tokens // tile):
                here = slice(j * tile, (j + 1) * tile)
                block = rows_ref[0, here, h * HEAD : (h + 1) * HEAD]
                out_ref[h, :, here] = block.astype(jnp.float32).T.astype(rows.dtype)

    return pl.pallas_call(
        kernel,
        out_shape=jax.ShapeDtypeStruct((heads, HEAD, tokens), rows.dtype),
        in_specs=[VMEM],
        out_specs=VMEM,
        compiler_params=pltpu.CompilerParams(vmem_limit_bytes=16 * MIB),
        name="turned",
    )(rows)


def tiles(count):
    def run(body):
        if count <= 2:
            for j in range(count):
                body(j)
        else:
            pl.loop(0, count)(body)

    return run


def tokens_of(j, tile):
    return pl.ds(j * tile if isinstance(j, int) else pl.multiple_of(j * tile, tile), tile)


def tile_of(rows, tokens):
    for parts in range(1, tokens // 256 + 1):
        if tokens % (256 * parts) == 0 and rows * (tokens // parts) * 4 <= 5 * MIB // 4:
            return tokens // parts
    return 256 if tokens % 256 == 0 else tokens


def dot(a, b, contract=((1,), (0,))):
    return lax.dot_general(a, b, (contract, ((), ())), preferred_element_type=jnp.float32)


def shuffle(rows, join):
    to = lax.broadcasted_iota(jnp.int32, (2 * rows, 2 * rows), 1 if join else 0)
    source = lax.broadcasted_iota(jnp.int32, (2 * rows, 2 * rows), 0 if join else 1)
    wanted = jnp.where(to < rows, 2 * to, 2 * (to - rows) + 1)
    return jnp.where(source == wanted, 1.0, 0.0).astype(jnp.bfloat16)


def split_chunks(chunks, h, rows, k_ref=None, v_ref=None, kt_ref=None, vt_ref=None):
    split = shuffle(rows, False)
    for i, chunk in enumerate(chunks):
        both = dot(split, chunk[h])
        here = slice(i * rows, (i + 1) * rows)
        keys, values = both[:rows], both[rows:]
        if k_ref is not None:
            k_ref[h, here, :] = keys.astype(jnp.bfloat16)
        if v_ref is not None:
            v_ref[h, here, :] = values.astype(jnp.bfloat16)
        if kt_ref is not None:
            kt_ref[h, :, here] = keys.T.astype(jnp.bfloat16)
        if vt_ref is not None:
            vt_ref[h, :HEAD, here] = values.T.astype(jnp.bfloat16)
    if vt_ref is not None:
        tail = (vt_ref.shape[1] - HEAD, vt_ref.shape[2])
        vt_ref[h, HEAD:, :] = jnp.ones(tail, jnp.bfloat16)


def join_chunks(outs, h, rows, gk_ref, gv_ref):
    join = shuffle(rows, True)
    for i, out in enumerate(outs):
        here = slice(i * rows, (i + 1) * rows)
        both = jnp.concatenate([gk_ref[h, here, :], gv_ref[h, here, :]], axis=0)
        out[h] = dot(join, both.astype(jnp.bfloat16)).astype(jnp.bfloat16)


def raise_scores(keys, qt, values_t, before):
    scores = dot(keys, qt)
    top = jnp.max(scores, axis=0, keepdims=True)
    if before is not None:
        top = jnp.maximum(top, before[0])
    raised = jnp.exp2((scores - top) * EXPONENT)
    low = raised.astype(jnp.bfloat16)
    summed = dot(values_t, low)
    total, context = summed[HEAD : HEAD + 1], summed[:HEAD]
    if before is not None:
        shrink = jnp.exp2((before[0] - top) * EXPONENT)
        total = total + before[1] * shrink
        context = context + before[2] * shrink
    return raised, low, top, total, context


def forward_kernel(count, first, tile, *refs):
    chunks, refs = refs[:count], refs[count:]
    qt_ref, refs = refs[0], refs[1:]
    if not first:
        stats_in, context_in, refs = refs[0], refs[1], refs[2:]
    stats_ref, context_ref, low_ref, k_ref, vt_ref = refs
    heads, pair_rows, _ = chunks[0].shape
    for h in range(heads):
        split_chunks(chunks, h, pair_rows // 2, k_ref=k_ref, vt_ref=vt_ref)

    @tiles(qt_ref.shape[2] // tile)
    def _(j):
        here = tokens_of(j, tile)
        for h in range(heads):
            before = None
            if not first:
                before = (stats_in[h, 0:1, here], stats_in[h, 1:2, here], context_in[h, :, here])
            _, low, top, total, context = raise_scores(
                k_ref[h], qt_ref[h, :, here], vt_ref[h], before
            )
            low_ref[h, :, here] = low
            stats_ref[h, 0:1, here] = top
            stats_ref[h, 1:2, here] = total
            context_ref[h, :, here] = context


def gradients(raised, low, scale, row_dot, qt, gt, refs, h):
    v_ref, kt_ref, gk_ref, gv_ref = refs
    grad_weights = dot(v_ref[h], gt)
    grad_scores = (raised * (grad_weights - row_dot)).astype(jnp.bfloat16)
    grad_q = dot(kt_ref[h], grad_scores) * (scale * FACTOR)
    scaled = (qt.astype(jnp.float32) * (scale * FACTOR)).astype(jnp.bfloat16)
    gk_ref[h] += dot(grad_scores, scaled, NT)
    gv_ref[h] += dot(low, (gt.astype(jnp.float32) * scale).astype(jnp.bfloat16), NT)
    return grad_q


def turn_kernel(count, tile, *refs):
    chunks, refs = refs[:count], refs[count:]
    qt_ref, gt_ref, stats_in, context_in = refs[:4]
    stats_ref, context_ref, grad_q_ref = refs[4:7]
    outs, refs = refs[7 : 7 + count], refs[7 + count :]
    k_ref, vt_ref, v_ref, kt_ref, gk_ref, gv_ref = refs
    heads, pair_rows, _ = chunks[0].shape
    rows = pair_rows // 2
    for h in range(heads):
        split_chunks(chunks, h, rows, k_ref, v_ref, kt_ref, vt_ref)
    gk_ref[...] = jnp.zeros_like(gk_ref)
    gv_ref[...] = jnp.zeros_like(gv_ref)

    @tiles(qt_ref.shape[2] // tile)
    def _(j):
        here = tokens_of(j, tile)
        for h in range(heads):
            qt, gt = qt_ref[h, :, here], gt_ref[h, :, here]
            before = (stats_in[h, 0:1, here], stats_in[h, 1:2, here], context_in[h, :, here])
            raised, low, top, total, context = raise_scores(k_ref[h], qt, vt_ref[h], before)
            scale = 1.0 / total
            context = context * scale
            row_dot = jnp.sum(gt.astype(jnp.float32) * context, axis=0, keepdims=True)
            context_ref[h, :, here] = context
            stats_ref[h, 0:1, here] = top
            stats_ref[h, 1:2, here] = scale
            stats_ref[h, 2:3, here] = row_dot
            grad_q_ref[h, :, here] = gradients(
                raised, low, scale, row_dot, qt, gt, (v_ref, kt_ref, gk_ref, gv_ref), h
            )

    for h in range(heads):
        join_chunks(outs, h, rows, gk_ref, gv_ref)


def backward_kernel(back, count, first, last, tile, *refs):
    refs = refs[back:]
    chunks, refs = refs[:count], refs[count:]
    low_ref, then_ref, qt_ref, gt_ref, stats_ref, grad_q_in = refs[:6]
    refs = refs[6:]
    if first:
        ready_ref, refs = refs[0], refs[1:]
    if first or last:
        rows_ref, refs = refs[0], refs[1:]
    if not last:
        grad_q_ref, refs = refs[0], refs[1:]
    outs, refs = refs[:count], refs[count:]
    v_ref, kt_ref, gk_ref, gv_ref = refs
    heads, pair_rows, _ = chunks[0].shape
    rows = pair_rows // 2
    for h in range(heads):
        split_chunks(chunks, h, rows, v_ref=v_ref, kt_ref=kt_ref)
    gk_ref[...] = jnp.zeros_like(gk_ref)
    gv_ref[...] = jnp.zeros_like(gv_ref)

    @tiles(qt_ref.shape[2] // tile)
    def _(j):
        here = tokens_of(j, tile)
        for h in range(heads):
            columns = slice(h * HEAD, (h + 1) * HEAD)
            qt, gt = qt_ref[h, :, here], gt_ref[h, :, here]
            top, scale, row_dot = (stats_ref[h, i : i + 1, here] for i in range(3))
            shrunk = jnp.exp2((then_ref[h, 0:1, here] - top) * EXPONENT)
            low = low_ref[h, :, here]
            raised = low.astype(jnp.float32)
            grad_q = grad_q_in[h, :, here] + gradients(
                raised, low, scale * shrunk, row_dot, qt, gt, refs, h
            )
            if last:
                rows_ref[0, here, columns] = grad_q.T.astype(rows_ref.dtype)
            else:
                grad_q_ref[h, :, here] = grad_q
            if first:
                rows_ref[0, here, columns] = ready_ref[h, :, here].T.astype(rows_ref.dtype)

    for h in range(heads):
        join_chunks(outs, h, rows, gk_ref, gv_ref)


def cost(heads, rows, tokens, matmuls):
    return pl.CostEstimate(
        flops=2 * matmuls * heads * rows * tokens * HEAD,
        bytes_accessed=heads * (rows + tokens) * HEAD * 8,
        transcendentals=heads * rows * tokens,
    )


def attend(groups, queries, upstream, send_back):
    heads, pair_rows, _ = groups[0][0].shape
    rows = pair_rows // 2
    enc_len = sum(len(g) for g in groups) * rows
    tokens = queries.shape[1]
    qt, gt = turned(queries), turned(upstream)
    stats_shape = jax.ShapeDtypeStruct((heads, 8, tokens), jnp.float32)
    wide_shape = jax.ShapeDtypeStruct((heads, HEAD, tokens), jnp.float32)
    rows_shape = jax.ShapeDtypeStruct(queries.shape, queries.dtype)
    compiler_params = params(enc_len)

    def natural(count):
        return pltpu.VMEM((heads, count * rows, HEAD), jnp.bfloat16)

    def across(count, extra=0):
        return pltpu.VMEM((heads, HEAD + extra, count * rows), jnp.bfloat16)

    def sums(count):
        return pltpu.VMEM((heads, count * rows, HEAD), jnp.float32)

    def shapes_of(group):
        return [jax.ShapeDtypeStruct(c.shape, c.dtype) for c in group]

    waits = {1: [], 0: [0]}
    state, kept = [], []
    for group in groups[:-1]:
        count = len(group)
        low_shape = jax.ShapeDtypeStruct((heads, count * rows, tokens), jnp.bfloat16)
        stats, context, low = pl.pallas_call(
            functools.partial(forward_kernel, count, not state, tile_of(count * rows, tokens)),
            out_shape=[stats_shape, wide_shape, low_shape],
            in_specs=[VMEM] * (count + 1 + len(state)),
            out_specs=[VMEM] * 3,
            scratch_shapes=[natural(count), across(count, 16)],
            compiler_params=compiler_params,
            cost_estimate=cost(heads, count * rows, tokens, 2),
            name="forward",
        )(*group, qt, *state)
        state = [stats, context]
        kept.append((low, stats))

    group, count = groups[-1], len(groups[-1])
    final, context, grad_q, *grads = pl.pallas_call(
        functools.partial(turn_kernel, count, tile_of(count * rows, tokens)),
        out_shape=[stats_shape, wide_shape, wide_shape] + shapes_of(group),
        in_specs=[VMEM] * (count + 4),
        out_specs=[VMEM] * (count + 3),
        scratch_shapes=[natural(count), across(count, 16), natural(count), across(count)]
        + [sums(count)] * 2,
        compiler_params=compiler_params,
        cost_estimate=cost(heads, count * rows, tokens, 6),
        name="turn",
    )(*group, qt, gt, *state)
    returned = [send_back(len(groups) - 1, grads)]

    for i in reversed(range(len(groups) - 1)):
        group, count = groups[i], len(groups[i])
        first, last = i == len(groups) - 2, i == 0
        back = sum((returned[k] for k in waits[i]), [])
        operands = [*group, *kept[i], qt, gt, final, grad_q, *([context] if first else [])]
        shapes = [rows_shape] * (first or last) + [wide_shape] * (not last)
        outs = pl.pallas_call(
            functools.partial(
                backward_kernel, len(back), count, first, last, tile_of(count * rows, tokens)
            ),
            out_shape=shapes + shapes_of(group),
            in_specs=[ANY] * len(back) + [VMEM] * len(operands),
            out_specs=[VMEM] * (len(shapes) + count),
            scratch_shapes=[natural(count), across(count), sums(count), sums(count)],
            compiler_params=compiler_params,
            cost_estimate=cost(heads, count * rows, tokens, 4),
            name="backward",
        )(*back, *operands)
        if first:
            context_rows = outs[0]
        if last:
            grad_query = outs[0]
        else:
            grad_q = outs[len(shapes) - 1]
        returned.append(send_back(i, outs[len(shapes) :]))
    return context_rows, grad_query


def shards(pairs, queries, upstream):
    _, rows, _, width = pairs.shape
    heads = queries.shape[2] // HEAD
    offsets = offset_groups()
    order = sum(offsets, [])
    blocks = []
    for offset, block in zip(order, pack(pairs, order, heads)):
        block = block.reshape(heads, 2 * rows, HEAD)
        blocks.append(lax.ppermute(block, AXES, route(offset, False)))
    groups = []
    for group in offsets:
        groups.append(blocks[: len(group)])
        blocks = blocks[len(group) :]
    homes, returned = [], []

    def send_back(i, grads):
        back = [lax.ppermute(g, AXES, route(o, True)) for o, g in zip(offsets[i], grads)]
        homes.extend(offsets[i])
        returned.extend(b.reshape(heads, rows, 2, HEAD) for b in back)
        return back

    context, grad_query = attend(groups, queries, upstream, send_back)
    return context, grad_query, unpack(returned, homes, width)


def solution(mesh):
    return jax.shard_map(
        shards,
        mesh=mesh,
        in_specs=(
            P("segment", ("seq", "tp"), None, None),
            P("segment", None, ("seq", "tp")),
            P("segment", None, ("seq", "tp")),
        ),
        out_specs=(
            P("segment", None, ("seq", "tp")),
            P("segment", None, ("seq", "tp")),
            P("segment", ("seq", "tp"), None, None),
        ),
        check_vma=False,
    )
```

```python
import functools

import jax
import jax.numpy as jnp
from jax import lax
from jax.experimental import pallas as pl
from jax.experimental.pallas import tpu as pltpu
from jax.sharding import PartitionSpec as P

HEAD = 128
AXES = ("segment", "seq", "tp")
FACTOR = HEAD**-0.5
EXPONENT = FACTOR * 1.4426950408889634
MIB = 1 << 20
NT = ((1,), (1,))
ANY = pl.BlockSpec(memory_space=pl.ANY)
HBM = pl.BlockSpec(memory_space=pltpu.HBM)
VMEM = pl.BlockSpec(memory_space=pltpu.VMEM)


def partner(index, distance, count):
    turned_round = (index & 1) * (count // 2) if count % 4 == 0 and distance % (count // 2) == 0 else 0
    total = index + distance + turned_round
    return total % count if isinstance(total, int) else lax.rem(total, count)


def offset_groups():
    seq_count = lax.axis_size("seq")
    tp_count = lax.axis_size("tp")
    order = [(dz, dy) for dz in range(seq_count) for dy in reversed(range(tp_count))]
    count = len(order)
    cuts = [0, count * 3 // 8, count * 3 // 4, count]
    return [order[a:b] for a, b in zip(cuts[:-1], cuts[1:])]


def group_at(offset):
    seq_count = lax.axis_size("seq")
    tp_count = lax.axis_size("tp")
    z = partner(lax.axis_index("seq"), offset[0], seq_count)
    y = lax.rem(lax.axis_index("tp") + offset[1], tp_count)
    return z * tp_count + y


def route(offset, back):
    segments, seq_count, tp_count = (lax.axis_size(a) for a in AXES)
    hops = []
    for s in range(segments):
        for z in range(seq_count):
            for y in range(tp_count):
                source = (s * seq_count + z) * tp_count + y
                s_to = (s + 1) % segments
                z_to = partner(z, offset[0], seq_count)
                y_to = (y + offset[1]) % tp_count
                target = (s_to * seq_count + z_to) * tp_count + y_to
                hops.append((target, source) if back else (source, target))
    return hops


def params(enc_len):
    return pltpu.CompilerParams(vmem_limit_bytes=(12 + enc_len * 36 // 4096) * MIB)


def pack(pairs, order, heads):
    _, rows, _, width = pairs.shape
    local = heads * HEAD

    def kernel(pairs_ref, *outs):
        @pl.loop(0, rows // 16)
        def _(r):
            here = pl.ds(pl.multiple_of(r * 16, 16), 16)
            for out, offset in zip(outs, order):
                base = group_at(offset) * local
                for h in range(heads):
                    column = pl.multiple_of(base + h * HEAD, HEAD)
                    out[h, here] = pairs_ref[0, here, :, pl.ds(column, HEAD)]

    return pl.pallas_call(
        kernel,
        out_shape=[jax.ShapeDtypeStruct((heads, rows, 2, HEAD), pairs.dtype)] * len(order),
        in_specs=[VMEM],
        out_specs=[VMEM] * len(order),
        compiler_params=pltpu.CompilerParams(vmem_limit_bytes=24 * MIB),
        name="pack",
    )(pairs)


def unpack(blocks, order, width):
    heads, rows, _, _ = blocks[0].shape
    local = heads * HEAD
    parts = 4 if rows % 64 == 0 else 1
    size = rows // parts

    def kernel(*refs):
        ins, out, held, sem = refs[: len(order)], refs[len(order)], refs[-2], refs[-1]

        def store(r):
            here = pl.ds(pl.multiple_of(r * size, size), size)
            return pltpu.make_async_copy(held.at[here], out.at[0, here], sem.at[r])

        @pl.loop(0, parts)
        def _(r):
            here = pl.ds(pl.multiple_of(r * size, size), size)
            for block, offset in zip(ins, order):
                base = group_at(offset) * local
                for h in range(heads):
                    column = pl.multiple_of(base + h * HEAD, HEAD)
                    held[here, :, pl.ds(column, HEAD)] = block[h, here]
            store(r).start()

        for r in range(parts):
            store(r).wait()

    return pl.pallas_call(
        kernel,
        out_shape=jax.ShapeDtypeStruct((1, rows, 2, width), blocks[0].dtype),
        in_specs=[VMEM] * len(order),
        out_specs=HBM,
        scratch_shapes=[
            pltpu.VMEM((rows, 2, width), blocks[0].dtype),
            pltpu.SemaphoreType.DMA((parts,)),
        ],
        compiler_params=pltpu.CompilerParams(vmem_limit_bytes=24 * MIB),
        name="unpack",
    )(*blocks)


def turned(rows):
    _, tokens, local = rows.shape
    heads = local // HEAD
    tile = 256 if tokens % 256 == 0 else tokens

    def kernel(rows_ref, out_ref):
        for h in range(heads):
            for j in range(tokens // tile):
                here = slice(j * tile, (j + 1) * tile)
                block = rows_ref[0, here, h * HEAD : (h + 1) * HEAD]
                out_ref[h, :, here] = block.astype(jnp.float32).T.astype(rows.dtype)

    return pl.pallas_call(
        kernel,
        out_shape=jax.ShapeDtypeStruct((heads, HEAD, tokens), rows.dtype),
        in_specs=[VMEM],
        out_specs=VMEM,
        compiler_params=pltpu.CompilerParams(vmem_limit_bytes=16 * MIB),
        name="turned",
    )(rows)


def tiles(count):
    def run(body):
        if count <= 2:
            for j in range(count):
                body(j)
        else:
            pl.loop(0, count)(body)

    return run


def tokens_of(j, tile):
    return pl.ds(j * tile if isinstance(j, int) else pl.multiple_of(j * tile, tile), tile)


def tile_of(rows, tokens):
    for parts in range(1, tokens // 256 + 1):
        if tokens % (256 * parts) == 0 and rows * (tokens // parts) * 4 <= 5 * MIB // 4:
            return tokens // parts
    return 256 if tokens % 256 == 0 else tokens


def dot(a, b, contract=((1,), (0,))):
    return lax.dot_general(a, b, (contract, ((), ())), preferred_element_type=jnp.float32)


def shuffle(rows, join):
    to = lax.broadcasted_iota(jnp.int32, (2 * rows, 2 * rows), 1 if join else 0)
    source = lax.broadcasted_iota(jnp.int32, (2 * rows, 2 * rows), 0 if join else 1)
    wanted = jnp.where(to < rows, 2 * to, 2 * (to - rows) + 1)
    return jnp.where(source == wanted, 1.0, 0.0).astype(jnp.bfloat16)


def split_chunks(chunks, h, rows, k_ref=None, v_ref=None, kt_ref=None, vt_ref=None):
    split = shuffle(rows, False)
    for i, chunk in enumerate(chunks):
        both = dot(split, chunk[h])
        here = slice(i * rows, (i + 1) * rows)
        keys, values = both[:rows], both[rows:]
        if k_ref is not None:
            k_ref[h, here, :] = keys.astype(jnp.bfloat16)
        if v_ref is not None:
            v_ref[h, here, :] = values.astype(jnp.bfloat16)
        if kt_ref is not None:
            kt_ref[h, :, here] = keys.T.astype(jnp.bfloat16)
        if vt_ref is not None:
            vt_ref[h, :HEAD, here] = values.T.astype(jnp.bfloat16)
    if vt_ref is not None:
        tail = (vt_ref.shape[1] - HEAD, vt_ref.shape[2])
        vt_ref[h, HEAD:, :] = jnp.ones(tail, jnp.bfloat16)


def join_chunks(outs, h, rows, gk_ref, gv_ref):
    join = shuffle(rows, True)
    for i, out in enumerate(outs):
        here = slice(i * rows, (i + 1) * rows)
        both = jnp.concatenate([gk_ref[h, here, :], gv_ref[h, here, :]], axis=0)
        out[h] = dot(join, both.astype(jnp.bfloat16)).astype(jnp.bfloat16)


def raise_scores(keys, qt, values_t, before):
    scores = dot(keys, qt)
    top = jnp.max(scores, axis=0, keepdims=True)
    if before is not None:
        top = jnp.maximum(top, before[0])
    raised = jnp.exp2((scores - top) * EXPONENT)
    low = raised.astype(jnp.bfloat16)
    summed = dot(values_t, low)
    total, context = summed[HEAD : HEAD + 1], summed[:HEAD]
    if before is not None:
        shrink = jnp.exp2((before[0] - top) * EXPONENT)
        total = total + before[1] * shrink
        context = context + before[2] * shrink
    return raised, low, top, total, context


def forward_kernel(count, first, tile, *refs):
    chunks, refs = refs[:count], refs[count:]
    qt_ref, refs = refs[0], refs[1:]
    if not first:
        stats_in, context_in, refs = refs[0], refs[1], refs[2:]
    stats_ref, context_ref, low_ref, k_ref, vt_ref = refs
    heads, pair_rows, _ = chunks[0].shape
    for h in range(heads):
        split_chunks(chunks, h, pair_rows // 2, k_ref=k_ref, vt_ref=vt_ref)

    @tiles(qt_ref.shape[2] // tile)
    def _(j):
        here = tokens_of(j, tile)
        for h in range(heads):
            before = None
            if not first:
                before = (stats_in[h, 0:1, here], stats_in[h, 1:2, here], context_in[h, :, here])
            _, low, top, total, context = raise_scores(
                k_ref[h], qt_ref[h, :, here], vt_ref[h], before
            )
            low_ref[h, :, here] = low
            stats_ref[h, 0:1, here] = top
            stats_ref[h, 1:2, here] = total
            context_ref[h, :, here] = context


def gradients(raised, low, scale, row_dot, qt, gt, refs, h):
    v_ref, kt_ref, gk_ref, gv_ref = refs
    grad_weights = dot(v_ref[h], gt)
    grad_scores = (raised * (grad_weights - row_dot)).astype(jnp.bfloat16)
    grad_q = dot(kt_ref[h], grad_scores) * (scale * FACTOR)
    scaled = (qt.astype(jnp.float32) * (scale * FACTOR)).astype(jnp.bfloat16)
    gk_ref[h] += dot(grad_scores, scaled, NT)
    gv_ref[h] += dot(low, (gt.astype(jnp.float32) * scale).astype(jnp.bfloat16), NT)
    return grad_q


def turn_kernel(count, tile, *refs):
    chunks, refs = refs[:count], refs[count:]
    qt_ref, gt_ref, stats_in, context_in = refs[:4]
    stats_ref, context_ref, grad_q_ref = refs[4:7]
    outs, refs = refs[7 : 7 + count], refs[7 + count :]
    k_ref, vt_ref, v_ref, kt_ref, gk_ref, gv_ref = refs
    heads, pair_rows, _ = chunks[0].shape
    rows = pair_rows // 2
    for h in range(heads):
        split_chunks(chunks, h, rows, k_ref, v_ref, kt_ref, vt_ref)
    gk_ref[...] = jnp.zeros_like(gk_ref)
    gv_ref[...] = jnp.zeros_like(gv_ref)

    @tiles(qt_ref.shape[2] // tile)
    def _(j):
        here = tokens_of(j, tile)
        for h in range(heads):
            qt, gt = qt_ref[h, :, here], gt_ref[h, :, here]
            before = (stats_in[h, 0:1, here], stats_in[h, 1:2, here], context_in[h, :, here])
            raised, low, top, total, context = raise_scores(k_ref[h], qt, vt_ref[h], before)
            scale = 1.0 / total
            context = context * scale
            row_dot = jnp.sum(gt.astype(jnp.float32) * context, axis=0, keepdims=True)
            context_ref[h, :, here] = context
            stats_ref[h, 0:1, here] = top
            stats_ref[h, 1:2, here] = scale
            stats_ref[h, 2:3, here] = row_dot
            grad_q_ref[h, :, here] = gradients(
                raised, low, scale, row_dot, qt, gt, (v_ref, kt_ref, gk_ref, gv_ref), h
            )

    for h in range(heads):
        join_chunks(outs, h, rows, gk_ref, gv_ref)


def backward_kernel(back, count, first, last, tile, *refs):
    refs = refs[back:]
    chunks, refs = refs[:count], refs[count:]
    low_ref, then_ref, qt_ref, gt_ref, stats_ref, grad_q_in = refs[:6]
    refs = refs[6:]
    if first:
        ready_ref, refs = refs[0], refs[1:]
    if first or last:
        rows_ref, refs = refs[0], refs[1:]
    if not last:
        grad_q_ref, refs = refs[0], refs[1:]
    outs, refs = refs[:count], refs[count:]
    v_ref, kt_ref, gk_ref, gv_ref = refs
    heads, pair_rows, _ = chunks[0].shape
    rows = pair_rows // 2
    for h in range(heads):
        split_chunks(chunks, h, rows, v_ref=v_ref, kt_ref=kt_ref)
    gk_ref[...] = jnp.zeros_like(gk_ref)
    gv_ref[...] = jnp.zeros_like(gv_ref)

    @tiles(qt_ref.shape[2] // tile)
    def _(j):
        here = tokens_of(j, tile)
        for h in range(heads):
            columns = slice(h * HEAD, (h + 1) * HEAD)
            qt, gt = qt_ref[h, :, here], gt_ref[h, :, here]
            top, scale, row_dot = (stats_ref[h, i : i + 1, here] for i in range(3))
            shrunk = jnp.exp2((then_ref[h, 0:1, here] - top) * EXPONENT)
            low = low_ref[h, :, here]
            raised = low.astype(jnp.float32)
            grad_q = grad_q_in[h, :, here] + gradients(
                raised, low, scale * shrunk, row_dot, qt, gt, refs, h
            )
            if last:
                rows_ref[0, here, columns] = grad_q.T.astype(rows_ref.dtype)
            else:
                grad_q_ref[h, :, here] = grad_q
            if first:
                rows_ref[0, here, columns] = ready_ref[h, :, here].T.astype(rows_ref.dtype)

    for h in range(heads):
        join_chunks(outs, h, rows, gk_ref, gv_ref)


def cost(heads, rows, tokens, matmuls):
    return pl.CostEstimate(
        flops=2 * matmuls * heads * rows * tokens * HEAD,
        bytes_accessed=heads * (rows + tokens) * HEAD * 8,
        transcendentals=heads * rows * tokens,
    )


def attend(groups, queries, upstream, send_back):
    heads, pair_rows, _ = groups[0][0].shape
    rows = pair_rows // 2
    enc_len = sum(len(g) for g in groups) * rows
    tokens = queries.shape[1]
    qt, gt = turned(queries), turned(upstream)
    stats_shape = jax.ShapeDtypeStruct((heads, 8, tokens), jnp.float32)
    wide_shape = jax.ShapeDtypeStruct((heads, HEAD, tokens), jnp.float32)
    rows_shape = jax.ShapeDtypeStruct(queries.shape, queries.dtype)
    compiler_params = params(enc_len)

    def natural(count):
        return pltpu.VMEM((heads, count * rows, HEAD), jnp.bfloat16)

    def across(count, extra=0):
        return pltpu.VMEM((heads, HEAD + extra, count * rows), jnp.bfloat16)

    def sums(count):
        return pltpu.VMEM((heads, count * rows, HEAD), jnp.float32)

    def shapes_of(group):
        return [jax.ShapeDtypeStruct(c.shape, c.dtype) for c in group]

    waits = {1: [], 0: [0]}
    state, kept = [], []
    for group in groups[:-1]:
        count = len(group)
        low_shape = jax.ShapeDtypeStruct((heads, count * rows, tokens), jnp.bfloat16)
        stats, context, low = pl.pallas_call(
            functools.partial(forward_kernel, count, not state, tile_of(count * rows, tokens)),
            out_shape=[stats_shape, wide_shape, low_shape],
            in_specs=[VMEM] * (count + 1 + len(state)),
            out_specs=[VMEM] * 3,
            scratch_shapes=[natural(count), across(count, 16)],
            compiler_params=compiler_params,
            cost_estimate=cost(heads, count * rows, tokens, 2),
            name="forward",
        )(*group, qt, *state)
        state = [stats, context]
        kept.append((low, stats))

    group, count = groups[-1], len(groups[-1])
    final, context, grad_q, *grads = pl.pallas_call(
        functools.partial(turn_kernel, count, tile_of(count * rows, tokens)),
        out_shape=[stats_shape, wide_shape, wide_shape] + shapes_of(group),
        in_specs=[VMEM] * (count + 4),
        out_specs=[VMEM] * (count + 3),
        scratch_shapes=[natural(count), across(count, 16), natural(count), across(count)]
        + [sums(count)] * 2,
        compiler_params=compiler_params,
        cost_estimate=cost(heads, count * rows, tokens, 6),
        name="turn",
    )(*group, qt, gt, *state)
    returned = [send_back(len(groups) - 1, grads)]

    for i in reversed(range(len(groups) - 1)):
        group, count = groups[i], len(groups[i])
        first, last = i == len(groups) - 2, i == 0
        back = sum((returned[k] for k in waits[i]), [])
        operands = [*group, *kept[i], qt, gt, final, grad_q, *([context] if first else [])]
        shapes = [rows_shape] * (first or last) + [wide_shape] * (not last)
        outs = pl.pallas_call(
            functools.partial(
                backward_kernel, len(back), count, first, last, tile_of(count * rows, tokens)
            ),
            out_shape=shapes + shapes_of(group),
            in_specs=[ANY] * len(back) + [VMEM] * len(operands),
            out_specs=[VMEM] * (len(shapes) + count),
            scratch_shapes=[natural(count), across(count), sums(count), sums(count)],
            compiler_params=compiler_params,
            cost_estimate=cost(heads, count * rows, tokens, 4),
            name="backward",
        )(*back, *operands)
        if first:
            context_rows = outs[0]
        if last:
            grad_query = outs[0]
        else:
            grad_q = outs[len(shapes) - 1]
        returned.append(send_back(i, outs[len(shapes) :]))
    return context_rows, grad_query


def shards(pairs, queries, upstream):
    _, rows, _, width = pairs.shape
    heads = queries.shape[2] // HEAD
    offsets = offset_groups()
    order = sum(offsets, [])
    blocks = []
    for offset, block in zip(order, pack(pairs, order, heads)):
        block = block.reshape(heads, 2 * rows, HEAD)
        blocks.append(lax.ppermute(block, AXES, route(offset, False)))
    groups = []
    for group in offsets:
        groups.append(blocks[: len(group)])
        blocks = blocks[len(group) :]
    homes, returned = [], []

    def send_back(i, grads):
        back = [lax.ppermute(g, AXES, route(o, True)) for o, g in zip(offsets[i], grads)]
        homes.extend(offsets[i])
        returned.extend(b.reshape(heads, rows, 2, HEAD) for b in back)
        return back

    context, grad_query = attend(groups, queries, upstream, send_back)
    return context, grad_query, unpack(returned, homes, width)


def solution(mesh):
    return jax.shard_map(
        shards,
        mesh=mesh,
        in_specs=(
            P("segment", ("seq", "tp"), None, None),
            P("segment", None, ("seq", "tp")),
            P("segment", None, ("seq", "tp")),
        ),
        out_specs=(
            P("segment", None, ("seq", "tp")),
            P("segment", None, ("seq", "tp")),
            P("segment", ("seq", "tp"), None, None),
        ),
        check_vma=False,
    )
```

```python
import functools

import jax
import jax.numpy as jnp
from jax import lax
from jax.experimental import pallas as pl
from jax.experimental.pallas import tpu as pltpu
from jax.sharding import PartitionSpec as P

HEAD = 128
AXES = ("segment", "seq", "tp")
FACTOR = HEAD**-0.5
EXPONENT = FACTOR * 1.4426950408889634
MIB = 1 << 20
NT = ((1,), (1,))
ANY = pl.BlockSpec(memory_space=pl.ANY)
HBM = pl.BlockSpec(memory_space=pltpu.HBM)
VMEM = pl.BlockSpec(memory_space=pltpu.VMEM)


def offset_groups():
    seq_count = lax.axis_size("seq")
    tp_count = lax.axis_size("tp")
    near = [(0, dy) for dy in reversed(range(tp_count))]
    far = [(dz, dy) for dy in reversed(range(tp_count)) for dz in range(1, seq_count)]
    far.sort(key=lambda o: -abs(o[0] - seq_count / 2))
    eighth = max(1, (len(near) + len(far)) // 8)
    short, long = far[: -2 * eighth], far[-2 * eighth :]
    short.sort(key=lambda o: -o[1])
    half = len(short) // 2
    return [
        short[:1] + near[:1] + short[1:half],
        short[half:] + near[1:],
        long[:eighth],
        long[eighth:],
    ]


def group_at(offset):
    seq_count = lax.axis_size("seq")
    tp_count = lax.axis_size("tp")
    z = lax.rem(lax.axis_index("seq") + offset[0], seq_count)
    y = lax.rem(lax.axis_index("tp") + offset[1], tp_count)
    return z * tp_count + y


def route(offset, back):
    segments, seq_count, tp_count = (lax.axis_size(a) for a in AXES)
    hops = []
    for s in range(segments):
        for z in range(seq_count):
            for y in range(tp_count):
                source = (s * seq_count + z) * tp_count + y
                s_to = (s + 1) % segments
                z_to = (z + offset[0]) % seq_count
                y_to = (y + offset[1]) % tp_count
                target = (s_to * seq_count + z_to) * tp_count + y_to
                hops.append((target, source) if back else (source, target))
    return hops


def params(enc_len):
    return pltpu.CompilerParams(vmem_limit_bytes=(12 + enc_len * 36 // 4096) * MIB)


def pack(pairs, order, heads):
    _, rows, _, width = pairs.shape
    local = heads * HEAD

    def kernel(pairs_ref, *outs):
        @pl.loop(0, rows // 16)
        def _(r):
            here = pl.ds(pl.multiple_of(r * 16, 16), 16)
            for out, offset in zip(outs, order):
                base = group_at(offset) * local
                for h in range(heads):
                    column = pl.multiple_of(base + h * HEAD, HEAD)
                    out[h, here] = pairs_ref[0, here, :, pl.ds(column, HEAD)]

    return pl.pallas_call(
        kernel,
        out_shape=[jax.ShapeDtypeStruct((heads, rows, 2, HEAD), pairs.dtype)] * len(order),
        in_specs=[VMEM],
        out_specs=[VMEM] * len(order),
        compiler_params=pltpu.CompilerParams(vmem_limit_bytes=24 * MIB),
        name="pack",
    )(pairs)


def unpack(blocks, order, width):
    heads, rows, _, _ = blocks[0].shape
    local = heads * HEAD
    parts = 4 if rows % 64 == 0 else 1
    size = rows // parts

    def kernel(*refs):
        ins, out, held, sem = refs[: len(order)], refs[len(order)], refs[-2], refs[-1]

        def store(r):
            here = pl.ds(pl.multiple_of(r * size, size), size)
            return pltpu.make_async_copy(held.at[here], out.at[0, here], sem.at[r])

        @pl.loop(0, parts)
        def _(r):
            here = pl.ds(pl.multiple_of(r * size, size), size)
            for block, offset in zip(ins, order):
                base = group_at(offset) * local
                for h in range(heads):
                    column = pl.multiple_of(base + h * HEAD, HEAD)
                    held[here, :, pl.ds(column, HEAD)] = block[h, here]
            store(r).start()

        for r in range(parts):
            store(r).wait()

    return pl.pallas_call(
        kernel,
        out_shape=jax.ShapeDtypeStruct((1, rows, 2, width), blocks[0].dtype),
        in_specs=[VMEM] * len(order),
        out_specs=HBM,
        scratch_shapes=[
            pltpu.VMEM((rows, 2, width), blocks[0].dtype),
            pltpu.SemaphoreType.DMA((parts,)),
        ],
        compiler_params=pltpu.CompilerParams(vmem_limit_bytes=24 * MIB),
        name="unpack",
    )(*blocks)


def turned(rows):
    _, tokens, local = rows.shape
    heads = local // HEAD
    tile = 256 if tokens % 256 == 0 else tokens

    def kernel(rows_ref, out_ref):
        for h in range(heads):
            for j in range(tokens // tile):
                here = slice(j * tile, (j + 1) * tile)
                block = rows_ref[0, here, h * HEAD : (h + 1) * HEAD]
                out_ref[h, :, here] = block.astype(jnp.float32).T.astype(rows.dtype)

    return pl.pallas_call(
        kernel,
        out_shape=jax.ShapeDtypeStruct((heads, HEAD, tokens), rows.dtype),
        in_specs=[VMEM],
        out_specs=VMEM,
        compiler_params=pltpu.CompilerParams(vmem_limit_bytes=16 * MIB),
        name="turned",
    )(rows)


def tiles(count):
    def run(body):
        if count <= 2:
            for j in range(count):
                body(j)
        else:
            pl.loop(0, count)(body)

    return run


def tokens_of(j, tile):
    return pl.ds(j * tile if isinstance(j, int) else pl.multiple_of(j * tile, tile), tile)


def tile_of(rows, tokens):
    for parts in range(1, tokens // 256 + 1):
        if tokens % (256 * parts) == 0 and rows * (tokens // parts) * 4 <= 5 * MIB // 4:
            return tokens // parts
    return 256 if tokens % 256 == 0 else tokens


def dot(a, b, contract=((1,), (0,))):
    return lax.dot_general(a, b, (contract, ((), ())), preferred_element_type=jnp.float32)


def shuffle(rows, join):
    to = lax.broadcasted_iota(jnp.int32, (2 * rows, 2 * rows), 1 if join else 0)
    source = lax.broadcasted_iota(jnp.int32, (2 * rows, 2 * rows), 0 if join else 1)
    wanted = jnp.where(to < rows, 2 * to, 2 * (to - rows) + 1)
    return jnp.where(source == wanted, 1.0, 0.0).astype(jnp.bfloat16)


def split_chunks(chunks, h, rows, k_ref=None, v_ref=None, kt_ref=None, vt_ref=None):
    split = shuffle(rows, False)
    for i, chunk in enumerate(chunks):
        both = dot(split, chunk[h])
        here = slice(i * rows, (i + 1) * rows)
        keys, values = both[:rows], both[rows:]
        if k_ref is not None:
            k_ref[h, here, :] = keys.astype(jnp.bfloat16)
        if v_ref is not None:
            v_ref[h, here, :] = values.astype(jnp.bfloat16)
        if kt_ref is not None:
            kt_ref[h, :, here] = keys.T.astype(jnp.bfloat16)
        if vt_ref is not None:
            vt_ref[h, :HEAD, here] = values.T.astype(jnp.bfloat16)
    if vt_ref is not None:
        tail = (vt_ref.shape[1] - HEAD, vt_ref.shape[2])
        vt_ref[h, HEAD:, :] = jnp.ones(tail, jnp.bfloat16)


def join_chunks(outs, h, rows, gk_ref, gv_ref):
    join = shuffle(rows, True)
    for i, out in enumerate(outs):
        here = slice(i * rows, (i + 1) * rows)
        both = jnp.concatenate([gk_ref[h, here, :], gv_ref[h, here, :]], axis=0)
        out[h] = dot(join, both.astype(jnp.bfloat16)).astype(jnp.bfloat16)


def raise_scores(keys, qt, values_t, before):
    scores = dot(keys, qt)
    top = jnp.max(scores, axis=0, keepdims=True)
    if before is not None:
        top = jnp.maximum(top, before[0])
    raised = jnp.exp2((scores - top) * EXPONENT)
    low = raised.astype(jnp.bfloat16)
    summed = dot(values_t, low)
    total, context = summed[HEAD : HEAD + 1], summed[:HEAD]
    if before is not None:
        shrink = jnp.exp2((before[0] - top) * EXPONENT)
        total = total + before[1] * shrink
        context = context + before[2] * shrink
    return raised, low, top, total, context


def forward_kernel(count, first, tile, *refs):
    chunks, refs = refs[:count], refs[count:]
    qt_ref, refs = refs[0], refs[1:]
    if not first:
        stats_in, context_in, refs = refs[0], refs[1], refs[2:]
    stats_ref, context_ref, low_ref, k_ref, vt_ref = refs
    heads, pair_rows, _ = chunks[0].shape
    for h in range(heads):
        split_chunks(chunks, h, pair_rows // 2, k_ref=k_ref, vt_ref=vt_ref)

    @tiles(qt_ref.shape[2] // tile)
    def _(j):
        here = tokens_of(j, tile)
        for h in range(heads):
            before = None
            if not first:
                before = (stats_in[h, 0:1, here], stats_in[h, 1:2, here], context_in[h, :, here])
            _, low, top, total, context = raise_scores(
                k_ref[h], qt_ref[h, :, here], vt_ref[h], before
            )
            low_ref[h, :, here] = low
            stats_ref[h, 0:1, here] = top
            stats_ref[h, 1:2, here] = total
            context_ref[h, :, here] = context


def gradients(raised, low, scale, row_dot, qt, gt, refs, h):
    v_ref, kt_ref, gk_ref, gv_ref = refs
    grad_weights = dot(v_ref[h], gt)
    grad_scores = (raised * (grad_weights - row_dot)).astype(jnp.bfloat16)
    grad_q = dot(kt_ref[h], grad_scores) * (scale * FACTOR)
    scaled = (qt.astype(jnp.float32) * (scale * FACTOR)).astype(jnp.bfloat16)
    gk_ref[h] += dot(grad_scores, scaled, NT)
    gv_ref[h] += dot(low, (gt.astype(jnp.float32) * scale).astype(jnp.bfloat16), NT)
    return grad_q


def turn_kernel(count, tile, *refs):
    chunks, refs = refs[:count], refs[count:]
    qt_ref, gt_ref, stats_in, context_in = refs[:4]
    stats_ref, context_ref, grad_q_ref = refs[4:7]
    outs, refs = refs[7 : 7 + count], refs[7 + count :]
    k_ref, vt_ref, v_ref, kt_ref, gk_ref, gv_ref = refs
    heads, pair_rows, _ = chunks[0].shape
    rows = pair_rows // 2
    for h in range(heads):
        split_chunks(chunks, h, rows, k_ref, v_ref, kt_ref, vt_ref)
    gk_ref[...] = jnp.zeros_like(gk_ref)
    gv_ref[...] = jnp.zeros_like(gv_ref)

    @tiles(qt_ref.shape[2] // tile)
    def _(j):
        here = tokens_of(j, tile)
        for h in range(heads):
            qt, gt = qt_ref[h, :, here], gt_ref[h, :, here]
            before = (stats_in[h, 0:1, here], stats_in[h, 1:2, here], context_in[h, :, here])
            raised, low, top, total, context = raise_scores(k_ref[h], qt, vt_ref[h], before)
            scale = 1.0 / total
            context = context * scale
            row_dot = jnp.sum(gt.astype(jnp.float32) * context, axis=0, keepdims=True)
            context_ref[h, :, here] = context
            stats_ref[h, 0:1, here] = top
            stats_ref[h, 1:2, here] = scale
            stats_ref[h, 2:3, here] = row_dot
            grad_q_ref[h, :, here] = gradients(
                raised, low, scale, row_dot, qt, gt, (v_ref, kt_ref, gk_ref, gv_ref), h
            )

    for h in range(heads):
        join_chunks(outs, h, rows, gk_ref, gv_ref)


def backward_kernel(back, counts, first, tile, *refs):
    refs = refs[back:]
    groups = []
    for count in counts:
        groups.append((refs[:count], refs[count], refs[count + 1]))
        refs = refs[count + 2 :]
    qt_ref, gt_ref, stats_ref, grad_q_in = refs[:4]
    if first:
        ready_ref, rows_ref, grad_q_ref, refs = refs[4], refs[5], refs[6], refs[7:]
    else:
        rows_ref, refs = refs[4], refs[5:]
    outs, refs = refs[: sum(counts)], refs[sum(counts) :]
    scratch = [refs[i : i + 4] for i in range(0, len(refs), 4)]
    heads, pair_rows, _ = groups[0][0][0].shape
    rows = pair_rows // 2
    for (chunks, _, _), (v_ref, kt_ref, gk_ref, gv_ref) in zip(groups, scratch):
        for h in range(heads):
            split_chunks(chunks, h, rows, v_ref=v_ref, kt_ref=kt_ref)
        gk_ref[...] = jnp.zeros_like(gk_ref)
        gv_ref[...] = jnp.zeros_like(gv_ref)

    @tiles(qt_ref.shape[2] // tile)
    def _(j):
        here = tokens_of(j, tile)
        for h in range(heads):
            columns = slice(h * HEAD, (h + 1) * HEAD)
            qt, gt = qt_ref[h, :, here], gt_ref[h, :, here]
            top, scale, row_dot = (stats_ref[h, i : i + 1, here] for i in range(3))
            grad_q = grad_q_in[h, :, here]
            for (_, low_ref, then_ref), own in zip(groups, scratch):
                shrunk = jnp.exp2((then_ref[h, 0:1, here] - top) * EXPONENT)
                low = low_ref[h, :, here]
                raised = low.astype(jnp.float32)
                grad_q = grad_q + gradients(
                    raised, low, scale * shrunk, row_dot, qt, gt, own, h
                )
            if first:
                grad_q_ref[h, :, here] = grad_q
                grad_q = ready_ref[h, :, here]
            rows_ref[0, here, columns] = grad_q.T.astype(rows_ref.dtype)

    for count, (_, _, gk_ref, gv_ref) in zip(counts, scratch):
        for h in range(heads):
            join_chunks(outs[:count], h, rows, gk_ref, gv_ref)
        outs = outs[count:]


def cost(heads, rows, tokens, matmuls):
    return pl.CostEstimate(
        flops=2 * matmuls * heads * rows * tokens * HEAD,
        bytes_accessed=heads * (rows + tokens) * HEAD * 8,
        transcendentals=heads * rows * tokens,
    )


def attend(groups, queries, upstream, send_back):
    heads, pair_rows, _ = groups[0][0].shape
    rows = pair_rows // 2
    enc_len = sum(len(g) for g in groups) * rows
    tokens = queries.shape[1]
    qt, gt = turned(queries), turned(upstream)
    stats_shape = jax.ShapeDtypeStruct((heads, 8, tokens), jnp.float32)
    wide_shape = jax.ShapeDtypeStruct((heads, HEAD, tokens), jnp.float32)
    rows_shape = jax.ShapeDtypeStruct(queries.shape, queries.dtype)
    compiler_params = params(enc_len)

    def natural(count):
        return pltpu.VMEM((heads, count * rows, HEAD), jnp.bfloat16)

    def across(count, extra=0):
        return pltpu.VMEM((heads, HEAD + extra, count * rows), jnp.bfloat16)

    def sums(count):
        return pltpu.VMEM((heads, count * rows, HEAD), jnp.float32)

    def shapes_of(group):
        return [jax.ShapeDtypeStruct(c.shape, c.dtype) for c in group]

    state, kept = [], []
    for group in groups[:-1]:
        count = len(group)
        low_shape = jax.ShapeDtypeStruct((heads, count * rows, tokens), jnp.bfloat16)
        stats, context, low = pl.pallas_call(
            functools.partial(forward_kernel, count, not state, tile_of(count * rows, tokens)),
            out_shape=[stats_shape, wide_shape, low_shape],
            in_specs=[VMEM] * (count + 1 + len(state)),
            out_specs=[VMEM] * 3,
            scratch_shapes=[natural(count), across(count, 16)],
            compiler_params=compiler_params,
            cost_estimate=cost(heads, count * rows, tokens, 2),
            name="forward",
        )(*group, qt, *state)
        state = [stats, context]
        kept.append((low, stats))

    group, count = groups[-1], len(groups[-1])
    final, context, grad_q, *grads = pl.pallas_call(
        functools.partial(turn_kernel, count, tile_of(count * rows, tokens)),
        out_shape=[stats_shape, wide_shape, wide_shape] + shapes_of(group),
        in_specs=[VMEM] * (count + 4),
        out_specs=[VMEM] * (count + 3),
        scratch_shapes=[natural(count), across(count, 16), natural(count), across(count)]
        + [sums(count)] * 2,
        compiler_params=compiler_params,
        cost_estimate=cost(heads, count * rows, tokens, 6),
        name="turn",
    )(*group, qt, gt, *state)
    returned = [send_back(len(groups) - 1, grads)]

    for part in (list(range(len(groups) - 2, 0, -1)), [0]):
        first = part != [0]
        counts = [len(groups[i]) for i in part]
        back = [] if first else returned[0]
        operands = []
        for i in part:
            operands += [*groups[i], *kept[i]]
        operands += [qt, gt, final, grad_q, *([context] if first else [])]
        shapes = [rows_shape, wide_shape] if first else [rows_shape]
        outs = pl.pallas_call(
            functools.partial(
                backward_kernel, len(back), counts, first, tile_of(max(counts) * rows, tokens)
            ),
            out_shape=shapes + shapes_of(sum((groups[i] for i in part), [])),
            in_specs=[ANY] * len(back) + [VMEM] * len(operands),
            out_specs=[VMEM] * (len(shapes) + sum(counts)),
            scratch_shapes=[
                shape
                for count in counts
                for shape in (natural(count), across(count), sums(count), sums(count))
            ],
            compiler_params=compiler_params,
            cost_estimate=cost(heads, sum(counts) * rows, tokens, 4),
            name="backward",
        )(*back, *operands)
        if first:
            context_rows, grad_q = outs[:2]
        else:
            grad_query = outs[0]
        blocks = list(outs[len(shapes) :])
        for i in part:
            returned.append(send_back(i, blocks[: len(groups[i])]))
            blocks = blocks[len(groups[i]) :]
    return context_rows, grad_query


def shards(pairs, queries, upstream):
    _, rows, _, width = pairs.shape
    heads = queries.shape[2] // HEAD
    offsets = offset_groups()
    order = sum(offsets, [])
    blocks = []
    for offset, block in zip(order, pack(pairs, order, heads)):
        block = block.reshape(heads, 2 * rows, HEAD)
        blocks.append(lax.ppermute(block, AXES, route(offset, False)))
    groups = []
    for group in offsets:
        groups.append(blocks[: len(group)])
        blocks = blocks[len(group) :]
    homes, returned = [], []

    def send_back(i, grads):
        back = [lax.ppermute(g, AXES, route(o, True)) for o, g in zip(offsets[i], grads)]
        homes.extend(offsets[i])
        returned.extend(b.reshape(heads, rows, 2, HEAD) for b in back)
        return back

    context, grad_query = attend(groups, queries, upstream, send_back)
    return context, grad_query, unpack(returned, homes, width)


def solution(mesh):
    return jax.shard_map(
        shards,
        mesh=mesh,
        in_specs=(
            P("segment", ("seq", "tp"), None, None),
            P("segment", None, ("seq", "tp")),
            P("segment", None, ("seq", "tp")),
        ),
        out_specs=(
            P("segment", None, ("seq", "tp")),
            P("segment", None, ("seq", "tp")),
            P("segment", ("seq", "tp"), None, None),
        ),
        check_vma=False,
    )
```

```python
import functools

import jax
import jax.numpy as jnp
from jax import lax
from jax.experimental import pallas as pl
from jax.experimental.pallas import tpu as pltpu
from jax.sharding import PartitionSpec as P

HEAD = 128
AXES = ("segment", "seq", "tp")
FACTOR = HEAD**-0.5
EXPONENT = FACTOR * 1.4426950408889634
MIB = 1 << 20
NT = ((1,), (1,))
WAITS = (False, False)
ANY = pl.BlockSpec(memory_space=pl.ANY)
HBM = pl.BlockSpec(memory_space=pltpu.HBM)
VMEM = pl.BlockSpec(memory_space=pltpu.VMEM)


def offset_groups():
    seq_count = lax.axis_size("seq")
    tp_count = lax.axis_size("tp")
    order = [(dz, dy) for dy in reversed(range(tp_count)) for dz in range(seq_count)]
    order.sort(key=lambda o: (-o[1], -abs(o[0] - seq_count / 2 - 0.25)))
    half = len(order) // 2
    return [order[:half], order[half:]]


def group_at(offset):
    seq_count = lax.axis_size("seq")
    tp_count = lax.axis_size("tp")
    z = lax.rem(lax.axis_index("seq") + offset[0], seq_count)
    y = lax.rem(lax.axis_index("tp") + offset[1], tp_count)
    return z * tp_count + y


def route(offset, parity, back):
    segments, seq_count, tp_count = (lax.axis_size(a) for a in AXES)
    hops = []
    for s in range(parity, segments, 2):
        for z in range(seq_count):
            for y in range(tp_count):
                source = (s * seq_count + z) * tp_count + y
                s_to = (s + 1) % segments
                z_to = (z + offset[0]) % seq_count
                y_to = (y + offset[1]) % tp_count
                target = (s_to * seq_count + z_to) * tp_count + y_to
                hops.append((target, source) if back else (source, target))
    return hops


def on_parity(parity, kernel):
    def run(*refs):
        @pl.when(lax.rem(lax.axis_index("segment"), 2) == parity)
        def _():
            kernel(*refs)

    return run


def params(enc_len):
    return pltpu.CompilerParams(vmem_limit_bytes=(12 + enc_len * 36 // 4096) * MIB)


def pack(pairs, order, heads):
    _, rows, _, width = pairs.shape
    local = heads * HEAD

    def kernel(pairs_ref, *outs):
        @pl.loop(0, rows // 16)
        def _(r):
            here = pl.ds(pl.multiple_of(r * 16, 16), 16)
            for out, offset in zip(outs, order):
                base = group_at(offset) * local
                for h in range(heads):
                    column = pl.multiple_of(base + h * HEAD, HEAD)
                    out[h, here] = pairs_ref[0, here, :, pl.ds(column, HEAD)]

    return pl.pallas_call(
        kernel,
        out_shape=[jax.ShapeDtypeStruct((heads, rows, 2, HEAD), pairs.dtype)] * len(order),
        in_specs=[VMEM],
        out_specs=[VMEM] * len(order),
        compiler_params=pltpu.CompilerParams(vmem_limit_bytes=24 * MIB),
        name="pack",
    )(pairs)


def unpack(blocks, order, width):
    heads, rows, _, _ = blocks[0].shape
    local = heads * HEAD
    count = len(order)
    parts = 4 if rows % 64 == 0 else 1
    size = rows // parts

    def kernel(*refs):
        out, held, sem = refs[2 * count], refs[-2], refs[-1]

        def store(r):
            here = pl.ds(pl.multiple_of(r * size, size), size)
            return pltpu.make_async_copy(held.at[here], out.at[0, here], sem.at[r])

        def fill(r, ins):
            here = pl.ds(pl.multiple_of(r * size, size), size)
            for block, offset in zip(ins, order):
                base = group_at(offset) * local
                for h in range(heads):
                    column = pl.multiple_of(base + h * HEAD, HEAD)
                    held[here, :, pl.ds(column, HEAD)] = block[h, here]

        @pl.loop(0, parts)
        def _(r):
            for parity in range(2):
                on_parity(parity, fill)(r, refs[parity * count : (parity + 1) * count])
            store(r).start()

        for r in range(parts):
            store(r).wait()

    return pl.pallas_call(
        kernel,
        out_shape=jax.ShapeDtypeStruct((1, rows, 2, width), blocks[0].dtype),
        in_specs=[VMEM] * (2 * count),
        out_specs=HBM,
        scratch_shapes=[
            pltpu.VMEM((rows, 2, width), blocks[0].dtype),
            pltpu.SemaphoreType.DMA((parts,)),
        ],
        compiler_params=pltpu.CompilerParams(vmem_limit_bytes=24 * MIB),
        name="unpack",
    )(*blocks)


def turned_back(arrays, dtype):
    heads, _, tokens = arrays[0].shape
    tile = 256 if tokens % 256 == 0 else tokens

    def kernel(*refs):
        out = refs[2]

        def turn(ref):
            for h in range(heads):
                for j in range(tokens // tile):
                    here = slice(j * tile, (j + 1) * tile)
                    out[0, here, h * HEAD : (h + 1) * HEAD] = ref[h, :, here].T.astype(dtype)

        on_parity(1, turn)(refs[0])
        on_parity(0, turn)(refs[1])

    return pl.pallas_call(
        kernel,
        out_shape=jax.ShapeDtypeStruct((1, tokens, heads * HEAD), dtype),
        in_specs=[VMEM] * 2,
        out_specs=VMEM,
        compiler_params=pltpu.CompilerParams(vmem_limit_bytes=16 * MIB),
        name="turned_back",
    )(*arrays)


def turned(rows):
    _, tokens, local = rows.shape
    heads = local // HEAD
    tile = 256 if tokens % 256 == 0 else tokens

    def kernel(rows_ref, out_ref):
        for h in range(heads):
            for j in range(tokens // tile):
                here = slice(j * tile, (j + 1) * tile)
                block = rows_ref[0, here, h * HEAD : (h + 1) * HEAD]
                out_ref[h, :, here] = block.astype(jnp.float32).T.astype(rows.dtype)

    return pl.pallas_call(
        kernel,
        out_shape=jax.ShapeDtypeStruct((heads, HEAD, tokens), rows.dtype),
        in_specs=[VMEM],
        out_specs=VMEM,
        compiler_params=pltpu.CompilerParams(vmem_limit_bytes=16 * MIB),
        name="turned",
    )(rows)


def tiles(count):
    def run(body):
        if count <= 2:
            for j in range(count):
                body(j)
        else:
            pl.loop(0, count)(body)

    return run


def tokens_of(j, tile):
    return pl.ds(j * tile if isinstance(j, int) else pl.multiple_of(j * tile, tile), tile)


def tile_of(rows, tokens):
    for parts in range(1, tokens // 256 + 1):
        if tokens % (256 * parts) == 0 and rows * (tokens // parts) * 4 <= 5 * MIB // 4:
            return tokens // parts
    return 256 if tokens % 256 == 0 else tokens


def dot(a, b, contract=((1,), (0,))):
    return lax.dot_general(a, b, (contract, ((), ())), preferred_element_type=jnp.float32)


def shuffle(rows, join):
    to = lax.broadcasted_iota(jnp.int32, (2 * rows, 2 * rows), 1 if join else 0)
    source = lax.broadcasted_iota(jnp.int32, (2 * rows, 2 * rows), 0 if join else 1)
    wanted = jnp.where(to < rows, 2 * to, 2 * (to - rows) + 1)
    return jnp.where(source == wanted, 1.0, 0.0).astype(jnp.bfloat16)


def split_chunks(chunks, h, rows, k_ref=None, v_ref=None, kt_ref=None, vt_ref=None):
    split = shuffle(rows, False)
    for i, chunk in enumerate(chunks):
        both = dot(split, chunk[h])
        here = slice(i * rows, (i + 1) * rows)
        keys, values = both[:rows], both[rows:]
        if k_ref is not None:
            k_ref[h, here, :] = keys.astype(jnp.bfloat16)
        if v_ref is not None:
            v_ref[h, here, :] = values.astype(jnp.bfloat16)
        if kt_ref is not None:
            kt_ref[h, :, here] = keys.T.astype(jnp.bfloat16)
        if vt_ref is not None:
            vt_ref[h, :HEAD, here] = values.T.astype(jnp.bfloat16)
    if vt_ref is not None:
        tail = (vt_ref.shape[1] - HEAD, vt_ref.shape[2])
        vt_ref[h, HEAD:, :] = jnp.ones(tail, jnp.bfloat16)


def join_chunks(outs, h, rows, gk_ref, gv_ref):
    join = shuffle(rows, True)
    for i, out in enumerate(outs):
        here = slice(i * rows, (i + 1) * rows)
        both = jnp.concatenate([gk_ref[h, here, :], gv_ref[h, here, :]], axis=0)
        out[h] = dot(join, both.astype(jnp.bfloat16)).astype(jnp.bfloat16)


def raise_scores(keys, qt, values_t, before):
    scores = dot(keys, qt)
    top = jnp.max(scores, axis=0, keepdims=True)
    if before is not None:
        top = jnp.maximum(top, before[0])
    raised = jnp.exp2((scores - top) * EXPONENT)
    low = raised.astype(jnp.bfloat16)
    summed = dot(values_t, low)
    total, context = summed[HEAD : HEAD + 1], summed[:HEAD]
    if before is not None:
        shrink = jnp.exp2((before[0] - top) * EXPONENT)
        total = total + before[1] * shrink
        context = context + before[2] * shrink
    return raised, low, top, total, context


def forward_kernel(count, first, tile, *refs):
    chunks, refs = refs[:count], refs[count:]
    qt_ref, refs = refs[0], refs[1:]
    if not first:
        stats_in, context_in, refs = refs[0], refs[1], refs[2:]
    stats_ref, context_ref, low_ref, k_ref, vt_ref = refs
    heads, pair_rows, _ = chunks[0].shape
    for h in range(heads):
        split_chunks(chunks, h, pair_rows // 2, k_ref=k_ref, vt_ref=vt_ref)

    @tiles(qt_ref.shape[2] // tile)
    def _(j):
        here = tokens_of(j, tile)
        for h in range(heads):
            before = None
            if not first:
                before = (stats_in[h, 0:1, here], stats_in[h, 1:2, here], context_in[h, :, here])
            _, low, top, total, context = raise_scores(
                k_ref[h], qt_ref[h, :, here], vt_ref[h], before
            )
            low_ref[h, :, here] = low
            stats_ref[h, 0:1, here] = top
            stats_ref[h, 1:2, here] = total
            context_ref[h, :, here] = context


def gradients(raised, low, scale, row_dot, qt, gt, refs, h):
    v_ref, kt_ref, gk_ref, gv_ref = refs
    grad_weights = dot(v_ref[h], gt)
    grad_scores = (raised * (grad_weights - row_dot)).astype(jnp.bfloat16)
    grad_q = dot(kt_ref[h], grad_scores) * (scale * FACTOR)
    scaled = (qt.astype(jnp.float32) * (scale * FACTOR)).astype(jnp.bfloat16)
    gk_ref[h] += dot(grad_scores, scaled, NT)
    gv_ref[h] += dot(low, (gt.astype(jnp.float32) * scale).astype(jnp.bfloat16), NT)
    return grad_q


def turn_kernel(count, tile, *refs):
    chunks, refs = refs[:count], refs[count:]
    qt_ref, gt_ref, stats_in, context_in = refs[:4]
    stats_ref, context_ref, grad_q_ref = refs[4:7]
    outs, refs = refs[7 : 7 + count], refs[7 + count :]
    k_ref, vt_ref, v_ref, kt_ref, gk_ref, gv_ref = refs
    heads, pair_rows, _ = chunks[0].shape
    rows = pair_rows // 2
    for h in range(heads):
        split_chunks(chunks, h, rows, k_ref, v_ref, kt_ref, vt_ref)
    gk_ref[...] = jnp.zeros_like(gk_ref)
    gv_ref[...] = jnp.zeros_like(gv_ref)

    @tiles(qt_ref.shape[2] // tile)
    def _(j):
        here = tokens_of(j, tile)
        for h in range(heads):
            qt, gt = qt_ref[h, :, here], gt_ref[h, :, here]
            before = (stats_in[h, 0:1, here], stats_in[h, 1:2, here], context_in[h, :, here])
            raised, low, top, total, context = raise_scores(k_ref[h], qt, vt_ref[h], before)
            scale = 1.0 / total
            context = context * scale
            row_dot = jnp.sum(gt.astype(jnp.float32) * context, axis=0, keepdims=True)
            context_ref[h, :, here] = context
            stats_ref[h, 0:1, here] = top
            stats_ref[h, 1:2, here] = scale
            stats_ref[h, 2:3, here] = row_dot
            grad_q_ref[h, :, here] = gradients(
                raised, low, scale, row_dot, qt, gt, (v_ref, kt_ref, gk_ref, gv_ref), h
            )

    for h in range(heads):
        join_chunks(outs, h, rows, gk_ref, gv_ref)


def backward_kernel(back, count, tile, *refs):
    refs = refs[back:]
    chunks, refs = refs[:count], refs[count:]
    low_ref, then_ref, qt_ref, gt_ref, stats_ref, grad_q_in, grad_q_ref = refs[:7]
    outs, own = refs[7 : 7 + count], refs[7 + count :]
    v_ref, kt_ref, gk_ref, gv_ref = own
    heads, pair_rows, _ = chunks[0].shape
    rows = pair_rows // 2
    for h in range(heads):
        split_chunks(chunks, h, rows, v_ref=v_ref, kt_ref=kt_ref)
    gk_ref[...] = jnp.zeros_like(gk_ref)
    gv_ref[...] = jnp.zeros_like(gv_ref)

    @tiles(qt_ref.shape[2] // tile)
    def _(j):
        here = tokens_of(j, tile)
        for h in range(heads):
            qt, gt = qt_ref[h, :, here], gt_ref[h, :, here]
            top, scale, row_dot = (stats_ref[h, i : i + 1, here] for i in range(3))
            shrunk = jnp.exp2((then_ref[h, 0:1, here] - top) * EXPONENT)
            low = low_ref[h, :, here]
            raised = low.astype(jnp.float32)
            grad_q_ref[h, :, here] = grad_q_in[h, :, here] + gradients(
                raised, low, scale * shrunk, row_dot, qt, gt, own, h
            )

    for h in range(heads):
        join_chunks(outs, h, rows, gk_ref, gv_ref)


def cost(heads, rows, tokens, matmuls):
    return pl.CostEstimate(
        flops=2 * matmuls * heads * rows * tokens * HEAD,
        bytes_accessed=heads * (rows + tokens) * HEAD * 8,
        transcendentals=heads * rows * tokens,
    )


def attend(groups, qt, gt, parity, send_back):
    heads, pair_rows, _ = groups[0][0].shape
    rows = pair_rows // 2
    enc_len = sum(len(g) for g in groups) * rows
    tokens = qt.shape[2]
    stats_shape = jax.ShapeDtypeStruct((heads, 8, tokens), jnp.float32)
    wide_shape = jax.ShapeDtypeStruct((heads, HEAD, tokens), jnp.float32)
    compiler_params = params(enc_len)

    def natural(count):
        return pltpu.VMEM((heads, count * rows, HEAD), jnp.bfloat16)

    def across(count, extra=0):
        return pltpu.VMEM((heads, HEAD + extra, count * rows), jnp.bfloat16)

    def sums(count):
        return pltpu.VMEM((heads, count * rows, HEAD), jnp.float32)

    def shapes_of(group):
        return [jax.ShapeDtypeStruct(c.shape, c.dtype) for c in group]

    def here(kernel, *static):
        return on_parity(parity, functools.partial(kernel, *static))

    group, count = groups[0], len(groups[0])
    tile = tile_of(count * rows, tokens)
    low_shape = jax.ShapeDtypeStruct((heads, count * rows, tokens), jnp.bfloat16)
    stats, context, low = pl.pallas_call(
        here(forward_kernel, count, True, tile),
        out_shape=[stats_shape, wide_shape, low_shape],
        in_specs=[VMEM] * (count + 1),
        out_specs=[VMEM] * 3,
        scratch_shapes=[natural(count), across(count, 16)],
        compiler_params=compiler_params,
        cost_estimate=cost(heads, count * rows, tokens, 2),
        name="forward",
    )(*group, qt)

    group, count = groups[1], len(groups[1])
    tile = tile_of(count * rows, tokens)
    final, context, grad_q, *grads = pl.pallas_call(
        here(turn_kernel, count, tile),
        out_shape=[stats_shape, wide_shape, wide_shape] + shapes_of(group),
        in_specs=[VMEM] * (count + 4),
        out_specs=[VMEM] * (count + 3),
        scratch_shapes=[natural(count), across(count, 16), natural(count), across(count)]
        + [sums(count)] * 2,
        compiler_params=compiler_params,
        cost_estimate=cost(heads, count * rows, tokens, 6),
        name="turn",
    )(*group, qt, gt, stats, context)
    back = send_back(1, grads)

    group, count = groups[0], len(groups[0])
    back = back if WAITS[parity] else []
    grad_q, *grads = pl.pallas_call(
        here(backward_kernel, len(back), count, tile_of(count * rows, tokens)),
        out_shape=[wide_shape] + shapes_of(group),
        in_specs=[ANY] * len(back) + [VMEM] * (count + 6),
        out_specs=[VMEM] * (count + 1),
        scratch_shapes=[natural(count), across(count), sums(count), sums(count)],
        compiler_params=compiler_params,
        cost_estimate=cost(heads, count * rows, tokens, 4),
        name="backward",
    )(*back, *group, low, stats, qt, gt, final, grad_q)
    send_back(0, grads)
    return context, grad_q


def shards(pairs, queries, upstream):
    _, rows, _, width = pairs.shape
    heads = queries.shape[2] // HEAD
    offsets = offset_groups()
    order = sum(offsets, [])
    blocks = [b.reshape(heads, 2 * rows, HEAD) for b in pack(pairs, order, heads)]
    qt, gt = turned(queries), turned(upstream)
    arrived = []
    for parity in range(2):
        moved = [lax.ppermute(b, AXES, route(o, parity, False)) for o, b in zip(order, blocks)]
        arrived.append([moved[: len(offsets[0])], moved[len(offsets[0]) :]])
    results, returned = [], []
    for parity in range(2):
        parts = [None, None]

        def send_back(i, grads):
            parts[i] = [
                lax.ppermute(g, AXES, route(o, parity, True)) for o, g in zip(offsets[i], grads)
            ]
            return parts[i]

        results.append(attend(arrived[parity], qt, gt, 1 - parity, send_back))
        returned += [b.reshape(heads, rows, 2, HEAD) for b in parts[0] + parts[1]]
    context = turned_back([results[0][0], results[1][0]], queries.dtype)
    grad_query = turned_back([results[0][1], results[1][1]], queries.dtype)
    return context, grad_query, unpack(returned, order, width)


def solution(mesh):
    return jax.shard_map(
        shards,
        mesh=mesh,
        in_specs=(
            P("segment", ("seq", "tp"), None, None),
            P("segment", None, ("seq", "tp")),
            P("segment", None, ("seq", "tp")),
        ),
        out_specs=(
            P("segment", None, ("seq", "tp")),
            P("segment", None, ("seq", "tp")),
            P("segment", ("seq", "tp"), None, None),
        ),
        check_vma=False,
    )
```

```python
import functools

import jax
import jax.numpy as jnp
from jax import lax
from jax.experimental import pallas as pl
from jax.experimental.pallas import tpu as pltpu
from jax.sharding import PartitionSpec as P

HEAD = 128
AXES = ("segment", "seq", "tp")
FACTOR = HEAD**-0.5
EXPONENT = FACTOR * 1.4426950408889634
MIB = 1 << 20
ANY = pl.BlockSpec(memory_space=pl.ANY)
HBM = pl.BlockSpec(memory_space=pltpu.HBM)
VMEM = pl.BlockSpec(memory_space=pltpu.VMEM)


def offset_groups():
    seq_count = lax.axis_size("seq")
    tp_count = lax.axis_size("tp")
    near = [(0, dy) for dy in reversed(range(tp_count))]
    far = [(dz, dy) for dy in reversed(range(tp_count)) for dz in range(1, seq_count)]
    far.sort(key=lambda o: -abs(o[0] - seq_count / 2))
    eighth = max(1, (len(near) + len(far)) // 8)
    short, long = far[: -2 * eighth], far[-2 * eighth :]
    short.sort(key=lambda o: -o[1])
    half = len(short) // 2
    return [
        short[:1] + near[:1] + short[1:half],
        short[half + eighth :] + near[1:],
        short[half : half + eighth] + long[:eighth],
        long[eighth:],
    ]


def group_at(offset):
    seq_count = lax.axis_size("seq")
    tp_count = lax.axis_size("tp")
    z = lax.rem(lax.axis_index("seq") + offset[0], seq_count)
    y = lax.rem(lax.axis_index("tp") + offset[1], tp_count)
    return z * tp_count + y


def route(offset, back):
    segments, seq_count, tp_count = (lax.axis_size(a) for a in AXES)
    hops = []
    for s in range(segments):
        for z in range(seq_count):
            for y in range(tp_count):
                source = (s * seq_count + z) * tp_count + y
                s_to = (s + 1) % segments
                z_to = (z + offset[0]) % seq_count
                y_to = (y + offset[1]) % tp_count
                target = (s_to * seq_count + z_to) * tp_count + y_to
                hops.append((target, source) if back else (source, target))
    return hops


def params(enc_len):
    return pltpu.CompilerParams(vmem_limit_bytes=(12 + enc_len * 36 // 4096) * MIB)


def pack(pairs, order, heads):
    _, rows, _, width = pairs.shape
    local = heads * HEAD

    def kernel(pairs_ref, *outs):
        @pl.loop(0, rows // 16)
        def _(r):
            here = pl.ds(pl.multiple_of(r * 16, 16), 16)
            for out, offset in zip(outs, order):
                base = group_at(offset) * local
                for h in range(heads):
                    column = pl.multiple_of(base + h * HEAD, HEAD)
                    out[h, here] = pairs_ref[0, here, :, pl.ds(column, HEAD)]

    return pl.pallas_call(
        kernel,
        out_shape=[jax.ShapeDtypeStruct((heads, rows, 2, HEAD), pairs.dtype)] * len(order),
        in_specs=[VMEM],
        out_specs=[VMEM] * len(order),
        compiler_params=pltpu.CompilerParams(vmem_limit_bytes=24 * MIB),
        name="pack",
    )(pairs)


def unpack(blocks, order, width):
    heads, rows, _, _ = blocks[0].shape
    local = heads * HEAD
    parts = 4 if rows % 64 == 0 else 1
    size = rows // parts

    def kernel(*refs):
        ins, out, held, sem = refs[: len(order)], refs[len(order)], refs[-2], refs[-1]

        def store(r):
            here = pl.ds(pl.multiple_of(r * size, size), size)
            return pltpu.make_async_copy(held.at[here], out.at[0, here], sem.at[r])

        @pl.loop(0, parts)
        def _(r):
            here = pl.ds(pl.multiple_of(r * size, size), size)
            for block, offset in zip(ins, order):
                base = group_at(offset) * local
                for h in range(heads):
                    column = pl.multiple_of(base + h * HEAD, HEAD)
                    held[here, :, pl.ds(column, HEAD)] = block[h, here]
            store(r).start()

        for r in range(parts):
            store(r).wait()

    return pl.pallas_call(
        kernel,
        out_shape=jax.ShapeDtypeStruct((1, rows, 2, width), blocks[0].dtype),
        in_specs=[VMEM] * len(order),
        out_specs=HBM,
        scratch_shapes=[
            pltpu.VMEM((rows, 2, width), blocks[0].dtype),
            pltpu.SemaphoreType.DMA((parts,)),
        ],
        compiler_params=pltpu.CompilerParams(vmem_limit_bytes=24 * MIB),
        name="unpack",
    )(*blocks)


def turned(rows):
    _, tokens, local = rows.shape
    heads = local // HEAD
    tile = 256 if tokens % 256 == 0 else tokens

    def kernel(rows_ref, out_ref):
        for h in range(heads):
            for j in range(tokens // tile):
                here = slice(j * tile, (j + 1) * tile)
                block = rows_ref[0, here, h * HEAD : (h + 1) * HEAD]
                out_ref[h, :, here] = block.astype(jnp.float32).T.astype(rows.dtype)

    return pl.pallas_call(
        kernel,
        out_shape=jax.ShapeDtypeStruct((heads, HEAD, tokens), rows.dtype),
        in_specs=[VMEM],
        out_specs=VMEM,
        compiler_params=pltpu.CompilerParams(vmem_limit_bytes=16 * MIB),
        name="turned",
    )(rows)


def tiles(count):
    def run(body):
        if count <= 2:
            for j in range(count):
                body(j)
        else:
            pl.loop(0, count)(body)

    return run


def tokens_of(j, tile):
    return pl.ds(j * tile if isinstance(j, int) else pl.multiple_of(j * tile, tile), tile)


def tile_of(rows, tokens):
    for parts in range(1, tokens // 256 + 1):
        if tokens % (256 * parts) == 0 and rows * (tokens // parts) * 4 <= 5 * MIB // 4:
            return tokens // parts
    return 256 if tokens % 256 == 0 else tokens


def dot(a, b, contract=((1,), (0,))):
    return lax.dot_general(a, b, (contract, ((), ())), preferred_element_type=jnp.float32)


def shuffle(rows, join):
    to = lax.broadcasted_iota(jnp.int32, (2 * rows, 2 * rows), 1 if join else 0)
    source = lax.broadcasted_iota(jnp.int32, (2 * rows, 2 * rows), 0 if join else 1)
    wanted = jnp.where(to < rows, 2 * to, 2 * (to - rows) + 1)
    return jnp.where(source == wanted, 1.0, 0.0).astype(jnp.bfloat16)


def split_chunks(chunks, h, rows, k_ref=None, v_ref=None, kt_ref=None, vt_ref=None):
    split = shuffle(rows, False)
    for i, chunk in enumerate(chunks):
        both = dot(split, chunk[h])
        here = slice(i * rows, (i + 1) * rows)
        keys, values = both[:rows], both[rows:]
        if k_ref is not None:
            k_ref[h, here, :] = keys.astype(jnp.bfloat16)
        if v_ref is not None:
            v_ref[h, here, :] = values.astype(jnp.bfloat16)
        if kt_ref is not None:
            kt_ref[h, :, here] = keys.T.astype(jnp.bfloat16)
        if vt_ref is not None:
            vt_ref[h, :HEAD, here] = values.T.astype(jnp.bfloat16)
    if vt_ref is not None:
        tail = (vt_ref.shape[1] - HEAD, vt_ref.shape[2])
        vt_ref[h, HEAD:, :] = jnp.ones(tail, jnp.bfloat16)


def join_chunks(outs, h, rows, gk_ref, gv_ref):
    join = shuffle(rows, True)
    for i, out in enumerate(outs):
        here = slice(i * rows, (i + 1) * rows)
        both = jnp.concatenate([gk_ref[h, here, :] * FACTOR, gv_ref[h, here, :]], axis=0)
        out[h] = dot(join, both.astype(jnp.bfloat16)).astype(jnp.bfloat16)


def raise_scores(keys, qt, values_t, before):
    scores = dot(keys, qt)
    top = jnp.max(scores, axis=0, keepdims=True)
    if before is not None:
        top = jnp.maximum(top, before[0])
    raised = jnp.exp2((scores - top) * EXPONENT)
    low = raised.astype(jnp.bfloat16)
    summed = dot(values_t, low)
    total, context = summed[HEAD : HEAD + 1], summed[:HEAD]
    if before is not None:
        shrink = jnp.exp2((before[0] - top) * EXPONENT)
        total = total + before[1] * shrink
        context = context + before[2] * shrink
    return raised, low, top, total, context


def forward_kernel(count, first, tile, *refs):
    chunks, refs = refs[:count], refs[count:]
    qt_ref, refs = refs[0], refs[1:]
    if not first:
        stats_in, context_in, refs = refs[0], refs[1], refs[2:]
    stats_ref, context_ref, low_ref, k_ref, vt_ref = refs
    heads, pair_rows, _ = chunks[0].shape
    for h in range(heads):
        split_chunks(chunks, h, pair_rows // 2, k_ref=k_ref, vt_ref=vt_ref)

    @tiles(qt_ref.shape[2] // tile)
    def _(j):
        here = tokens_of(j, tile)
        for h in range(heads):
            before = None
            if not first:
                before = (stats_in[h, 0:1, here], stats_in[h, 1:2, here], context_in[h, :, here])
            _, low, top, total, context = raise_scores(
                k_ref[h], qt_ref[h, :, here], vt_ref[h], before
            )
            low_ref[h, :, here] = low
            stats_ref[h, 0:1, here] = top
            stats_ref[h, 1:2, here] = total
            context_ref[h, :, here] = context


def gradients(raised, scale, row_dot, rows, gt, refs, h):
    v_ref, kt_ref, gk_ref, gv_ref = refs
    query_rows, grad_rows = rows
    weights = raised * scale
    grad_weights = dot(v_ref[h], gt)
    grad_scores = (weights * (grad_weights - row_dot)).astype(jnp.bfloat16)
    gv_ref[h] += dot(weights.astype(jnp.bfloat16), grad_rows)
    gk_ref[h] += dot(grad_scores, query_rows)
    return dot(kt_ref[h], grad_scores) * FACTOR


def turn_kernel(count, tile, *refs):
    chunks, refs = refs[:count], refs[count:]
    q_ref, g_ref, qt_ref, gt_ref, stats_in, context_in = refs[:6]
    stats_ref, context_ref, grad_q_ref = refs[6:9]
    outs, refs = refs[9 : 9 + count], refs[9 + count :]
    k_ref, vt_ref, v_ref, kt_ref, gk_ref, gv_ref = refs
    heads, pair_rows, _ = chunks[0].shape
    rows = pair_rows // 2
    for h in range(heads):
        split_chunks(chunks, h, rows, k_ref, v_ref, kt_ref, vt_ref)
    gk_ref[...] = jnp.zeros_like(gk_ref)
    gv_ref[...] = jnp.zeros_like(gv_ref)

    @tiles(qt_ref.shape[2] // tile)
    def _(j):
        here = tokens_of(j, tile)
        for h in range(heads):
            qt, gt = qt_ref[h, :, here], gt_ref[h, :, here]
            before = (stats_in[h, 0:1, here], stats_in[h, 1:2, here], context_in[h, :, here])
            raised, _, top, total, context = raise_scores(k_ref[h], qt, vt_ref[h], before)
            columns = slice(h * HEAD, (h + 1) * HEAD)
            rows_here = q_ref[0, here, columns], g_ref[0, here, columns]
            scale = 1.0 / total
            context = context * scale
            row_dot = jnp.sum(gt.astype(jnp.float32) * context, axis=0, keepdims=True)
            context_ref[h, :, here] = context
            stats_ref[h, 0:1, here] = top
            stats_ref[h, 1:2, here] = scale
            stats_ref[h, 2:3, here] = row_dot
            grad_q_ref[h, :, here] = gradients(
                raised, scale, row_dot, rows_here, gt, (v_ref, kt_ref, gk_ref, gv_ref), h
            )

    for h in range(heads):
        join_chunks(outs, h, rows, gk_ref, gv_ref)


def backward_kernel(back, counts, first, tile, *refs):
    refs = refs[back:]
    groups = []
    for count in counts:
        groups.append((refs[:count], refs[count], refs[count + 1]))
        refs = refs[count + 2 :]
    q_ref, g_ref, gt_ref, stats_ref, grad_q_in = refs[:5]
    if first:
        ready_ref, rows_ref, grad_q_ref, refs = refs[5], refs[6], refs[7], refs[8:]
    else:
        rows_ref, refs = refs[5], refs[6:]
    outs, refs = refs[: sum(counts)], refs[sum(counts) :]
    scratch = [refs[i : i + 4] for i in range(0, len(refs), 4)]
    heads, pair_rows, _ = groups[0][0][0].shape
    rows = pair_rows // 2
    for (chunks, _, _), (v_ref, kt_ref, gk_ref, gv_ref) in zip(groups, scratch):
        for h in range(heads):
            split_chunks(chunks, h, rows, v_ref=v_ref, kt_ref=kt_ref)
        gk_ref[...] = jnp.zeros_like(gk_ref)
        gv_ref[...] = jnp.zeros_like(gv_ref)

    @tiles(gt_ref.shape[2] // tile)
    def _(j):
        here = tokens_of(j, tile)
        for h in range(heads):
            columns = slice(h * HEAD, (h + 1) * HEAD)
            rows_here = q_ref[0, here, columns], g_ref[0, here, columns]
            gt = gt_ref[h, :, here]
            top, scale, row_dot = (stats_ref[h, i : i + 1, here] for i in range(3))
            grad_q = grad_q_in[h, :, here]
            for (_, low_ref, then_ref), own in zip(groups, scratch):
                shrunk = jnp.exp2((then_ref[h, 0:1, here] - top) * EXPONENT)
                raised = low_ref[h, :, here].astype(jnp.float32)
                grad_q = grad_q + gradients(
                    raised, scale * shrunk, row_dot, rows_here, gt, own, h
                )
            if first:
                grad_q_ref[h, :, here] = grad_q
                grad_q = ready_ref[h, :, here]
            rows_ref[0, here, columns] = grad_q.T.astype(rows_ref.dtype)

    for count, (_, _, gk_ref, gv_ref) in zip(counts, scratch):
        for h in range(heads):
            join_chunks(outs[:count], h, rows, gk_ref, gv_ref)
        outs = outs[count:]


def cost(heads, rows, tokens, matmuls):
    return pl.CostEstimate(
        flops=2 * matmuls * heads * rows * tokens * HEAD,
        bytes_accessed=heads * (rows + tokens) * HEAD * 8,
        transcendentals=heads * rows * tokens,
    )


def attend(groups, queries, upstream, send_back):
    heads, pair_rows, _ = groups[0][0].shape
    rows = pair_rows // 2
    enc_len = sum(len(g) for g in groups) * rows
    tokens = queries.shape[1]
    qt, gt = turned(queries), turned(upstream)
    stats_shape = jax.ShapeDtypeStruct((heads, 8, tokens), jnp.float32)
    wide_shape = jax.ShapeDtypeStruct((heads, HEAD, tokens), jnp.float32)
    rows_shape = jax.ShapeDtypeStruct(queries.shape, queries.dtype)
    compiler_params = params(enc_len)

    def natural(count):
        return pltpu.VMEM((heads, count * rows, HEAD), jnp.bfloat16)

    def across(count, extra=0):
        return pltpu.VMEM((heads, HEAD + extra, count * rows), jnp.bfloat16)

    def sums(count):
        return pltpu.VMEM((heads, count * rows, HEAD), jnp.float32)

    def shapes_of(group):
        return [jax.ShapeDtypeStruct(c.shape, c.dtype) for c in group]

    state, kept = [], []
    for group in groups[:-1]:
        count = len(group)
        low_shape = jax.ShapeDtypeStruct((heads, count * rows, tokens), jnp.bfloat16)
        stats, context, low = pl.pallas_call(
            functools.partial(forward_kernel, count, not state, tile_of(count * rows, tokens)),
            out_shape=[stats_shape, wide_shape, low_shape],
            in_specs=[VMEM] * (count + 1 + len(state)),
            out_specs=[VMEM] * 3,
            scratch_shapes=[natural(count), across(count, 16)],
            compiler_params=compiler_params,
            cost_estimate=cost(heads, count * rows, tokens, 2),
            name="forward",
        )(*group, qt, *state)
        state = [stats, context]
        kept.append((low, stats))

    group, count = groups[-1], len(groups[-1])
    final, context, grad_q, *grads = pl.pallas_call(
        functools.partial(turn_kernel, count, tile_of(count * rows, tokens)),
        out_shape=[stats_shape, wide_shape, wide_shape] + shapes_of(group),
        in_specs=[VMEM] * (count + 6),
        out_specs=[VMEM] * (count + 3),
        scratch_shapes=[natural(count), across(count, 16), natural(count), across(count)]
        + [sums(count)] * 2,
        compiler_params=compiler_params,
        cost_estimate=cost(heads, count * rows, tokens, 6),
        name="turn",
    )(*group, queries, upstream, qt, gt, *state)
    returned = [send_back(len(groups) - 1, grads)]

    for part in ([len(groups) - 2], list(range(len(groups) - 3, -1, -1))):
        first = part[-1] > 0
        counts = [len(groups[i]) for i in part]
        back = [] if first else returned[0]
        operands = []
        for i in part:
            operands += [*groups[i], *kept[i]]
        operands += [queries, upstream, gt, final, grad_q, *([context] if first else [])]
        shapes = [rows_shape, wide_shape] if first else [rows_shape]
        outs = pl.pallas_call(
            functools.partial(
                backward_kernel, len(back), counts, first, tile_of(max(counts) * rows, tokens)
            ),
            out_shape=shapes + shapes_of(sum((groups[i] for i in part), [])),
            in_specs=[ANY] * len(back) + [VMEM] * len(operands),
            out_specs=[VMEM] * (len(shapes) + sum(counts)),
            scratch_shapes=[
                shape
                for count in counts
                for shape in (natural(count), across(count), sums(count), sums(count))
            ],
            compiler_params=compiler_params,
            cost_estimate=cost(heads, sum(counts) * rows, tokens, 4),
            name="backward",
        )(*back, *operands)
        if first:
            context_rows, grad_q = outs[:2]
        else:
            grad_query = outs[0]
        blocks = list(outs[len(shapes) :])
        for i in part:
            returned.append(send_back(i, blocks[: len(groups[i])]))
            blocks = blocks[len(groups[i]) :]
    return context_rows, grad_query


def shards(pairs, queries, upstream):
    _, rows, _, width = pairs.shape
    heads = queries.shape[2] // HEAD
    offsets = offset_groups()
    order = sum(offsets, [])
    blocks = []
    for offset, block in zip(order, pack(pairs, order, heads)):
        block = block.reshape(heads, 2 * rows, HEAD)
        blocks.append(lax.ppermute(block, AXES, route(offset, False)))
    groups = []
    for group in offsets:
        groups.append(blocks[: len(group)])
        blocks = blocks[len(group) :]
    homes, returned = [], []

    def send_back(i, grads):
        back = [lax.ppermute(g, AXES, route(o, True)) for o, g in zip(offsets[i], grads)]
        homes.extend(offsets[i])
        returned.extend(b.reshape(heads, rows, 2, HEAD) for b in back)
        return back

    context, grad_query = attend(groups, queries, upstream, send_back)
    return context, grad_query, unpack(returned, homes, width)


def solution(mesh):
    return jax.shard_map(
        shards,
        mesh=mesh,
        in_specs=(
            P("segment", ("seq", "tp"), None, None),
            P("segment", None, ("seq", "tp")),
            P("segment", None, ("seq", "tp")),
        ),
        out_specs=(
            P("segment", None, ("seq", "tp")),
            P("segment", None, ("seq", "tp")),
            P("segment", ("seq", "tp"), None, None),
        ),
        check_vma=False,
    )
```

```python
import functools

import jax
import jax.numpy as jnp
from jax import lax
from jax.experimental import pallas as pl
from jax.experimental.pallas import tpu as pltpu
from jax.sharding import PartitionSpec as P

HEAD = 128
AXES = ("segment", "seq", "tp")
FACTOR = HEAD**-0.5
EXPONENT = FACTOR * 1.4426950408889634
MIB = 1 << 20
ANY = pl.BlockSpec(memory_space=pl.ANY)
HBM = pl.BlockSpec(memory_space=pltpu.HBM)
VMEM = pl.BlockSpec(memory_space=pltpu.VMEM)


def offset_groups():
    seq_count = lax.axis_size("seq")
    tp_count = lax.axis_size("tp")
    near = [(0, dy) for dy in reversed(range(tp_count))]
    far = [(dz, dy) for dy in reversed(range(tp_count)) for dz in range(1, seq_count)]
    far.sort(key=lambda o: -abs(o[0] - seq_count / 2))
    eighth = max(1, (len(near) + len(far)) // 8)
    short, long = far[: -2 * eighth], far[-2 * eighth :]
    short.sort(key=lambda o: -o[1])
    half = len(short) // 2
    return [
        short[:1] + near[:1] + short[1:half],
        short[half:] + near[1:],
        long[:eighth],
        long[eighth:],
    ]


def group_at(offset):
    seq_count = lax.axis_size("seq")
    tp_count = lax.axis_size("tp")
    z = lax.rem(lax.axis_index("seq") + offset[0], seq_count)
    y = lax.rem(lax.axis_index("tp") + offset[1], tp_count)
    return z * tp_count + y


def route(offset, back):
    segments, seq_count, tp_count = (lax.axis_size(a) for a in AXES)
    hops = []
    for s in range(segments):
        for z in range(seq_count):
            for y in range(tp_count):
                source = (s * seq_count + z) * tp_count + y
                s_to = (s + 1) % segments
                z_to = (z + offset[0]) % seq_count
                y_to = (y + offset[1]) % tp_count
                target = (s_to * seq_count + z_to) * tp_count + y_to
                hops.append((target, source) if back else (source, target))
    return hops


def params(enc_len):
    return pltpu.CompilerParams(vmem_limit_bytes=(12 + enc_len * 36 // 4096) * MIB)


def pack(pairs, order, heads):
    _, rows, _, width = pairs.shape
    local = heads * HEAD

    def kernel(pairs_ref, *outs):
        @pl.loop(0, rows // 16)
        def _(r):
            here = pl.ds(pl.multiple_of(r * 16, 16), 16)
            for out, offset in zip(outs, order):
                base = group_at(offset) * local
                for h in range(heads):
                    column = pl.multiple_of(base + h * HEAD, HEAD)
                    out[h, here] = pairs_ref[0, here, :, pl.ds(column, HEAD)]

    return pl.pallas_call(
        kernel,
        out_shape=[jax.ShapeDtypeStruct((heads, rows, 2, HEAD), pairs.dtype)] * len(order),
        in_specs=[VMEM],
        out_specs=[VMEM] * len(order),
        compiler_params=pltpu.CompilerParams(vmem_limit_bytes=24 * MIB),
        name="pack",
    )(pairs)


def unpack(blocks, order, width):
    heads, rows, _, _ = blocks[0].shape
    local = heads * HEAD
    parts = 4 if rows % 64 == 0 else 1
    size = rows // parts

    def kernel(*refs):
        ins, out, held, sem = refs[: len(order)], refs[len(order)], refs[-2], refs[-1]

        def store(r):
            here = pl.ds(pl.multiple_of(r * size, size), size)
            return pltpu.make_async_copy(held.at[here], out.at[0, here], sem.at[r])

        @pl.loop(0, parts)
        def _(r):
            here = pl.ds(pl.multiple_of(r * size, size), size)
            for block, offset in zip(ins, order):
                base = group_at(offset) * local
                for h in range(heads):
                    column = pl.multiple_of(base + h * HEAD, HEAD)
                    held[here, :, pl.ds(column, HEAD)] = block[h, here]
            store(r).start()

        for r in range(parts):
            store(r).wait()

    return pl.pallas_call(
        kernel,
        out_shape=jax.ShapeDtypeStruct((1, rows, 2, width), blocks[0].dtype),
        in_specs=[VMEM] * len(order),
        out_specs=HBM,
        scratch_shapes=[
            pltpu.VMEM((rows, 2, width), blocks[0].dtype),
            pltpu.SemaphoreType.DMA((parts,)),
        ],
        compiler_params=pltpu.CompilerParams(vmem_limit_bytes=24 * MIB),
        name="unpack",
    )(*blocks)


def turned(rows):
    _, tokens, local = rows.shape
    heads = local // HEAD
    tile = 256 if tokens % 256 == 0 else tokens

    def kernel(rows_ref, out_ref):
        for h in range(heads):
            for j in range(tokens // tile):
                here = slice(j * tile, (j + 1) * tile)
                block = rows_ref[0, here, h * HEAD : (h + 1) * HEAD]
                out_ref[h, :, here] = block.astype(jnp.float32).T.astype(rows.dtype)

    return pl.pallas_call(
        kernel,
        out_shape=jax.ShapeDtypeStruct((heads, HEAD, tokens), rows.dtype),
        in_specs=[VMEM],
        out_specs=VMEM,
        compiler_params=pltpu.CompilerParams(vmem_limit_bytes=16 * MIB),
        name="turned",
    )(rows)


def tiles(count):
    def run(body):
        if count <= 2:
            for j in range(count):
                body(j)
        else:
            pl.loop(0, count)(body)

    return run


def tokens_of(j, tile):
    return pl.ds(j * tile if isinstance(j, int) else pl.multiple_of(j * tile, tile), tile)


def tile_of(rows, tokens):
    for parts in range(1, tokens // 256 + 1):
        if tokens % (256 * parts) == 0 and rows * (tokens // parts) * 4 <= 5 * MIB // 4:
            return tokens // parts
    return 256 if tokens % 256 == 0 else tokens


def dot(a, b, contract=((1,), (0,))):
    return lax.dot_general(a, b, (contract, ((), ())), preferred_element_type=jnp.float32)


def shuffle(rows, join):
    to = lax.broadcasted_iota(jnp.int32, (2 * rows, 2 * rows), 1 if join else 0)
    source = lax.broadcasted_iota(jnp.int32, (2 * rows, 2 * rows), 0 if join else 1)
    wanted = jnp.where(to < rows, 2 * to, 2 * (to - rows) + 1)
    return jnp.where(source == wanted, 1.0, 0.0).astype(jnp.bfloat16)


def split_chunks(chunks, h, rows, k_ref=None, v_ref=None, kt_ref=None, vt_ref=None):
    split = shuffle(rows, False)
    for i, chunk in enumerate(chunks):
        both = dot(split, chunk[h])
        here = slice(i * rows, (i + 1) * rows)
        keys, values = both[:rows], both[rows:]
        if k_ref is not None:
            k_ref[h, here, :] = keys.astype(jnp.bfloat16)
        if v_ref is not None:
            v_ref[h, here, :] = values.astype(jnp.bfloat16)
        if kt_ref is not None:
            kt_ref[h, :, here] = keys.T.astype(jnp.bfloat16)
        if vt_ref is not None:
            vt_ref[h, :HEAD, here] = values.T.astype(jnp.bfloat16)
    if vt_ref is not None:
        tail = (vt_ref.shape[1] - HEAD, vt_ref.shape[2])
        vt_ref[h, HEAD:, :] = jnp.ones(tail, jnp.bfloat16)


def join_chunks(outs, h, rows, gk_ref, gv_ref):
    join = shuffle(rows, True)
    for i, out in enumerate(outs):
        here = slice(i * rows, (i + 1) * rows)
        both = jnp.concatenate([gk_ref[h, here, :] * FACTOR, gv_ref[h, here, :]], axis=0)
        out[h] = dot(join, both.astype(jnp.bfloat16)).astype(jnp.bfloat16)


def raise_scores(keys, qt, values_t, before):
    scores = dot(keys, qt)
    top = jnp.max(scores, axis=0, keepdims=True)
    if before is not None:
        top = jnp.maximum(top, before[0])
    raised = jnp.exp2((scores - top) * EXPONENT)
    low = raised.astype(jnp.bfloat16)
    summed = dot(values_t, low)
    total, context = summed[HEAD : HEAD + 1], summed[:HEAD]
    if before is not None:
        shrink = jnp.exp2((before[0] - top) * EXPONENT)
        total = total + before[1] * shrink
        context = context + before[2] * shrink
    return raised, low, top, total, context


def forward_kernel(count, first, tile, *refs):
    chunks, refs = refs[:count], refs[count:]
    qt_ref, refs = refs[0], refs[1:]
    if not first:
        stats_in, context_in, refs = refs[0], refs[1], refs[2:]
    stats_ref, context_ref, low_ref, k_ref, vt_ref = refs
    heads, pair_rows, _ = chunks[0].shape
    for h in range(heads):
        split_chunks(chunks, h, pair_rows // 2, k_ref=k_ref, vt_ref=vt_ref)

    @tiles(qt_ref.shape[2] // tile)
    def _(j):
        here = tokens_of(j, tile)
        for h in range(heads):
            before = None
            if not first:
                before = (stats_in[h, 0:1, here], stats_in[h, 1:2, here], context_in[h, :, here])
            _, low, top, total, context = raise_scores(
                k_ref[h], qt_ref[h, :, here], vt_ref[h], before
            )
            low_ref[h, :, here] = low
            stats_ref[h, 0:1, here] = top
            stats_ref[h, 1:2, here] = total
            context_ref[h, :, here] = context


def gradients(raised, scale, row_dot, rows, gt, refs, h):
    v_ref, kt_ref, gk_ref, gv_ref = refs
    query_rows, grad_rows = rows
    weights = raised * scale
    grad_weights = dot(v_ref[h], gt)
    grad_scores = (weights * (grad_weights - row_dot)).astype(jnp.bfloat16)
    gv_ref[h] += dot(weights.astype(jnp.bfloat16), grad_rows)
    gk_ref[h] += dot(grad_scores, query_rows)
    return dot(kt_ref[h], grad_scores) * FACTOR


def turn_kernel(count, tile, *refs):
    chunks, refs = refs[:count], refs[count:]
    q_ref, g_ref, qt_ref, gt_ref, stats_in, context_in = refs[:6]
    stats_ref, context_ref, grad_q_ref = refs[6:9]
    outs, refs = refs[9 : 9 + count], refs[9 + count :]
    k_ref, vt_ref, v_ref, kt_ref, gk_ref, gv_ref = refs
    heads, pair_rows, _ = chunks[0].shape
    rows = pair_rows // 2
    for h in range(heads):
        split_chunks(chunks, h, rows, k_ref, v_ref, kt_ref, vt_ref)
    gk_ref[...] = jnp.zeros_like(gk_ref)
    gv_ref[...] = jnp.zeros_like(gv_ref)

    @tiles(qt_ref.shape[2] // tile)
    def _(j):
        here = tokens_of(j, tile)
        for h in range(heads):
            qt, gt = qt_ref[h, :, here], gt_ref[h, :, here]
            before = (stats_in[h, 0:1, here], stats_in[h, 1:2, here], context_in[h, :, here])
            raised, _, top, total, context = raise_scores(k_ref[h], qt, vt_ref[h], before)
            columns = slice(h * HEAD, (h + 1) * HEAD)
            rows_here = q_ref[0, here, columns], g_ref[0, here, columns]
            scale = 1.0 / total
            context = context * scale
            row_dot = jnp.sum(gt.astype(jnp.float32) * context, axis=0, keepdims=True)
            context_ref[h, :, here] = context
            stats_ref[h, 0:1, here] = top
            stats_ref[h, 1:2, here] = scale
            stats_ref[h, 2:3, here] = row_dot
            grad_q_ref[h, :, here] = gradients(
                raised, scale, row_dot, rows_here, gt, (v_ref, kt_ref, gk_ref, gv_ref), h
            )

    for h in range(heads):
        join_chunks(outs, h, rows, gk_ref, gv_ref)


def backward_kernel(back, counts, ready, last, tile, *refs):
    refs = refs[back:]
    groups = []
    for count in counts:
        groups.append((refs[:count], refs[count], refs[count + 1]))
        refs = refs[count + 2 :]
    q_ref, g_ref, gt_ref, stats_ref, grad_q_in = refs[:5]
    refs = refs[5:]
    if ready:
        ready_ref, refs = refs[0], refs[1:]
    if ready or last:
        rows_ref, refs = refs[0], refs[1:]
    if not last:
        grad_q_ref, refs = refs[0], refs[1:]
    outs, refs = refs[: sum(counts)], refs[sum(counts) :]
    scratch = [refs[i : i + 4] for i in range(0, len(refs), 4)]
    heads, pair_rows, _ = groups[0][0][0].shape
    rows = pair_rows // 2
    for (chunks, _, _), (v_ref, kt_ref, gk_ref, gv_ref) in zip(groups, scratch):
        for h in range(heads):
            split_chunks(chunks, h, rows, v_ref=v_ref, kt_ref=kt_ref)
        gk_ref[...] = jnp.zeros_like(gk_ref)
        gv_ref[...] = jnp.zeros_like(gv_ref)

    @tiles(gt_ref.shape[2] // tile)
    def _(j):
        here = tokens_of(j, tile)
        for h in range(heads):
            columns = slice(h * HEAD, (h + 1) * HEAD)
            rows_here = q_ref[0, here, columns], g_ref[0, here, columns]
            gt = gt_ref[h, :, here]
            top, scale, row_dot = (stats_ref[h, i : i + 1, here] for i in range(3))
            grad_q = grad_q_in[h, :, here]
            for (_, low_ref, then_ref), own in zip(groups, scratch):
                shrunk = jnp.exp2((then_ref[h, 0:1, here] - top) * EXPONENT)
                raised = low_ref[h, :, here].astype(jnp.float32)
                grad_q = grad_q + gradients(
                    raised, scale * shrunk, row_dot, rows_here, gt, own, h
                )
            if not last:
                grad_q_ref[h, :, here] = grad_q
            if ready:
                grad_q = ready_ref[h, :, here]
            if ready or last:
                rows_ref[0, here, columns] = grad_q.T.astype(rows_ref.dtype)

    for count, (_, _, gk_ref, gv_ref) in zip(counts, scratch):
        for h in range(heads):
            join_chunks(outs[:count], h, rows, gk_ref, gv_ref)
        outs = outs[count:]


def cost(heads, rows, tokens, matmuls):
    return pl.CostEstimate(
        flops=2 * matmuls * heads * rows * tokens * HEAD,
        bytes_accessed=heads * (rows + tokens) * HEAD * 8,
        transcendentals=heads * rows * tokens,
    )


def attend(groups, queries, upstream, send_back):
    heads, pair_rows, _ = groups[0][0].shape
    rows = pair_rows // 2
    enc_len = sum(len(g) for g in groups) * rows
    tokens = queries.shape[1]
    qt, gt = turned(queries), turned(upstream)
    stats_shape = jax.ShapeDtypeStruct((heads, 8, tokens), jnp.float32)
    wide_shape = jax.ShapeDtypeStruct((heads, HEAD, tokens), jnp.float32)
    rows_shape = jax.ShapeDtypeStruct(queries.shape, queries.dtype)
    compiler_params = params(enc_len)

    def natural(count):
        return pltpu.VMEM((heads, count * rows, HEAD), jnp.bfloat16)

    def across(count, extra=0):
        return pltpu.VMEM((heads, HEAD + extra, count * rows), jnp.bfloat16)

    def sums(count):
        return pltpu.VMEM((heads, count * rows, HEAD), jnp.float32)

    def shapes_of(group):
        return [jax.ShapeDtypeStruct(c.shape, c.dtype) for c in group]

    state, kept = [], []
    for group in groups[:-1]:
        count = len(group)
        low_shape = jax.ShapeDtypeStruct((heads, count * rows, tokens), jnp.bfloat16)
        stats, context, low = pl.pallas_call(
            functools.partial(forward_kernel, count, not state, tile_of(count * rows, tokens)),
            out_shape=[stats_shape, wide_shape, low_shape],
            in_specs=[VMEM] * (count + 1 + len(state)),
            out_specs=[VMEM] * 3,
            scratch_shapes=[natural(count), across(count, 16)],
            compiler_params=compiler_params,
            cost_estimate=cost(heads, count * rows, tokens, 2),
            name="forward",
        )(*group, qt, *state)
        state = [stats, context]
        kept.append((low, stats))

    group, count = groups[-1], len(groups[-1])
    final, context, grad_q, *grads = pl.pallas_call(
        functools.partial(turn_kernel, count, tile_of(count * rows, tokens)),
        out_shape=[stats_shape, wide_shape, wide_shape] + shapes_of(group),
        in_specs=[VMEM] * (count + 6),
        out_specs=[VMEM] * (count + 3),
        scratch_shapes=[natural(count), across(count, 16), natural(count), across(count)]
        + [sums(count)] * 2,
        compiler_params=compiler_params,
        cost_estimate=cost(heads, count * rows, tokens, 6),
        name="turn",
    )(*group, queries, upstream, qt, gt, *state)
    returned = [send_back(len(groups) - 1, grads)]

    for i in reversed(range(len(groups) - 1)):
        part, ready, last = [i], i == 1, i == 0
        counts = [len(groups[k]) for k in part]
        back = returned[1] + returned[0] if last else []
        operands = []
        for k in part:
            operands += [*groups[k], *kept[k]]
        operands += [queries, upstream, gt, final, grad_q, *([context] if ready else [])]
        shapes = [rows_shape] * (ready or last) + [wide_shape] * (not last)
        outs = pl.pallas_call(
            functools.partial(
                backward_kernel,
                len(back),
                counts,
                ready,
                last,
                tile_of(max(counts) * rows, tokens),
            ),
            out_shape=shapes + shapes_of(sum((groups[k] for k in part), [])),
            in_specs=[ANY] * len(back) + [VMEM] * len(operands),
            out_specs=[VMEM] * (len(shapes) + sum(counts)),
            scratch_shapes=[
                shape
                for count in counts
                for shape in (natural(count), across(count), sums(count), sums(count))
            ],
            compiler_params=compiler_params,
            cost_estimate=cost(heads, sum(counts) * rows, tokens, 4),
            name="backward",
        )(*back, *operands)
        if ready:
            context_rows = outs[0]
        if last:
            grad_query = outs[0]
        else:
            grad_q = outs[len(shapes) - 1]
        blocks = list(outs[len(shapes) :])
        for k in part:
            returned.append(send_back(k, blocks[: len(groups[k])]))
            blocks = blocks[len(groups[k]) :]
    return context_rows, grad_query


def shards(pairs, queries, upstream):
    _, rows, _, width = pairs.shape
    heads = queries.shape[2] // HEAD
    offsets = offset_groups()
    order = sum(offsets, [])
    blocks = []
    for offset, block in zip(order, pack(pairs, order, heads)):
        block = block.reshape(heads, 2 * rows, HEAD)
        blocks.append(lax.ppermute(block, AXES, route(offset, False)))
    groups = []
    for group in offsets:
        groups.append(blocks[: len(group)])
        blocks = blocks[len(group) :]
    homes, returned = [], []

    def send_back(i, grads):
        back = [lax.ppermute(g, AXES, route(o, True)) for o, g in zip(offsets[i], grads)]
        homes.extend(offsets[i])
        returned.extend(b.reshape(heads, rows, 2, HEAD) for b in back)
        return back

    context, grad_query = attend(groups, queries, upstream, send_back)
    return context, grad_query, unpack(returned, homes, width)


def solution(mesh):
    return jax.shard_map(
        shards,
        mesh=mesh,
        in_specs=(
            P("segment", ("seq", "tp"), None, None),
            P("segment", None, ("seq", "tp")),
            P("segment", None, ("seq", "tp")),
        ),
        out_specs=(
            P("segment", None, ("seq", "tp")),
            P("segment", None, ("seq", "tp")),
            P("segment", ("seq", "tp"), None, None),
        ),
        check_vma=False,
    )
```

```python
import functools

import jax
import jax.numpy as jnp
from jax import lax
from jax.experimental import pallas as pl
from jax.experimental.pallas import tpu as pltpu
from jax.sharding import PartitionSpec as P

HEAD = 128
AXES = ("segment", "seq", "tp")
FACTOR = HEAD**-0.5
EXPONENT = FACTOR * 1.4426950408889634
MIB = 1 << 20
ANY = pl.BlockSpec(memory_space=pl.ANY)
HBM = pl.BlockSpec(memory_space=pltpu.HBM)
VMEM = pl.BlockSpec(memory_space=pltpu.VMEM)


def offset_groups():
    seq_count = lax.axis_size("seq")
    tp_count = lax.axis_size("tp")
    near = [(0, dy) for dy in reversed(range(tp_count))]
    far = [(dz, dy) for dy in reversed(range(tp_count)) for dz in range(1, seq_count)]
    far.sort(key=lambda o: -abs(o[0] - seq_count / 2))
    eighth = max(1, (len(near) + len(far)) // 8)
    short, long = far[: -2 * eighth], far[-2 * eighth :]
    short.sort(key=lambda o: -o[1])
    half = len(short) // 2
    return [
        short[:1] + near[:1] + short[1:half],
        short[half:] + near[1:],
        long[:eighth],
        long[eighth:],
    ]


def group_at(offset):
    seq_count = lax.axis_size("seq")
    tp_count = lax.axis_size("tp")
    z = lax.rem(lax.axis_index("seq") + offset[0], seq_count)
    y = lax.rem(lax.axis_index("tp") + offset[1], tp_count)
    return z * tp_count + y


def route(offset, back):
    segments, seq_count, tp_count = (lax.axis_size(a) for a in AXES)
    hops = []
    for s in range(segments):
        for z in range(seq_count):
            for y in range(tp_count):
                source = (s * seq_count + z) * tp_count + y
                s_to = (s + 1) % segments
                z_to = (z + offset[0]) % seq_count
                y_to = (y + offset[1]) % tp_count
                target = (s_to * seq_count + z_to) * tp_count + y_to
                hops.append((target, source) if back else (source, target))
    return hops


def params(enc_len):
    return pltpu.CompilerParams(vmem_limit_bytes=(12 + enc_len * 36 // 4096) * MIB)


def pack(pairs, order, heads):
    _, rows, _, width = pairs.shape
    local = heads * HEAD

    def kernel(pairs_ref, *outs):
        @pl.loop(0, rows // 16)
        def _(r):
            here = pl.ds(pl.multiple_of(r * 16, 16), 16)
            for out, offset in zip(outs, order):
                base = group_at(offset) * local
                for h in range(heads):
                    column = pl.multiple_of(base + h * HEAD, HEAD)
                    out[h, here] = pairs_ref[0, here, :, pl.ds(column, HEAD)]

    return pl.pallas_call(
        kernel,
        out_shape=[jax.ShapeDtypeStruct((heads, rows, 2, HEAD), pairs.dtype)] * len(order),
        in_specs=[VMEM],
        out_specs=[VMEM] * len(order),
        compiler_params=pltpu.CompilerParams(vmem_limit_bytes=24 * MIB),
        name="pack",
    )(pairs)


def unpack(blocks, order, width):
    heads, rows, _, _ = blocks[0].shape
    local = heads * HEAD
    parts = 4 if rows % 64 == 0 else 1
    size = rows // parts

    def kernel(*refs):
        ins, out, held, sem = refs[: len(order)], refs[len(order)], refs[-2], refs[-1]

        def store(r):
            here = pl.ds(pl.multiple_of(r * size, size), size)
            return pltpu.make_async_copy(held.at[here], out.at[0, here], sem.at[r])

        @pl.loop(0, parts)
        def _(r):
            here = pl.ds(pl.multiple_of(r * size, size), size)
            for block, offset in zip(ins, order):
                base = group_at(offset) * local
                for h in range(heads):
                    column = pl.multiple_of(base + h * HEAD, HEAD)
                    held[here, :, pl.ds(column, HEAD)] = block[h, here]
            store(r).start()

        for r in range(parts):
            store(r).wait()

    return pl.pallas_call(
        kernel,
        out_shape=jax.ShapeDtypeStruct((1, rows, 2, width), blocks[0].dtype),
        in_specs=[VMEM] * len(order),
        out_specs=HBM,
        scratch_shapes=[
            pltpu.VMEM((rows, 2, width), blocks[0].dtype),
            pltpu.SemaphoreType.DMA((parts,)),
        ],
        compiler_params=pltpu.CompilerParams(vmem_limit_bytes=24 * MIB),
        name="unpack",
    )(*blocks)


def turned(rows):
    _, tokens, local = rows.shape
    heads = local // HEAD
    tile = 256 if tokens % 256 == 0 else tokens

    def kernel(rows_ref, out_ref):
        for h in range(heads):
            for j in range(tokens // tile):
                here = slice(j * tile, (j + 1) * tile)
                block = rows_ref[0, here, h * HEAD : (h + 1) * HEAD]
                out_ref[h, :, here] = block.astype(jnp.float32).T.astype(rows.dtype)

    return pl.pallas_call(
        kernel,
        out_shape=jax.ShapeDtypeStruct((heads, HEAD, tokens), rows.dtype),
        in_specs=[VMEM],
        out_specs=VMEM,
        compiler_params=pltpu.CompilerParams(vmem_limit_bytes=16 * MIB),
        name="turned",
    )(rows)


def tiles(count):
    def run(body):
        if count <= 2:
            for j in range(count):
                body(j)
        else:
            pl.loop(0, count)(body)

    return run


def tokens_of(j, tile):
    return pl.ds(j * tile if isinstance(j, int) else pl.multiple_of(j * tile, tile), tile)


def tile_of(rows, tokens):
    for parts in range(1, tokens // 256 + 1):
        if tokens % (256 * parts) == 0 and rows * (tokens // parts) * 4 <= 5 * MIB // 4:
            return tokens // parts
    return 256 if tokens % 256 == 0 else tokens


def dot(a, b, contract=((1,), (0,))):
    return lax.dot_general(a, b, (contract, ((), ())), preferred_element_type=jnp.float32)


def shuffle(rows, join):
    to = lax.broadcasted_iota(jnp.int32, (2 * rows, 2 * rows), 1 if join else 0)
    source = lax.broadcasted_iota(jnp.int32, (2 * rows, 2 * rows), 0 if join else 1)
    wanted = jnp.where(to < rows, 2 * to, 2 * (to - rows) + 1)
    return jnp.where(source == wanted, 1.0, 0.0).astype(jnp.bfloat16)


def split_chunks(chunks, h, rows, k_ref=None, v_ref=None, kt_ref=None, vt_ref=None):
    split = shuffle(rows, False)
    for i, chunk in enumerate(chunks):
        both = dot(split, chunk[h])
        here = slice(i * rows, (i + 1) * rows)
        keys, values = both[:rows], both[rows:]
        if k_ref is not None:
            k_ref[h, here, :] = keys.astype(jnp.bfloat16)
        if v_ref is not None:
            v_ref[h, here, :] = values.astype(jnp.bfloat16)
        if kt_ref is not None:
            kt_ref[h, :, here] = keys.T.astype(jnp.bfloat16)
        if vt_ref is not None:
            vt_ref[h, :HEAD, here] = values.T.astype(jnp.bfloat16)
    if vt_ref is not None:
        tail = (vt_ref.shape[1] - HEAD, vt_ref.shape[2])
        vt_ref[h, HEAD:, :] = jnp.ones(tail, jnp.bfloat16)


def join_chunks(outs, h, rows, gk_ref, gv_ref):
    join = shuffle(rows, True)
    for i, out in enumerate(outs):
        here = slice(i * rows, (i + 1) * rows)
        both = jnp.concatenate([gk_ref[h, here, :] * FACTOR, gv_ref[h, here, :]], axis=0)
        out[h] = dot(join, both.astype(jnp.bfloat16)).astype(jnp.bfloat16)


def raise_scores(keys, qt, values_t, before):
    scores = dot(keys, qt)
    top = jnp.max(scores, axis=0, keepdims=True)
    if before is not None:
        top = jnp.maximum(top, before[0])
    raised = jnp.exp2((scores - top) * EXPONENT)
    low = raised.astype(jnp.bfloat16)
    summed = dot(values_t, low)
    total, context = summed[HEAD : HEAD + 1], summed[:HEAD]
    if before is not None:
        shrink = jnp.exp2((before[0] - top) * EXPONENT)
        total = total + before[1] * shrink
        context = context + before[2] * shrink
    return raised, low, top, total, context


def forward_kernel(count, first, tile, *refs):
    chunks, refs = refs[:count], refs[count:]
    qt_ref, refs = refs[0], refs[1:]
    if not first:
        stats_in, context_in, refs = refs[0], refs[1], refs[2:]
    stats_ref, context_ref, low_ref, k_ref, vt_ref = refs
    heads, pair_rows, _ = chunks[0].shape
    for h in range(heads):
        split_chunks(chunks, h, pair_rows // 2, k_ref=k_ref, vt_ref=vt_ref)

    @tiles(qt_ref.shape[2] // tile)
    def _(j):
        here = tokens_of(j, tile)
        for h in range(heads):
            before = None
            if not first:
                before = (stats_in[h, 0:1, here], stats_in[h, 1:2, here], context_in[h, :, here])
            _, low, top, total, context = raise_scores(
                k_ref[h], qt_ref[h, :, here], vt_ref[h], before
            )
            low_ref[h, :, here] = low
            stats_ref[h, 0:1, here] = top
            stats_ref[h, 1:2, here] = total
            context_ref[h, :, here] = context


def gradients(raised, scale, row_dot, rows, gt, refs, h):
    v_ref, kt_ref, gk_ref, gv_ref = refs
    query_rows, grad_rows = rows
    weights = raised * scale
    grad_weights = dot(v_ref[h], gt)
    grad_scores = (weights * (grad_weights - row_dot)).astype(jnp.bfloat16)
    gv_ref[h] += dot(weights.astype(jnp.bfloat16), grad_rows)
    gk_ref[h] += dot(grad_scores, query_rows)
    return dot(kt_ref[h], grad_scores) * FACTOR


def turn_kernel(count, tile, *refs):
    chunks, refs = refs[:count], refs[count:]
    q_ref, g_ref, qt_ref, gt_ref, stats_in, context_in = refs[:6]
    stats_ref, context_ref, grad_q_ref = refs[6:9]
    outs, refs = refs[9 : 9 + count], refs[9 + count :]
    k_ref, vt_ref, v_ref, kt_ref, gk_ref, gv_ref = refs
    heads, pair_rows, _ = chunks[0].shape
    rows = pair_rows // 2
    for h in range(heads):
        split_chunks(chunks, h, rows, k_ref, v_ref, kt_ref, vt_ref)
    gk_ref[...] = jnp.zeros_like(gk_ref)
    gv_ref[...] = jnp.zeros_like(gv_ref)

    @tiles(qt_ref.shape[2] // tile)
    def _(j):
        here = tokens_of(j, tile)
        for h in range(heads):
            qt, gt = qt_ref[h, :, here], gt_ref[h, :, here]
            before = (stats_in[h, 0:1, here], stats_in[h, 1:2, here], context_in[h, :, here])
            raised, _, top, total, context = raise_scores(k_ref[h], qt, vt_ref[h], before)
            columns = slice(h * HEAD, (h + 1) * HEAD)
            rows_here = q_ref[0, here, columns], g_ref[0, here, columns]
            scale = 1.0 / total
            context = context * scale
            row_dot = jnp.sum(gt.astype(jnp.float32) * context, axis=0, keepdims=True)
            context_ref[h, :, here] = context
            stats_ref[h, 0:1, here] = top
            stats_ref[h, 1:2, here] = scale
            stats_ref[h, 2:3, here] = row_dot
            grad_q_ref[h, :, here] = gradients(
                raised, scale, row_dot, rows_here, gt, (v_ref, kt_ref, gk_ref, gv_ref), h
            )

    for h in range(heads):
        join_chunks(outs, h, rows, gk_ref, gv_ref)


def backward_kernel(back, counts, first, tile, *refs):
    refs = refs[back:]
    groups = []
    for count in counts:
        groups.append((refs[:count], refs[count], refs[count + 1]))
        refs = refs[count + 2 :]
    q_ref, g_ref, gt_ref, stats_ref, grad_q_in = refs[:5]
    if first:
        ready_ref, rows_ref, grad_q_ref, refs = refs[5], refs[6], refs[7], refs[8:]
    else:
        rows_ref, refs = refs[5], refs[6:]
    outs, refs = refs[: sum(counts)], refs[sum(counts) :]
    scratch = [refs[i : i + 4] for i in range(0, len(refs), 4)]
    heads, pair_rows, _ = groups[0][0][0].shape
    rows = pair_rows // 2
    for (chunks, _, _), (v_ref, kt_ref, gk_ref, gv_ref) in zip(groups, scratch):
        for h in range(heads):
            split_chunks(chunks, h, rows, v_ref=v_ref, kt_ref=kt_ref)
        gk_ref[...] = jnp.zeros_like(gk_ref)
        gv_ref[...] = jnp.zeros_like(gv_ref)

    @tiles(gt_ref.shape[2] // tile)
    def _(j):
        here = tokens_of(j, tile)
        for h in range(heads):
            columns = slice(h * HEAD, (h + 1) * HEAD)
            rows_here = q_ref[0, here, columns], g_ref[0, here, columns]
            gt = gt_ref[h, :, here]
            top, scale, row_dot = (stats_ref[h, i : i + 1, here] for i in range(3))
            grad_q = grad_q_in[h, :, here]
            for (_, low_ref, then_ref), own in zip(groups, scratch):
                shrunk = jnp.exp2((then_ref[h, 0:1, here] - top) * EXPONENT)
                raised = low_ref[h, :, here].astype(jnp.float32)
                grad_q = grad_q + gradients(
                    raised, scale * shrunk, row_dot, rows_here, gt, own, h
                )
            if first:
                grad_q_ref[h, :, here] = grad_q
                grad_q = ready_ref[h, :, here]
            rows_ref[0, here, columns] = grad_q.T.astype(rows_ref.dtype)

    for count, (_, _, gk_ref, gv_ref) in zip(counts, scratch):
        for h in range(heads):
            join_chunks(outs[:count], h, rows, gk_ref, gv_ref)
        outs = outs[count:]


def cost(heads, rows, tokens, matmuls):
    return pl.CostEstimate(
        flops=2 * matmuls * heads * rows * tokens * HEAD,
        bytes_accessed=heads * (rows + tokens) * HEAD * 8,
        transcendentals=heads * rows * tokens,
    )


def attend(groups, queries, upstream, send_back):
    heads, pair_rows, _ = groups[0][0].shape
    rows = pair_rows // 2
    enc_len = sum(len(g) for g in groups) * rows
    tokens = queries.shape[1]
    qt, gt = turned(queries), turned(upstream)
    stats_shape = jax.ShapeDtypeStruct((heads, 8, tokens), jnp.float32)
    wide_shape = jax.ShapeDtypeStruct((heads, HEAD, tokens), jnp.float32)
    rows_shape = jax.ShapeDtypeStruct(queries.shape, queries.dtype)
    compiler_params = params(enc_len)

    def natural(count):
        return pltpu.VMEM((heads, count * rows, HEAD), jnp.bfloat16)

    def across(count, extra=0):
        return pltpu.VMEM((heads, HEAD + extra, count * rows), jnp.bfloat16)

    def sums(count):
        return pltpu.VMEM((heads, count * rows, HEAD), jnp.float32)

    def shapes_of(group):
        return [jax.ShapeDtypeStruct(c.shape, c.dtype) for c in group]

    state, kept = [], []
    for group in groups[:-1]:
        count = len(group)
        low_shape = jax.ShapeDtypeStruct((heads, count * rows, tokens), jnp.bfloat16)
        stats, context, low = pl.pallas_call(
            functools.partial(forward_kernel, count, not state, tile_of(count * rows, tokens)),
            out_shape=[stats_shape, wide_shape, low_shape],
            in_specs=[VMEM] * (count + 1 + len(state)),
            out_specs=[VMEM] * 3,
            scratch_shapes=[natural(count), across(count, 16)],
            compiler_params=compiler_params,
            cost_estimate=cost(heads, count * rows, tokens, 2),
            name="forward",
        )(*group, qt, *state)
        state = [stats, context]
        kept.append((low, stats))

    group, count = groups[-1], len(groups[-1])
    final, context, grad_q, *grads = pl.pallas_call(
        functools.partial(turn_kernel, count, tile_of(count * rows, tokens)),
        out_shape=[stats_shape, wide_shape, wide_shape] + shapes_of(group),
        in_specs=[VMEM] * (count + 6),
        out_specs=[VMEM] * (count + 3),
        scratch_shapes=[natural(count), across(count, 16), natural(count), across(count)]
        + [sums(count)] * 2,
        compiler_params=compiler_params,
        cost_estimate=cost(heads, count * rows, tokens, 6),
        name="turn",
    )(*group, queries, upstream, qt, gt, *state)
    returned = [send_back(len(groups) - 1, grads)]

    for part in (list(range(len(groups) - 2, 0, -1)), [0]):
        first = part != [0]
        counts = [len(groups[i]) for i in part]
        back = [] if first else returned[0]
        operands = []
        for i in part:
            operands += [*groups[i], *kept[i]]
        operands += [queries, upstream, gt, final, grad_q, *([context] if first else [])]
        shapes = [rows_shape, wide_shape] if first else [rows_shape]
        outs = pl.pallas_call(
            functools.partial(
                backward_kernel, len(back), counts, first, tile_of(max(counts) * rows, tokens)
            ),
            out_shape=shapes + shapes_of(sum((groups[i] for i in part), [])),
            in_specs=[ANY] * len(back) + [VMEM] * len(operands),
            out_specs=[VMEM] * (len(shapes) + sum(counts)),
            scratch_shapes=[
                shape
                for count in counts
                for shape in (natural(count), across(count), sums(count), sums(count))
            ],
            compiler_params=compiler_params,
            cost_estimate=cost(heads, sum(counts) * rows, tokens, 4),
            name="backward",
        )(*back, *operands)
        if first:
            context_rows, grad_q = outs[:2]
        else:
            grad_query = outs[0]
        blocks = list(outs[len(shapes) :])
        for i in part:
            returned.append(send_back(i, blocks[: len(groups[i])]))
            blocks = blocks[len(groups[i]) :]
    return context_rows, grad_query


def shards(pairs, queries, upstream):
    _, rows, _, width = pairs.shape
    heads = queries.shape[2] // HEAD
    offsets = offset_groups()
    order = sum(offsets, [])
    blocks = []
    for offset, block in zip(order, pack(pairs, order, heads)):
        block = block.reshape(heads, 2 * rows, HEAD)
        blocks.append(lax.ppermute(block, AXES, route(offset, False)))
    groups = []
    for group in offsets:
        groups.append(blocks[: len(group)])
        blocks = blocks[len(group) :]
    homes, returned = [], []

    def send_back(i, grads):
        back = [lax.ppermute(g, AXES, route(o, True)) for o, g in zip(offsets[i], grads)]
        homes.extend(offsets[i])
        returned.extend(b.reshape(heads, rows, 2, HEAD) for b in back)
        return back

    context, grad_query = attend(groups, queries, upstream, send_back)
    return context, grad_query, unpack(returned, homes, width)


def solution(mesh):
    return jax.shard_map(
        shards,
        mesh=mesh,
        in_specs=(
            P("segment", ("seq", "tp"), None, None),
            P("segment", None, ("seq", "tp")),
            P("segment", None, ("seq", "tp")),
        ),
        out_specs=(
            P("segment", None, ("seq", "tp")),
            P("segment", None, ("seq", "tp")),
            P("segment", ("seq", "tp"), None, None),
        ),
        check_vma=False,
    )
```

```python
import functools

import jax
import jax.numpy as jnp
from jax import lax
from jax.experimental import pallas as pl
from jax.experimental.pallas import tpu as pltpu
from jax.sharding import PartitionSpec as P

HEAD = 128
AXES = ("segment", "seq", "tp")
FACTOR = HEAD**-0.5
EXPONENT = FACTOR * 1.4426950408889634
MIB = 1 << 20
ANY = pl.BlockSpec(memory_space=pl.ANY)
HBM = pl.BlockSpec(memory_space=pltpu.HBM)
VMEM = pl.BlockSpec(memory_space=pltpu.VMEM)


def offset_groups():
    seq_count = lax.axis_size("seq")
    tp_count = lax.axis_size("tp")
    near = [(0, dy) for dy in reversed(range(tp_count))]
    far = [(dz, dy) for dy in reversed(range(tp_count)) for dz in range(1, seq_count)]
    far.sort(key=lambda o: -abs(o[0] - seq_count / 2))
    eighth = max(1, (len(near) + len(far)) // 8)
    short, long = far[: -2 * eighth], far[-2 * eighth :]
    short.sort(key=lambda o: -o[1])
    half = len(short) // 2
    return [
        short[:1] + near[:1] + short[1:half],
        short[half:] + near[1:],
        long[:eighth],
        long[eighth:],
    ]


def group_at(offset):
    seq_count = lax.axis_size("seq")
    tp_count = lax.axis_size("tp")
    z = lax.rem(lax.axis_index("seq") + offset[0], seq_count)
    y = lax.rem(lax.axis_index("tp") + offset[1], tp_count)
    return z * tp_count + y


def route(offset, back):
    segments, seq_count, tp_count = (lax.axis_size(a) for a in AXES)
    hops = []
    for s in range(segments):
        for z in range(seq_count):
            for y in range(tp_count):
                source = (s * seq_count + z) * tp_count + y
                s_to = (s + 1) % segments
                z_to = (z + offset[0]) % seq_count
                y_to = (y + offset[1]) % tp_count
                target = (s_to * seq_count + z_to) * tp_count + y_to
                hops.append((target, source) if back else (source, target))
    return hops


def params(enc_len):
    return pltpu.CompilerParams(vmem_limit_bytes=(12 + enc_len * 36 // 4096) * MIB)


def pack(pairs, order, heads):
    _, rows, _, width = pairs.shape
    local = heads * HEAD

    def kernel(pairs_ref, *outs):
        @pl.loop(0, rows // 16)
        def _(r):
            here = pl.ds(pl.multiple_of(r * 16, 16), 16)
            for out, offset in zip(outs, order):
                base = group_at(offset) * local
                for h in range(heads):
                    column = pl.multiple_of(base + h * HEAD, HEAD)
                    out[h, here] = pairs_ref[0, here, :, pl.ds(column, HEAD)]

    return pl.pallas_call(
        kernel,
        out_shape=[jax.ShapeDtypeStruct((heads, rows, 2, HEAD), pairs.dtype)] * len(order),
        in_specs=[VMEM],
        out_specs=[VMEM] * len(order),
        compiler_params=pltpu.CompilerParams(vmem_limit_bytes=24 * MIB),
        name="pack",
    )(pairs)


def unpack(blocks, order, width):
    heads, rows, _, _ = blocks[0].shape
    local = heads * HEAD
    parts = 4 if rows % 64 == 0 else 1
    size = rows // parts

    def kernel(*refs):
        ins, out, held, sem = refs[: len(order)], refs[len(order)], refs[-2], refs[-1]

        def store(r):
            here = pl.ds(pl.multiple_of(r * size, size), size)
            return pltpu.make_async_copy(held.at[here], out.at[0, here], sem.at[r])

        @pl.loop(0, parts)
        def _(r):
            here = pl.ds(pl.multiple_of(r * size, size), size)
            for block, offset in zip(ins, order):
                base = group_at(offset) * local
                for h in range(heads):
                    column = pl.multiple_of(base + h * HEAD, HEAD)
                    held[here, :, pl.ds(column, HEAD)] = block[h, here]
            store(r).start()

        for r in range(parts):
            store(r).wait()

    return pl.pallas_call(
        kernel,
        out_shape=jax.ShapeDtypeStruct((1, rows, 2, width), blocks[0].dtype),
        in_specs=[VMEM] * len(order),
        out_specs=HBM,
        scratch_shapes=[
            pltpu.VMEM((rows, 2, width), blocks[0].dtype),
            pltpu.SemaphoreType.DMA((parts,)),
        ],
        compiler_params=pltpu.CompilerParams(vmem_limit_bytes=24 * MIB),
        name="unpack",
    )(*blocks)


def turned(rows):
    _, tokens, local = rows.shape
    heads = local // HEAD
    tile = 256 if tokens % 256 == 0 else tokens

    def kernel(rows_ref, out_ref):
        for h in range(heads):
            for j in range(tokens // tile):
                here = slice(j * tile, (j + 1) * tile)
                block = rows_ref[0, here, h * HEAD : (h + 1) * HEAD]
                out_ref[h, :, here] = block.astype(jnp.float32).T.astype(rows.dtype)

    return pl.pallas_call(
        kernel,
        out_shape=jax.ShapeDtypeStruct((heads, HEAD, tokens), rows.dtype),
        in_specs=[VMEM],
        out_specs=VMEM,
        compiler_params=pltpu.CompilerParams(vmem_limit_bytes=16 * MIB),
        name="turned",
    )(rows)


def tiles(count):
    def run(body):
        if count <= 2:
            for j in range(count):
                body(j)
        else:
            pl.loop(0, count)(body)

    return run


def tokens_of(j, tile):
    return pl.ds(j * tile if isinstance(j, int) else pl.multiple_of(j * tile, tile), tile)


def tile_of(rows, tokens):
    for parts in range(1, tokens // 256 + 1):
        if tokens % (256 * parts) == 0 and rows * (tokens // parts) * 4 <= 5 * MIB // 4:
            return tokens // parts
    return 256 if tokens % 256 == 0 else tokens


def turned_back(columns, dtype):
    heads, _, tokens = columns.shape
    tile = 256 if tokens % 256 == 0 else tokens

    def kernel(columns_ref, out_ref):
        for h in range(heads):
            for j in range(tokens // tile):
                here = slice(j * tile, (j + 1) * tile)
                block = columns_ref[h, :, here].T.astype(dtype)
                out_ref[0, here, h * HEAD : (h + 1) * HEAD] = block

    return pl.pallas_call(
        kernel,
        out_shape=jax.ShapeDtypeStruct((1, tokens, heads * HEAD), dtype),
        in_specs=[VMEM],
        out_specs=VMEM,
        compiler_params=pltpu.CompilerParams(vmem_limit_bytes=16 * MIB),
        name="turned_back",
    )(columns)


def dot(a, b, contract=((1,), (0,))):
    return lax.dot_general(a, b, (contract, ((), ())), preferred_element_type=jnp.float32)


def shuffle(rows, join):
    to = lax.broadcasted_iota(jnp.int32, (2 * rows, 2 * rows), 1 if join else 0)
    source = lax.broadcasted_iota(jnp.int32, (2 * rows, 2 * rows), 0 if join else 1)
    wanted = jnp.where(to < rows, 2 * to, 2 * (to - rows) + 1)
    return jnp.where(source == wanted, 1.0, 0.0).astype(jnp.bfloat16)


def split_chunks(chunks, h, rows, k_ref=None, v_ref=None, kt_ref=None, vt_ref=None):
    split = shuffle(rows, False)
    for i, chunk in enumerate(chunks):
        both = dot(split, chunk[h])
        here = slice(i * rows, (i + 1) * rows)
        keys, values = both[:rows], both[rows:]
        if k_ref is not None:
            k_ref[h, here, :] = keys.astype(jnp.bfloat16)
        if v_ref is not None:
            v_ref[h, here, :] = values.astype(jnp.bfloat16)
        if kt_ref is not None:
            kt_ref[h, :, here] = keys.T.astype(jnp.bfloat16)
        if vt_ref is not None:
            vt_ref[h, :HEAD, here] = values.T.astype(jnp.bfloat16)
    if vt_ref is not None:
        tail = (vt_ref.shape[1] - HEAD, vt_ref.shape[2])
        vt_ref[h, HEAD:, :] = jnp.ones(tail, jnp.bfloat16)


def join_chunks(outs, h, rows, gk_ref, gv_ref):
    join = shuffle(rows, True)
    for i, out in enumerate(outs):
        here = slice(i * rows, (i + 1) * rows)
        both = jnp.concatenate([gk_ref[h, here, :] * FACTOR, gv_ref[h, here, :]], axis=0)
        out[h] = dot(join, both.astype(jnp.bfloat16)).astype(jnp.bfloat16)


def raise_scores(keys, qt, values_t, before):
    scores = dot(keys, qt)
    top = jnp.max(scores, axis=0, keepdims=True)
    if before is not None:
        top = jnp.maximum(top, before[0])
    raised = jnp.exp2((scores - top) * EXPONENT)
    low = raised.astype(jnp.bfloat16)
    summed = dot(values_t, low)
    total, context = summed[HEAD : HEAD + 1], summed[:HEAD]
    if before is not None:
        shrink = jnp.exp2((before[0] - top) * EXPONENT)
        total = total + before[1] * shrink
        context = context + before[2] * shrink
    return raised, low, top, total, context


def forward_kernel(count, first, tile, *refs):
    chunks, refs = refs[:count], refs[count:]
    qt_ref, refs = refs[0], refs[1:]
    if not first:
        stats_in, context_in, refs = refs[0], refs[1], refs[2:]
    stats_ref, context_ref, low_ref, k_ref, vt_ref = refs
    heads, pair_rows, _ = chunks[0].shape
    for h in range(heads):
        split_chunks(chunks, h, pair_rows // 2, k_ref=k_ref, vt_ref=vt_ref)

    @tiles(qt_ref.shape[2] // tile)
    def _(j):
        here = tokens_of(j, tile)
        for h in range(heads):
            before = None
            if not first:
                before = (stats_in[h, 0:1, here], stats_in[h, 1:2, here], context_in[h, :, here])
            _, low, top, total, context = raise_scores(
                k_ref[h], qt_ref[h, :, here], vt_ref[h], before
            )
            low_ref[h, :, here] = low
            stats_ref[h, 0:1, here] = top
            stats_ref[h, 1:2, here] = total
            context_ref[h, :, here] = context


def gradients(raised, scale, row_dot, rows, gt, refs, h):
    v_ref, kt_ref, gk_ref, gv_ref = refs
    query_rows, grad_rows = rows
    weights = raised * scale
    grad_weights = dot(v_ref[h], gt)
    grad_scores = (weights * (grad_weights - row_dot)).astype(jnp.bfloat16)
    gv_ref[h] += dot(weights.astype(jnp.bfloat16), grad_rows)
    gk_ref[h] += dot(grad_scores, query_rows)
    return dot(kt_ref[h], grad_scores) * FACTOR


def turn_kernel(count, tile, *refs):
    chunks, refs = refs[:count], refs[count:]
    q_ref, g_ref, qt_ref, gt_ref, stats_in, context_in = refs[:6]
    stats_ref, context_ref, grad_q_ref = refs[6:9]
    outs, refs = refs[9 : 9 + count], refs[9 + count :]
    k_ref, vt_ref, v_ref, kt_ref, gk_ref, gv_ref = refs
    heads, pair_rows, _ = chunks[0].shape
    rows = pair_rows // 2
    for h in range(heads):
        split_chunks(chunks, h, rows, k_ref, v_ref, kt_ref, vt_ref)
    gk_ref[...] = jnp.zeros_like(gk_ref)
    gv_ref[...] = jnp.zeros_like(gv_ref)

    @tiles(qt_ref.shape[2] // tile)
    def _(j):
        here = tokens_of(j, tile)
        for h in range(heads):
            qt, gt = qt_ref[h, :, here], gt_ref[h, :, here]
            before = (stats_in[h, 0:1, here], stats_in[h, 1:2, here], context_in[h, :, here])
            raised, _, top, total, context = raise_scores(k_ref[h], qt, vt_ref[h], before)
            columns = slice(h * HEAD, (h + 1) * HEAD)
            rows_here = q_ref[0, here, columns], g_ref[0, here, columns]
            scale = 1.0 / total
            context = context * scale
            row_dot = jnp.sum(gt.astype(jnp.float32) * context, axis=0, keepdims=True)
            context_ref[h, :, here] = context
            stats_ref[h, 0:1, here] = top
            stats_ref[h, 1:2, here] = scale
            stats_ref[h, 2:3, here] = row_dot
            grad_q_ref[h, :, here] = gradients(
                raised, scale, row_dot, rows_here, gt, (v_ref, kt_ref, gk_ref, gv_ref), h
            )

    for h in range(heads):
        join_chunks(outs, h, rows, gk_ref, gv_ref)


def backward_kernel(back, counts, tile, *refs):
    refs = refs[back:]
    groups = []
    for count in counts:
        groups.append((refs[:count], refs[count], refs[count + 1]))
        refs = refs[count + 2 :]
    q_ref, g_ref, gt_ref, stats_ref, grad_q_in = refs[:5]
    grad_q_ref, refs = refs[5], refs[6:]
    outs, refs = refs[: sum(counts)], refs[sum(counts) :]
    scratch = [refs[i : i + 4] for i in range(0, len(refs), 4)]
    heads, pair_rows, _ = groups[0][0][0].shape
    rows = pair_rows // 2
    for (chunks, _, _), (v_ref, kt_ref, gk_ref, gv_ref) in zip(groups, scratch):
        for h in range(heads):
            split_chunks(chunks, h, rows, v_ref=v_ref, kt_ref=kt_ref)
        gk_ref[...] = jnp.zeros_like(gk_ref)
        gv_ref[...] = jnp.zeros_like(gv_ref)

    @tiles(gt_ref.shape[2] // tile)
    def _(j):
        here = tokens_of(j, tile)
        for h in range(heads):
            columns = slice(h * HEAD, (h + 1) * HEAD)
            rows_here = q_ref[0, here, columns], g_ref[0, here, columns]
            gt = gt_ref[h, :, here]
            top, scale, row_dot = (stats_ref[h, i : i + 1, here] for i in range(3))
            grad_q = grad_q_in[h, :, here]
            for (_, low_ref, then_ref), own in zip(groups, scratch):
                shrunk = jnp.exp2((then_ref[h, 0:1, here] - top) * EXPONENT)
                raised = low_ref[h, :, here].astype(jnp.float32)
                grad_q = grad_q + gradients(
                    raised, scale * shrunk, row_dot, rows_here, gt, own, h
                )
            grad_q_ref[h, :, here] = grad_q

    for count, (_, _, gk_ref, gv_ref) in zip(counts, scratch):
        for h in range(heads):
            join_chunks(outs[:count], h, rows, gk_ref, gv_ref)
        outs = outs[count:]


def cost(heads, rows, tokens, matmuls):
    return pl.CostEstimate(
        flops=2 * matmuls * heads * rows * tokens * HEAD,
        bytes_accessed=heads * (rows + tokens) * HEAD * 8,
        transcendentals=heads * rows * tokens,
    )


def attend(groups, queries, upstream, send_back):
    heads, pair_rows, _ = groups[0][0].shape
    rows = pair_rows // 2
    enc_len = sum(len(g) for g in groups) * rows
    tokens = queries.shape[1]
    qt, gt = turned(queries), turned(upstream)
    stats_shape = jax.ShapeDtypeStruct((heads, 8, tokens), jnp.float32)
    wide_shape = jax.ShapeDtypeStruct((heads, HEAD, tokens), jnp.float32)
    compiler_params = params(enc_len)

    def natural(count):
        return pltpu.VMEM((heads, count * rows, HEAD), jnp.bfloat16)

    def across(count, extra=0):
        return pltpu.VMEM((heads, HEAD + extra, count * rows), jnp.bfloat16)

    def sums(count):
        return pltpu.VMEM((heads, count * rows, HEAD), jnp.float32)

    def shapes_of(group):
        return [jax.ShapeDtypeStruct(c.shape, c.dtype) for c in group]

    state, kept = [], []
    for group in groups[:-1]:
        count = len(group)
        low_shape = jax.ShapeDtypeStruct((heads, count * rows, tokens), jnp.bfloat16)
        stats, context, low = pl.pallas_call(
            functools.partial(forward_kernel, count, not state, tile_of(count * rows, tokens)),
            out_shape=[stats_shape, wide_shape, low_shape],
            in_specs=[VMEM] * (count + 1 + len(state)),
            out_specs=[VMEM] * 3,
            scratch_shapes=[natural(count), across(count, 16)],
            compiler_params=compiler_params,
            cost_estimate=cost(heads, count * rows, tokens, 2),
            name="forward",
        )(*group, qt, *state)
        state = [stats, context]
        kept.append((low, stats))

    group, count = groups[-1], len(groups[-1])
    final, context, grad_q, *grads = pl.pallas_call(
        functools.partial(turn_kernel, count, tile_of(count * rows, tokens)),
        out_shape=[stats_shape, wide_shape, wide_shape] + shapes_of(group),
        in_specs=[VMEM] * (count + 6),
        out_specs=[VMEM] * (count + 3),
        scratch_shapes=[natural(count), across(count, 16), natural(count), across(count)]
        + [sums(count)] * 2,
        compiler_params=compiler_params,
        cost_estimate=cost(heads, count * rows, tokens, 6),
        name="turn",
    )(*group, queries, upstream, qt, gt, *state)
    returned = [send_back(len(groups) - 1, grads)]

    for part in (list(range(len(groups) - 2, 0, -1)), [0]):
        first = part != [0]
        counts = [len(groups[i]) for i in part]
        back = [] if first else returned[0]
        operands = []
        for i in part:
            operands += [*groups[i], *kept[i]]
        operands += [queries, upstream, gt, final, grad_q]
        outs = pl.pallas_call(
            functools.partial(
                backward_kernel, len(back), counts, tile_of(max(counts) * rows, tokens)
            ),
            out_shape=[wide_shape] + shapes_of(sum((groups[i] for i in part), [])),
            in_specs=[ANY] * len(back) + [VMEM] * len(operands),
            out_specs=[VMEM] * (1 + sum(counts)),
            scratch_shapes=[
                shape
                for count in counts
                for shape in (natural(count), across(count), sums(count), sums(count))
            ],
            compiler_params=compiler_params,
            cost_estimate=cost(heads, sum(counts) * rows, tokens, 4),
            name="backward",
        )(*back, *operands)
        grad_q, blocks = outs[0], list(outs[1:])
        for i in part:
            returned.append(send_back(i, blocks[: len(groups[i])]))
            blocks = blocks[len(groups[i]) :]
    return turned_back(context, queries.dtype), turned_back(grad_q, queries.dtype)


def shards(pairs, queries, upstream):
    _, rows, _, width = pairs.shape
    heads = queries.shape[2] // HEAD
    offsets = offset_groups()
    order = sum(offsets, [])
    blocks = []
    first = len(offsets[0])
    packed = pack(pairs, order[:first], heads) + pack(pairs, order[first:], heads)
    for offset, block in zip(order, packed):
        block = block.reshape(heads, 2 * rows, HEAD)
        blocks.append(lax.ppermute(block, AXES, route(offset, False)))
    groups = []
    for group in offsets:
        groups.append(blocks[: len(group)])
        blocks = blocks[len(group) :]
    homes, returned = [], []

    def send_back(i, grads):
        back = [lax.ppermute(g, AXES, route(o, True)) for o, g in zip(offsets[i], grads)]
        homes.extend(offsets[i])
        returned.extend(b.reshape(heads, rows, 2, HEAD) for b in back)
        return back

    context, grad_query = attend(groups, queries, upstream, send_back)
    return context, grad_query, unpack(returned, homes, width)


def solution(mesh):
    return jax.shard_map(
        shards,
        mesh=mesh,
        in_specs=(
            P("segment", ("seq", "tp"), None, None),
            P("segment", None, ("seq", "tp")),
            P("segment", None, ("seq", "tp")),
        ),
        out_specs=(
            P("segment", None, ("seq", "tp")),
            P("segment", None, ("seq", "tp")),
            P("segment", ("seq", "tp"), None, None),
        ),
        check_vma=False,
    )
```

```python
import functools

import jax
import jax.numpy as jnp
from jax import lax
from jax.experimental import pallas as pl
from jax.experimental.pallas import tpu as pltpu
from jax.sharding import PartitionSpec as P

HEAD = 128
AXES = ("segment", "seq", "tp")
FACTOR = HEAD**-0.5
EXPONENT = FACTOR * 1.4426950408889634
MIB = 1 << 20
ANY = pl.BlockSpec(memory_space=pl.ANY)
HBM = pl.BlockSpec(memory_space=pltpu.HBM)
VMEM = pl.BlockSpec(memory_space=pltpu.VMEM)


def offset_groups():
    seq_count = lax.axis_size("seq")
    tp_count = lax.axis_size("tp")
    near = [(0, dy) for dy in reversed(range(tp_count))]
    far = [(dz, dy) for dy in reversed(range(tp_count)) for dz in range(1, seq_count)]
    far.sort(key=lambda o: -abs(o[0] - seq_count / 2))
    eighth = max(1, (len(near) + len(far)) // 8)
    short, long = far[: -2 * eighth], far[-2 * eighth :]
    short.sort(key=lambda o: -o[1])
    half = len(short) // 2
    return [
        short[1:half] + short[:1] + near[:1],
        short[half:] + near[1:],
        long[:eighth],
        long[eighth:],
    ]


def group_at(offset):
    seq_count = lax.axis_size("seq")
    tp_count = lax.axis_size("tp")
    z = lax.rem(lax.axis_index("seq") + offset[0], seq_count)
    y = lax.rem(lax.axis_index("tp") + offset[1], tp_count)
    return z * tp_count + y


def route(offset, back):
    segments, seq_count, tp_count = (lax.axis_size(a) for a in AXES)
    hops = []
    for s in range(segments):
        for z in range(seq_count):
            for y in range(tp_count):
                source = (s * seq_count + z) * tp_count + y
                s_to = (s + 1) % segments
                z_to = (z + offset[0]) % seq_count
                y_to = (y + offset[1]) % tp_count
                target = (s_to * seq_count + z_to) * tp_count + y_to
                hops.append((target, source) if back else (source, target))
    return hops


def params(enc_len):
    return pltpu.CompilerParams(vmem_limit_bytes=(12 + enc_len * 36 // 4096) * MIB)


def pack(pairs, order, heads):
    _, rows, _, width = pairs.shape
    local = heads * HEAD

    def kernel(pairs_ref, *outs):
        @pl.loop(0, rows // 16)
        def _(r):
            here = pl.ds(pl.multiple_of(r * 16, 16), 16)
            for out, offset in zip(outs, order):
                base = group_at(offset) * local
                for h in range(heads):
                    column = pl.multiple_of(base + h * HEAD, HEAD)
                    out[h, here] = pairs_ref[0, here, :, pl.ds(column, HEAD)]

    return pl.pallas_call(
        kernel,
        out_shape=[jax.ShapeDtypeStruct((heads, rows, 2, HEAD), pairs.dtype)] * len(order),
        in_specs=[VMEM],
        out_specs=[VMEM] * len(order),
        compiler_params=pltpu.CompilerParams(vmem_limit_bytes=24 * MIB),
        name="pack",
    )(pairs)


def unpack(blocks, order, width):
    heads, rows, _, _ = blocks[0].shape
    local = heads * HEAD
    parts = 4 if rows % 64 == 0 else 1
    size = rows // parts

    def kernel(*refs):
        ins, out, held, sem = refs[: len(order)], refs[len(order)], refs[-2], refs[-1]

        def store(r):
            here = pl.ds(pl.multiple_of(r * size, size), size)
            return pltpu.make_async_copy(held.at[here], out.at[0, here], sem.at[r])

        @pl.loop(0, parts)
        def _(r):
            here = pl.ds(pl.multiple_of(r * size, size), size)
            for block, offset in zip(ins, order):
                base = group_at(offset) * local
                for h in range(heads):
                    column = pl.multiple_of(base + h * HEAD, HEAD)
                    held[here, :, pl.ds(column, HEAD)] = block[h, here]
            store(r).start()

        for r in range(parts):
            store(r).wait()

    return pl.pallas_call(
        kernel,
        out_shape=jax.ShapeDtypeStruct((1, rows, 2, width), blocks[0].dtype),
        in_specs=[VMEM] * len(order),
        out_specs=HBM,
        scratch_shapes=[
            pltpu.VMEM((rows, 2, width), blocks[0].dtype),
            pltpu.SemaphoreType.DMA((parts,)),
        ],
        compiler_params=pltpu.CompilerParams(vmem_limit_bytes=24 * MIB),
        name="unpack",
    )(*blocks)


def turned(rows):
    _, tokens, local = rows.shape
    heads = local // HEAD
    tile = 256 if tokens % 256 == 0 else tokens

    def kernel(rows_ref, out_ref):
        for h in range(heads):
            for j in range(tokens // tile):
                here = slice(j * tile, (j + 1) * tile)
                block = rows_ref[0, here, h * HEAD : (h + 1) * HEAD]
                out_ref[h, :, here] = block.astype(jnp.float32).T.astype(rows.dtype)

    return pl.pallas_call(
        kernel,
        out_shape=jax.ShapeDtypeStruct((heads, HEAD, tokens), rows.dtype),
        in_specs=[VMEM],
        out_specs=VMEM,
        compiler_params=pltpu.CompilerParams(vmem_limit_bytes=16 * MIB),
        name="turned",
    )(rows)


def tiles(count):
    def run(body):
        if count <= 2:
            for j in range(count):
                body(j)
        else:
            pl.loop(0, count)(body)

    return run


def tokens_of(j, tile):
    return pl.ds(j * tile if isinstance(j, int) else pl.multiple_of(j * tile, tile), tile)


def tile_of(rows, tokens):
    for parts in range(1, tokens // 256 + 1):
        if tokens % (256 * parts) == 0 and rows * (tokens // parts) * 4 <= 5 * MIB // 4:
            return tokens // parts
    return 256 if tokens % 256 == 0 else tokens


def turned_back(columns, dtype):
    heads, _, tokens = columns.shape
    tile = 256 if tokens % 256 == 0 else tokens

    def kernel(columns_ref, out_ref):
        for h in range(heads):
            for j in range(tokens // tile):
                here = slice(j * tile, (j + 1) * tile)
                block = columns_ref[h, :, here].T.astype(dtype)
                out_ref[0, here, h * HEAD : (h + 1) * HEAD] = block

    return pl.pallas_call(
        kernel,
        out_shape=jax.ShapeDtypeStruct((1, tokens, heads * HEAD), dtype),
        in_specs=[VMEM],
        out_specs=VMEM,
        compiler_params=pltpu.CompilerParams(vmem_limit_bytes=16 * MIB),
        name="turned_back",
    )(columns)


def dot(a, b, contract=((1,), (0,))):
    return lax.dot_general(a, b, (contract, ((), ())), preferred_element_type=jnp.float32)


def shuffle(rows, join):
    to = lax.broadcasted_iota(jnp.int32, (2 * rows, 2 * rows), 1 if join else 0)
    source = lax.broadcasted_iota(jnp.int32, (2 * rows, 2 * rows), 0 if join else 1)
    wanted = jnp.where(to < rows, 2 * to, 2 * (to - rows) + 1)
    return jnp.where(source == wanted, 1.0, 0.0).astype(jnp.bfloat16)


def split_chunks(chunks, h, rows, k_ref=None, v_ref=None, kt_ref=None, vt_ref=None):
    split = shuffle(rows, False)
    for i, chunk in enumerate(chunks):
        both = dot(split, chunk[h])
        here = slice(i * rows, (i + 1) * rows)
        keys, values = both[:rows], both[rows:]
        if k_ref is not None:
            k_ref[h, here, :] = keys.astype(jnp.bfloat16)
        if v_ref is not None:
            v_ref[h, here, :] = values.astype(jnp.bfloat16)
        if kt_ref is not None:
            kt_ref[h, :, here] = keys.T.astype(jnp.bfloat16)
        if vt_ref is not None:
            vt_ref[h, :HEAD, here] = values.T.astype(jnp.bfloat16)
    if vt_ref is not None:
        tail = (vt_ref.shape[1] - HEAD, vt_ref.shape[2])
        vt_ref[h, HEAD:, :] = jnp.ones(tail, jnp.bfloat16)


def join_chunks(outs, h, rows, gk_ref, gv_ref):
    join = shuffle(rows, True)
    for i, out in enumerate(outs):
        here = slice(i * rows, (i + 1) * rows)
        both = jnp.concatenate([gk_ref[h, here, :] * FACTOR, gv_ref[h, here, :]], axis=0)
        out[h] = dot(join, both.astype(jnp.bfloat16)).astype(jnp.bfloat16)


def raise_scores(keys, qt, values_t, before):
    scores = dot(keys, qt)
    top = jnp.max(scores, axis=0, keepdims=True)
    if before is not None:
        top = jnp.maximum(top, before[0])
    raised = jnp.exp2((scores - top) * EXPONENT)
    low = raised.astype(jnp.bfloat16)
    summed = dot(values_t, low)
    total, context = summed[HEAD : HEAD + 1], summed[:HEAD]
    if before is not None:
        shrink = jnp.exp2((before[0] - top) * EXPONENT)
        total = total + before[1] * shrink
        context = context + before[2] * shrink
    return raised, low, top, total, context


def forward_kernel(count, first, tile, *refs):
    chunks, refs = refs[:count], refs[count:]
    qt_ref, refs = refs[0], refs[1:]
    if not first:
        stats_in, context_in, refs = refs[0], refs[1], refs[2:]
    stats_ref, context_ref, low_ref, k_ref, vt_ref = refs
    heads, pair_rows, _ = chunks[0].shape
    for h in range(heads):
        split_chunks(chunks, h, pair_rows // 2, k_ref=k_ref, vt_ref=vt_ref)

    @tiles(qt_ref.shape[2] // tile)
    def _(j):
        here = tokens_of(j, tile)
        for h in range(heads):
            before = None
            if not first:
                before = (stats_in[h, 0:1, here], stats_in[h, 1:2, here], context_in[h, :, here])
            _, low, top, total, context = raise_scores(
                k_ref[h], qt_ref[h, :, here], vt_ref[h], before
            )
            low_ref[h, :, here] = low
            stats_ref[h, 0:1, here] = top
            stats_ref[h, 1:2, here] = total
            context_ref[h, :, here] = context


def gradients(raised, scale, row_dot, rows, gt, refs, h):
    v_ref, kt_ref, gk_ref, gv_ref = refs
    query_rows, grad_rows = rows
    weights = raised * scale
    grad_weights = dot(v_ref[h], gt)
    grad_scores = (weights * (grad_weights - row_dot)).astype(jnp.bfloat16)
    gv_ref[h] += dot(weights.astype(jnp.bfloat16), grad_rows)
    gk_ref[h] += dot(grad_scores, query_rows)
    return dot(kt_ref[h], grad_scores) * FACTOR


def turn_kernel(count, tile, *refs):
    chunks, refs = refs[:count], refs[count:]
    q_ref, g_ref, qt_ref, gt_ref, stats_in, context_in = refs[:6]
    stats_ref, context_ref, grad_q_ref = refs[6:9]
    outs, refs = refs[9 : 9 + count], refs[9 + count :]
    k_ref, vt_ref, v_ref, kt_ref, gk_ref, gv_ref = refs
    heads, pair_rows, _ = chunks[0].shape
    rows = pair_rows // 2
    for h in range(heads):
        split_chunks(chunks, h, rows, k_ref, v_ref, kt_ref, vt_ref)
    gk_ref[...] = jnp.zeros_like(gk_ref)
    gv_ref[...] = jnp.zeros_like(gv_ref)

    @tiles(qt_ref.shape[2] // tile)
    def _(j):
        here = tokens_of(j, tile)
        for h in range(heads):
            qt, gt = qt_ref[h, :, here], gt_ref[h, :, here]
            before = (stats_in[h, 0:1, here], stats_in[h, 1:2, here], context_in[h, :, here])
            raised, _, top, total, context = raise_scores(k_ref[h], qt, vt_ref[h], before)
            columns = slice(h * HEAD, (h + 1) * HEAD)
            rows_here = q_ref[0, here, columns], g_ref[0, here, columns]
            scale = 1.0 / total
            context = context * scale
            row_dot = jnp.sum(gt.astype(jnp.float32) * context, axis=0, keepdims=True)
            context_ref[h, :, here] = context
            stats_ref[h, 0:1, here] = top
            stats_ref[h, 1:2, here] = scale
            stats_ref[h, 2:3, here] = row_dot
            grad_q_ref[h, :, here] = gradients(
                raised, scale, row_dot, rows_here, gt, (v_ref, kt_ref, gk_ref, gv_ref), h
            )

    for h in range(heads):
        join_chunks(outs, h, rows, gk_ref, gv_ref)


def backward_kernel(back, counts, tile, *refs):
    refs = refs[back:]
    groups = []
    for count in counts:
        groups.append((refs[:count], refs[count], refs[count + 1]))
        refs = refs[count + 2 :]
    q_ref, g_ref, gt_ref, stats_ref, grad_q_in = refs[:5]
    grad_q_ref, refs = refs[5], refs[6:]
    outs, refs = refs[: sum(counts)], refs[sum(counts) :]
    scratch = [refs[i : i + 4] for i in range(0, len(refs), 4)]
    heads, pair_rows, _ = groups[0][0][0].shape
    rows = pair_rows // 2
    for (chunks, _, _), (v_ref, kt_ref, gk_ref, gv_ref) in zip(groups, scratch):
        for h in range(heads):
            split_chunks(chunks, h, rows, v_ref=v_ref, kt_ref=kt_ref)
        gk_ref[...] = jnp.zeros_like(gk_ref)
        gv_ref[...] = jnp.zeros_like(gv_ref)

    @tiles(gt_ref.shape[2] // tile)
    def _(j):
        here = tokens_of(j, tile)
        for h in range(heads):
            columns = slice(h * HEAD, (h + 1) * HEAD)
            rows_here = q_ref[0, here, columns], g_ref[0, here, columns]
            gt = gt_ref[h, :, here]
            top, scale, row_dot = (stats_ref[h, i : i + 1, here] for i in range(3))
            grad_q = grad_q_in[h, :, here]
            for (_, low_ref, then_ref), own in zip(groups, scratch):
                shrunk = jnp.exp2((then_ref[h, 0:1, here] - top) * EXPONENT)
                raised = low_ref[h, :, here].astype(jnp.float32)
                grad_q = grad_q + gradients(
                    raised, scale * shrunk, row_dot, rows_here, gt, own, h
                )
            grad_q_ref[h, :, here] = grad_q

    for count, (_, _, gk_ref, gv_ref) in zip(counts, scratch):
        for h in range(heads):
            join_chunks(outs[:count], h, rows, gk_ref, gv_ref)
        outs = outs[count:]


def cost(heads, rows, tokens, matmuls):
    return pl.CostEstimate(
        flops=2 * matmuls * heads * rows * tokens * HEAD,
        bytes_accessed=heads * (rows + tokens) * HEAD * 8,
        transcendentals=heads * rows * tokens,
    )


def attend(groups, queries, upstream, send_back):
    heads, pair_rows, _ = groups[0][0].shape
    rows = pair_rows // 2
    enc_len = sum(len(g) for g in groups) * rows
    tokens = queries.shape[1]
    qt, gt = turned(queries), turned(upstream)
    stats_shape = jax.ShapeDtypeStruct((heads, 8, tokens), jnp.float32)
    wide_shape = jax.ShapeDtypeStruct((heads, HEAD, tokens), jnp.float32)
    compiler_params = params(enc_len)

    def natural(count):
        return pltpu.VMEM((heads, count * rows, HEAD), jnp.bfloat16)

    def across(count, extra=0):
        return pltpu.VMEM((heads, HEAD + extra, count * rows), jnp.bfloat16)

    def sums(count):
        return pltpu.VMEM((heads, count * rows, HEAD), jnp.float32)

    def shapes_of(group):
        return [jax.ShapeDtypeStruct(c.shape, c.dtype) for c in group]

    state, kept = [], []
    for group in groups[:-1]:
        count = len(group)
        low_shape = jax.ShapeDtypeStruct((heads, count * rows, tokens), jnp.bfloat16)
        stats, context, low = pl.pallas_call(
            functools.partial(forward_kernel, count, not state, tile_of(count * rows, tokens)),
            out_shape=[stats_shape, wide_shape, low_shape],
            in_specs=[VMEM] * (count + 1 + len(state)),
            out_specs=[VMEM] * 3,
            scratch_shapes=[natural(count), across(count, 16)],
            compiler_params=compiler_params,
            cost_estimate=cost(heads, count * rows, tokens, 2),
            name="forward",
        )(*group, qt, *state)
        state = [stats, context]
        kept.append((low, stats))

    group, count = groups[-1], len(groups[-1])
    final, context, grad_q, *grads = pl.pallas_call(
        functools.partial(turn_kernel, count, tile_of(count * rows, tokens)),
        out_shape=[stats_shape, wide_shape, wide_shape] + shapes_of(group),
        in_specs=[VMEM] * (count + 6),
        out_specs=[VMEM] * (count + 3),
        scratch_shapes=[natural(count), across(count, 16), natural(count), across(count)]
        + [sums(count)] * 2,
        compiler_params=compiler_params,
        cost_estimate=cost(heads, count * rows, tokens, 6),
        name="turn",
    )(*group, queries, upstream, qt, gt, *state)
    returned = [send_back(len(groups) - 1, grads)]

    for part in (list(range(len(groups) - 2, 0, -1)), [0]):
        first = part != [0]
        counts = [len(groups[i]) for i in part]
        back = [] if first else returned[0]
        operands = []
        for i in part:
            operands += [*groups[i], *kept[i]]
        operands += [queries, upstream, gt, final, grad_q]
        outs = pl.pallas_call(
            functools.partial(
                backward_kernel, len(back), counts, tile_of(max(counts) * rows, tokens)
            ),
            out_shape=[wide_shape] + shapes_of(sum((groups[i] for i in part), [])),
            in_specs=[ANY] * len(back) + [VMEM] * len(operands),
            out_specs=[VMEM] * (1 + sum(counts)),
            scratch_shapes=[
                shape
                for count in counts
                for shape in (natural(count), across(count), sums(count), sums(count))
            ],
            compiler_params=compiler_params,
            cost_estimate=cost(heads, sum(counts) * rows, tokens, 4),
            name="backward",
        )(*back, *operands)
        grad_q, blocks = outs[0], list(outs[1:])
        for i in part:
            returned.append(send_back(i, blocks[: len(groups[i])]))
            blocks = blocks[len(groups[i]) :]
    return turned_back(context, queries.dtype), turned_back(grad_q, queries.dtype)


def shards(pairs, queries, upstream):
    _, rows, _, width = pairs.shape
    heads = queries.shape[2] // HEAD
    offsets = offset_groups()
    order = sum(offsets, [])
    blocks = []
    first = len(offsets[0])
    packed = pack(pairs, order[:first], heads) + pack(pairs, order[first:], heads)
    for offset, block in zip(order, packed):
        block = block.reshape(heads, 2 * rows, HEAD)
        blocks.append(lax.ppermute(block, AXES, route(offset, False)))
    groups = []
    for group in offsets:
        groups.append(blocks[: len(group)])
        blocks = blocks[len(group) :]
    homes, returned = [], []

    def send_back(i, grads):
        sent = sorted(zip(offsets[i], grads), key=lambda s: (s[0][0] > 0) == (i == 1))
        back = [lax.ppermute(g, AXES, route(o, True)) for o, g in sent]
        homes.extend(o for o, _ in sent)
        returned.extend(b.reshape(heads, rows, 2, HEAD) for b in back)
        return back

    context, grad_query = attend(groups, queries, upstream, send_back)
    return context, grad_query, unpack(returned, homes, width)


def solution(mesh):
    return jax.shard_map(
        shards,
        mesh=mesh,
        in_specs=(
            P("segment", ("seq", "tp"), None, None),
            P("segment", None, ("seq", "tp")),
            P("segment", None, ("seq", "tp")),
        ),
        out_specs=(
            P("segment", None, ("seq", "tp")),
            P("segment", None, ("seq", "tp")),
            P("segment", ("seq", "tp"), None, None),
        ),
        check_vma=False,
    )
```

```python
import functools

import jax
import jax.numpy as jnp
from jax import lax
from jax.experimental import pallas as pl
from jax.experimental.pallas import tpu as pltpu
from jax.sharding import PartitionSpec as P

HEAD = 128
AXES = ("segment", "seq", "tp")
FACTOR = HEAD**-0.5
EXPONENT = FACTOR * 1.4426950408889634
MIB = 1 << 20
ANY = pl.BlockSpec(memory_space=pl.ANY)
HBM = pl.BlockSpec(memory_space=pltpu.HBM)
VMEM = pl.BlockSpec(memory_space=pltpu.VMEM)


def offset_groups():
    seq_count = lax.axis_size("seq")
    tp_count = lax.axis_size("tp")
    near = [(0, dy) for dy in reversed(range(tp_count))]
    far = [(dz, dy) for dy in reversed(range(tp_count)) for dz in range(1, seq_count)]
    far.sort(key=lambda o: -abs(o[0] - seq_count / 2))
    eighth = max(1, (len(near) + len(far)) // 8)
    short, long = far[: -2 * eighth], far[-2 * eighth :]
    short.sort(key=lambda o: -o[1])
    half = len(short) // 2
    return [
        short[1:half] + short[:1] + near[:1],
        short[half:] + near[1:],
        long[:eighth],
        long[eighth:],
    ]


def group_at(offset):
    seq_count = lax.axis_size("seq")
    tp_count = lax.axis_size("tp")
    z = lax.rem(lax.axis_index("seq") + offset[0], seq_count)
    y = lax.rem(lax.axis_index("tp") + offset[1], tp_count)
    return z * tp_count + y


def route(offset, back):
    segments, seq_count, tp_count = (lax.axis_size(a) for a in AXES)
    hops = []
    for s in range(segments):
        for z in range(seq_count):
            for y in range(tp_count):
                source = (s * seq_count + z) * tp_count + y
                s_to = (s + 1) % segments
                z_to = (z + offset[0]) % seq_count
                y_to = (y + offset[1]) % tp_count
                target = (s_to * seq_count + z_to) * tp_count + y_to
                hops.append((target, source) if back else (source, target))
    return hops


def params(enc_len):
    return pltpu.CompilerParams(vmem_limit_bytes=(12 + enc_len * 36 // 4096) * MIB)


def pack(pairs, order, heads):
    _, rows, _, width = pairs.shape
    local = heads * HEAD

    def kernel(pairs_ref, *outs):
        @pl.loop(0, rows // 16)
        def _(r):
            here = pl.ds(pl.multiple_of(r * 16, 16), 16)
            for out, offset in zip(outs, order):
                base = group_at(offset) * local
                for h in range(heads):
                    column = pl.multiple_of(base + h * HEAD, HEAD)
                    out[h, here] = pairs_ref[0, here, :, pl.ds(column, HEAD)]

    return pl.pallas_call(
        kernel,
        out_shape=[jax.ShapeDtypeStruct((heads, rows, 2, HEAD), pairs.dtype)] * len(order),
        in_specs=[VMEM],
        out_specs=[VMEM] * len(order),
        compiler_params=pltpu.CompilerParams(vmem_limit_bytes=24 * MIB),
        name="pack",
    )(pairs)


def unpack(blocks, order, width):
    heads, rows, _, _ = blocks[0].shape
    local = heads * HEAD
    parts = 4 if rows % 64 == 0 else 1
    size = rows // parts

    def kernel(*refs):
        ins, out, held, sem = refs[: len(order)], refs[len(order)], refs[-2], refs[-1]

        def store(r):
            here = pl.ds(pl.multiple_of(r * size, size), size)
            return pltpu.make_async_copy(held.at[here], out.at[0, here], sem.at[r])

        @pl.loop(0, parts)
        def _(r):
            here = pl.ds(pl.multiple_of(r * size, size), size)
            for block, offset in zip(ins, order):
                base = group_at(offset) * local
                for h in range(heads):
                    column = pl.multiple_of(base + h * HEAD, HEAD)
                    held[here, :, pl.ds(column, HEAD)] = block[h, here]
            store(r).start()

        for r in range(parts):
            store(r).wait()

    return pl.pallas_call(
        kernel,
        out_shape=jax.ShapeDtypeStruct((1, rows, 2, width), blocks[0].dtype),
        in_specs=[VMEM] * len(order),
        out_specs=HBM,
        scratch_shapes=[
            pltpu.VMEM((rows, 2, width), blocks[0].dtype),
            pltpu.SemaphoreType.DMA((parts,)),
        ],
        compiler_params=pltpu.CompilerParams(vmem_limit_bytes=24 * MIB),
        name="unpack",
    )(*blocks)


def turned(rows):
    _, tokens, local = rows.shape
    heads = local // HEAD
    tile = 256 if tokens % 256 == 0 else tokens

    def kernel(rows_ref, out_ref):
        for h in range(heads):
            for j in range(tokens // tile):
                here = slice(j * tile, (j + 1) * tile)
                block = rows_ref[0, here, h * HEAD : (h + 1) * HEAD]
                out_ref[h, :, here] = block.astype(jnp.float32).T.astype(rows.dtype)

    return pl.pallas_call(
        kernel,
        out_shape=jax.ShapeDtypeStruct((heads, HEAD, tokens), rows.dtype),
        in_specs=[VMEM],
        out_specs=VMEM,
        compiler_params=pltpu.CompilerParams(vmem_limit_bytes=16 * MIB),
        name="turned",
    )(rows)


def tiles(count):
    def run(body):
        if count <= 2:
            for j in range(count):
                body(j)
        else:
            pl.loop(0, count)(body)

    return run


def tokens_of(j, tile):
    return pl.ds(j * tile if isinstance(j, int) else pl.multiple_of(j * tile, tile), tile)


def tile_of(rows, tokens):
    for parts in range(1, tokens // 256 + 1):
        if tokens % (256 * parts) == 0 and rows * (tokens // parts) * 4 <= 5 * MIB // 4:
            return tokens // parts
    return 256 if tokens % 256 == 0 else tokens


def turned_back(columns, dtype):
    heads, _, tokens = columns.shape
    tile = 256 if tokens % 256 == 0 else tokens

    def kernel(columns_ref, out_ref):
        for h in range(heads):
            for j in range(tokens // tile):
                here = slice(j * tile, (j + 1) * tile)
                block = columns_ref[h, :, here].T.astype(dtype)
                out_ref[0, here, h * HEAD : (h + 1) * HEAD] = block

    return pl.pallas_call(
        kernel,
        out_shape=jax.ShapeDtypeStruct((1, tokens, heads * HEAD), dtype),
        in_specs=[VMEM],
        out_specs=VMEM,
        compiler_params=pltpu.CompilerParams(vmem_limit_bytes=16 * MIB),
        name="turned_back",
    )(columns)


def dot(a, b, contract=((1,), (0,))):
    return lax.dot_general(a, b, (contract, ((), ())), preferred_element_type=jnp.float32)


def shuffle(rows, join):
    to = lax.broadcasted_iota(jnp.int32, (2 * rows, 2 * rows), 1 if join else 0)
    source = lax.broadcasted_iota(jnp.int32, (2 * rows, 2 * rows), 0 if join else 1)
    wanted = jnp.where(to < rows, 2 * to, 2 * (to - rows) + 1)
    return jnp.where(source == wanted, 1.0, 0.0).astype(jnp.bfloat16)


def reordered(blocks, join):
    heads, pair_rows, _ = blocks[0].shape

    def kernel(*refs):
        order = shuffle(pair_rows // 2, join)
        for block, out in zip(refs[: len(blocks)], refs[len(blocks) :]):
            for h in range(heads):
                out[h] = dot(order, block[h]).astype(out.dtype)

    return pl.pallas_call(
        kernel,
        out_shape=[jax.ShapeDtypeStruct(b.shape, b.dtype) for b in blocks],
        in_specs=[VMEM] * len(blocks),
        out_specs=[VMEM] * len(blocks),
        compiler_params=pltpu.CompilerParams(vmem_limit_bytes=24 * MIB),
        name="reordered",
    )(*blocks)


def split_chunks(chunks, h, rows, refs, done):
    k_ref, v_ref, kt_ref, vt_ref = refs
    split = None if done else shuffle(rows, False)
    for i, chunk in enumerate(chunks):
        both = chunk[h].astype(jnp.float32) if done else dot(split, chunk[h])
        here = slice(i * rows, (i + 1) * rows)
        keys, values = both[:rows], both[rows:]
        k_ref[h, here, :] = keys.astype(jnp.bfloat16)
        v_ref[h, here, :] = values.astype(jnp.bfloat16)
        kt_ref[h, :, here] = keys.T.astype(jnp.bfloat16)
        vt_ref[h, :HEAD, here] = values.T.astype(jnp.bfloat16)
    tail = (vt_ref.shape[1] - HEAD, vt_ref.shape[2])
    vt_ref[h, HEAD:, :] = jnp.ones(tail, jnp.bfloat16)


def store_chunks(outs, h, rows, gk_ref, gv_ref, join):
    order = shuffle(rows, True) if join else None
    for i, out in enumerate(outs):
        here = slice(i * rows, (i + 1) * rows)
        both = jnp.concatenate([gk_ref[h, here, :] * FACTOR, gv_ref[h, here, :]], axis=0)
        both = both.astype(jnp.bfloat16)
        out[h] = dot(order, both).astype(jnp.bfloat16) if join else both


def raise_scores(keys, qt, values_t, before):
    scores = dot(keys, qt)
    top = jnp.max(scores, axis=0, keepdims=True)
    if before is not None:
        top = jnp.maximum(top, before[0])
    raised = jnp.exp2((scores - top) * EXPONENT)
    low = raised.astype(jnp.bfloat16)
    summed = dot(values_t, low)
    total, context = summed[HEAD : HEAD + 1], summed[:HEAD]
    if before is not None:
        shrink = jnp.exp2((before[0] - top) * EXPONENT)
        total = total + before[1] * shrink
        context = context + before[2] * shrink
    return raised, low, top, total, context


def forward_kernel(count, first, tile, *refs):
    chunks, refs = refs[:count], refs[count:]
    qt_ref, refs = refs[0], refs[1:]
    if not first:
        stats_in, context_in, refs = refs[0], refs[1], refs[2:]
    stats_ref, context_ref, low_ref, v_ref, kt_ref, k_ref, vt_ref = refs
    heads, pair_rows, _ = chunks[0].shape
    for h in range(heads):
        split_chunks(chunks, h, pair_rows // 2, (k_ref, v_ref, kt_ref, vt_ref), False)

    @tiles(qt_ref.shape[2] // tile)
    def _(j):
        here = tokens_of(j, tile)
        for h in range(heads):
            before = None
            if not first:
                before = (stats_in[h, 0:1, here], stats_in[h, 1:2, here], context_in[h, :, here])
            _, low, top, total, context = raise_scores(
                k_ref[h], qt_ref[h, :, here], vt_ref[h], before
            )
            low_ref[h, :, here] = low
            stats_ref[h, 0:1, here] = top
            stats_ref[h, 1:2, here] = total
            context_ref[h, :, here] = context


def gradients(raised, scale, row_dot, rows, gt, refs, h):
    v_ref, kt_ref, gk_ref, gv_ref = refs
    query_rows, grad_rows = rows
    weights = raised * scale
    grad_weights = dot(v_ref[h], gt)
    grad_scores = (weights * (grad_weights - row_dot)).astype(jnp.bfloat16)
    gv_ref[h] += dot(weights.astype(jnp.bfloat16), grad_rows)
    gk_ref[h] += dot(grad_scores, query_rows)
    return dot(kt_ref[h], grad_scores) * FACTOR


def turn_kernel(count, tile, *refs):
    chunks, refs = refs[:count], refs[count:]
    q_ref, g_ref, qt_ref, gt_ref, stats_in, context_in = refs[:6]
    stats_ref, context_ref, grad_q_ref = refs[6:9]
    outs, refs = refs[9 : 9 + count], refs[9 + count :]
    k_ref, vt_ref, v_ref, kt_ref, gk_ref, gv_ref = refs
    heads, pair_rows, _ = chunks[0].shape
    rows = pair_rows // 2
    for h in range(heads):
        split_chunks(chunks, h, rows, (k_ref, v_ref, kt_ref, vt_ref), True)
    gk_ref[...] = jnp.zeros_like(gk_ref)
    gv_ref[...] = jnp.zeros_like(gv_ref)

    @tiles(qt_ref.shape[2] // tile)
    def _(j):
        here = tokens_of(j, tile)
        for h in range(heads):
            qt, gt = qt_ref[h, :, here], gt_ref[h, :, here]
            before = (stats_in[h, 0:1, here], stats_in[h, 1:2, here], context_in[h, :, here])
            raised, _, top, total, context = raise_scores(k_ref[h], qt, vt_ref[h], before)
            columns = slice(h * HEAD, (h + 1) * HEAD)
            rows_here = q_ref[0, here, columns], g_ref[0, here, columns]
            scale = 1.0 / total
            context = context * scale
            row_dot = jnp.sum(gt.astype(jnp.float32) * context, axis=0, keepdims=True)
            context_ref[h, :, here] = context
            stats_ref[h, 0:1, here] = top
            stats_ref[h, 1:2, here] = scale
            stats_ref[h, 2:3, here] = row_dot
            grad_q_ref[h, :, here] = gradients(
                raised, scale, row_dot, rows_here, gt, (v_ref, kt_ref, gk_ref, gv_ref), h
            )

    for h in range(heads):
        store_chunks(outs, h, rows, gk_ref, gv_ref, False)


def backward_kernel(back, counts, join, tile, *refs):
    refs = refs[back:]
    groups = [refs[4 * i : 4 * i + 4] for i in range(len(counts))]
    refs = refs[4 * len(counts) :]
    q_ref, g_ref, gt_ref, stats_ref, grad_q_in, grad_q_ref = refs[:6]
    outs, refs = refs[6 : 6 + sum(counts)], refs[6 + sum(counts) :]
    sums = [refs[i : i + 2] for i in range(0, len(refs), 2)]
    heads, pair_rows, _ = outs[0].shape
    for ref in refs:
        ref[...] = jnp.zeros_like(ref)

    @tiles(gt_ref.shape[2] // tile)
    def _(j):
        here = tokens_of(j, tile)
        for h in range(heads):
            columns = slice(h * HEAD, (h + 1) * HEAD)
            rows_here = q_ref[0, here, columns], g_ref[0, here, columns]
            gt = gt_ref[h, :, here]
            top, scale, row_dot = (stats_ref[h, i : i + 1, here] for i in range(3))
            grad_q = grad_q_in[h, :, here]
            for (low_ref, then_ref, v_ref, kt_ref), own in zip(groups, sums):
                shrunk = jnp.exp2((then_ref[h, 0:1, here] - top) * EXPONENT)
                raised = low_ref[h, :, here].astype(jnp.float32)
                grad_q = grad_q + gradients(
                    raised, scale * shrunk, row_dot, rows_here, gt, (v_ref, kt_ref, *own), h
                )
            grad_q_ref[h, :, here] = grad_q

    for count, (gk_ref, gv_ref) in zip(counts, sums):
        for h in range(heads):
            store_chunks(outs[:count], h, pair_rows // 2, gk_ref, gv_ref, join)
        outs = outs[count:]


def cost(heads, rows, tokens, matmuls):
    return pl.CostEstimate(
        flops=2 * matmuls * heads * rows * tokens * HEAD,
        bytes_accessed=heads * (rows + tokens) * HEAD * 8,
        transcendentals=heads * rows * tokens,
    )


def attend(groups, queries, upstream, send_back):
    heads, pair_rows, _ = groups[0][0].shape
    rows = pair_rows // 2
    enc_len = sum(len(g) for g in groups) * rows
    tokens = queries.shape[1]
    qt, gt = turned(queries), turned(upstream)
    stats_shape = jax.ShapeDtypeStruct((heads, 8, tokens), jnp.float32)
    wide_shape = jax.ShapeDtypeStruct((heads, HEAD, tokens), jnp.float32)
    compiler_params = params(enc_len)

    def natural(count):
        return pltpu.VMEM((heads, count * rows, HEAD), jnp.bfloat16)

    def across(count, extra=0):
        return pltpu.VMEM((heads, HEAD + extra, count * rows), jnp.bfloat16)

    def sums(count):
        return pltpu.VMEM((heads, count * rows, HEAD), jnp.float32)

    def shapes_of(group):
        return [jax.ShapeDtypeStruct(c.shape, c.dtype) for c in group]

    state, kept = [], []
    for group in groups[:-1]:
        count = len(group)
        low_shape = jax.ShapeDtypeStruct((heads, count * rows, tokens), jnp.bfloat16)
        v_shape = jax.ShapeDtypeStruct((heads, count * rows, HEAD), jnp.bfloat16)
        kt_shape = jax.ShapeDtypeStruct((heads, HEAD, count * rows), jnp.bfloat16)
        stats, context, *saved = pl.pallas_call(
            functools.partial(forward_kernel, count, not state, tile_of(count * rows, tokens)),
            out_shape=[stats_shape, wide_shape, low_shape, v_shape, kt_shape],
            in_specs=[VMEM] * (count + 1 + len(state)),
            out_specs=[VMEM] * 5,
            scratch_shapes=[natural(count), across(count, 16)],
            compiler_params=compiler_params,
            cost_estimate=cost(heads, count * rows, tokens, 2),
            name="forward",
        )(*group, qt, *state)
        state = [stats, context]
        kept.append((saved[0], stats, *saved[1:]))

    group, count = groups[-1], len(groups[-1])
    final, context, grad_q, *grads = pl.pallas_call(
        functools.partial(turn_kernel, count, tile_of(count * rows, tokens)),
        out_shape=[stats_shape, wide_shape, wide_shape] + shapes_of(group),
        in_specs=[VMEM] * (count + 6),
        out_specs=[VMEM] * (count + 3),
        scratch_shapes=[natural(count), across(count, 16), natural(count), across(count)]
        + [sums(count)] * 2,
        compiler_params=compiler_params,
        cost_estimate=cost(heads, count * rows, tokens, 6),
        name="turn",
    )(*group, queries, upstream, qt, gt, *state)
    returned = [send_back(len(groups) - 1, grads)]

    for part in (list(range(len(groups) - 2, 0, -1)), [0]):
        first = part != [0]
        counts = [len(groups[i]) for i in part]
        back = [] if first else returned[0]
        operands = []
        for i in part:
            operands += kept[i]
        operands += [queries, upstream, gt, final, grad_q]
        outs = pl.pallas_call(
            functools.partial(
                backward_kernel, len(back), counts, not first, tile_of(max(counts) * rows, tokens)
            ),
            out_shape=[wide_shape] + shapes_of(sum((groups[i] for i in part), [])),
            in_specs=[ANY] * len(back) + [VMEM] * len(operands),
            out_specs=[VMEM] * (1 + sum(counts)),
            scratch_shapes=[sums(count) for count in counts for _ in range(2)],
            compiler_params=compiler_params,
            cost_estimate=cost(heads, sum(counts) * rows, tokens, 4),
            name="backward",
        )(*back, *operands)
        grad_q, blocks = outs[0], list(outs[1:])
        for i in part:
            returned.append(send_back(i, blocks[: len(groups[i])]))
            blocks = blocks[len(groups[i]) :]
    return turned_back(context, queries.dtype), turned_back(grad_q, queries.dtype)


def shards(pairs, queries, upstream):
    _, rows, _, width = pairs.shape
    heads = queries.shape[2] // HEAD
    offsets = offset_groups()
    order = sum(offsets, [])
    blocks = []
    first = len(offsets[0])
    packed = pack(pairs, order[:first], heads) + pack(pairs, order[first:], heads)
    packed = [block.reshape(heads, 2 * rows, HEAD) for block in packed]
    final = len(offsets[-1])
    packed[-final:] = reordered(packed[-final:], False)
    for offset, block in zip(order, packed):
        blocks.append(lax.ppermute(block, AXES, route(offset, False)))
    groups = []
    for group in offsets:
        groups.append(blocks[: len(group)])
        blocks = blocks[len(group) :]
    homes, returned = [], []

    def send_back(i, grads):
        sent = sorted(zip(offsets[i], grads), key=lambda s: (s[0][0] > 0) == (i == 1))
        back = [lax.ppermute(g, AXES, route(o, True)) for o, g in sent]
        homes.extend(o for o, _ in sent)
        returned.append(back)
        return back

    context, grad_query = attend(groups, queries, upstream, send_back)
    early = reordered(sum(returned[:-1], []), True)
    returned = [b.reshape(heads, rows, 2, HEAD) for b in list(early) + returned[-1]]
    return context, grad_query, unpack(returned, homes, width)


def solution(mesh):
    return jax.shard_map(
        shards,
        mesh=mesh,
        in_specs=(
            P("segment", ("seq", "tp"), None, None),
            P("segment", None, ("seq", "tp")),
            P("segment", None, ("seq", "tp")),
        ),
        out_specs=(
            P("segment", None, ("seq", "tp")),
            P("segment", None, ("seq", "tp")),
            P("segment", ("seq", "tp"), None, None),
        ),
        check_vma=False,
    )
```

```python
import functools

import jax
import jax.numpy as jnp
from jax import lax
from jax.experimental import pallas as pl
from jax.experimental.pallas import tpu as pltpu
from jax.sharding import PartitionSpec as P

HEAD = 128
AXES = ("segment", "seq", "tp")
FACTOR = HEAD**-0.5
EXPONENT = FACTOR * 1.4426950408889634
MIB = 1 << 20
ANY = pl.BlockSpec(memory_space=pl.ANY)
HBM = pl.BlockSpec(memory_space=pltpu.HBM)
VMEM = pl.BlockSpec(memory_space=pltpu.VMEM)


def offset_groups():
    seq_count = lax.axis_size("seq")
    tp_count = lax.axis_size("tp")
    near = [(0, dy) for dy in reversed(range(tp_count))]
    far = [(dz, dy) for dy in reversed(range(tp_count)) for dz in range(1, seq_count)]
    far.sort(key=lambda o: -abs(o[0] - seq_count / 2))
    eighth = max(1, (len(near) + len(far)) // 8)
    short, long = far[: -2 * eighth], far[-2 * eighth :]
    short.sort(key=lambda o: -o[1])
    half = len(short) // 2
    return [
        short[1:half] + short[:1] + near[:1],
        short[half:] + near[1:],
        long[:eighth],
        long[eighth:],
    ]


def group_at(offset):
    seq_count = lax.axis_size("seq")
    tp_count = lax.axis_size("tp")
    z = lax.rem(lax.axis_index("seq") + offset[0], seq_count)
    y = lax.rem(lax.axis_index("tp") + offset[1], tp_count)
    return z * tp_count + y


def route(offset, back):
    segments, seq_count, tp_count = (lax.axis_size(a) for a in AXES)
    hops = []
    for s in range(segments):
        for z in range(seq_count):
            for y in range(tp_count):
                source = (s * seq_count + z) * tp_count + y
                s_to = (s + 1) % segments
                z_to = (z + offset[0]) % seq_count
                y_to = (y + offset[1]) % tp_count
                target = (s_to * seq_count + z_to) * tp_count + y_to
                hops.append((target, source) if back else (source, target))
    return hops


def params(enc_len):
    return pltpu.CompilerParams(vmem_limit_bytes=(12 + enc_len * 36 // 4096) * MIB)


def pack(pairs, order, heads):
    _, rows, _, width = pairs.shape
    local = heads * HEAD

    def kernel(pairs_ref, *outs):
        @pl.loop(0, rows // 16)
        def _(r):
            here = pl.ds(pl.multiple_of(r * 16, 16), 16)
            for out, offset in zip(outs, order):
                base = group_at(offset) * local
                for h in range(heads):
                    column = pl.multiple_of(base + h * HEAD, HEAD)
                    out[h, here] = pairs_ref[0, here, :, pl.ds(column, HEAD)]

    return pl.pallas_call(
        kernel,
        out_shape=[jax.ShapeDtypeStruct((heads, rows, 2, HEAD), pairs.dtype)] * len(order),
        in_specs=[VMEM],
        out_specs=[VMEM] * len(order),
        compiler_params=pltpu.CompilerParams(vmem_limit_bytes=24 * MIB),
        name="pack",
    )(pairs)


def unpack(blocks, order, width):
    heads, rows, _, _ = blocks[0].shape
    local = heads * HEAD
    parts = 4 if rows % 64 == 0 else 1
    size = rows // parts

    def kernel(*refs):
        ins, out, held, sem = refs[: len(order)], refs[len(order)], refs[-2], refs[-1]

        def store(r):
            here = pl.ds(pl.multiple_of(r * size, size), size)
            return pltpu.make_async_copy(held.at[here], out.at[0, here], sem.at[r])

        @pl.loop(0, parts)
        def _(r):
            here = pl.ds(pl.multiple_of(r * size, size), size)
            for block, offset in zip(ins, order):
                base = group_at(offset) * local
                for h in range(heads):
                    column = pl.multiple_of(base + h * HEAD, HEAD)
                    held[here, :, pl.ds(column, HEAD)] = block[h, here]
            store(r).start()

        for r in range(parts):
            store(r).wait()

    return pl.pallas_call(
        kernel,
        out_shape=jax.ShapeDtypeStruct((1, rows, 2, width), blocks[0].dtype),
        in_specs=[VMEM] * len(order),
        out_specs=HBM,
        scratch_shapes=[
            pltpu.VMEM((rows, 2, width), blocks[0].dtype),
            pltpu.SemaphoreType.DMA((parts,)),
        ],
        compiler_params=pltpu.CompilerParams(vmem_limit_bytes=24 * MIB),
        name="unpack",
    )(*blocks)


def turned(rows):
    _, tokens, local = rows.shape
    heads = local // HEAD
    tile = 256 if tokens % 256 == 0 else tokens

    def kernel(rows_ref, out_ref):
        for h in range(heads):
            for j in range(tokens // tile):
                here = slice(j * tile, (j + 1) * tile)
                block = rows_ref[0, here, h * HEAD : (h + 1) * HEAD]
                out_ref[h, :, here] = block.astype(jnp.float32).T.astype(rows.dtype)

    return pl.pallas_call(
        kernel,
        out_shape=jax.ShapeDtypeStruct((heads, HEAD, tokens), rows.dtype),
        in_specs=[VMEM],
        out_specs=VMEM,
        compiler_params=pltpu.CompilerParams(vmem_limit_bytes=16 * MIB),
        name="turned",
    )(rows)


def tiles(count):
    def run(body):
        if count <= 2:
            for j in range(count):
                body(j)
        else:
            pl.loop(0, count)(body)

    return run


def tokens_of(j, tile):
    return pl.ds(j * tile if isinstance(j, int) else pl.multiple_of(j * tile, tile), tile)


def tile_of(rows, tokens):
    for parts in range(1, tokens // 256 + 1):
        if tokens % (256 * parts) == 0 and rows * (tokens // parts) * 4 <= 5 * MIB // 4:
            return tokens // parts
    return 256 if tokens % 256 == 0 else tokens


def turned_back(parts, dtype):
    tokens = parts[0].shape[2]
    heads = sum(p.shape[0] for p in parts)
    tile = 256 if tokens % 256 == 0 else tokens

    def kernel(*refs):
        out_ref = refs[-1]
        sources = [(ref, k) for ref in refs[:-1] for k in range(ref.shape[0])]
        for h, (ref, k) in enumerate(sources):
            for j in range(tokens // tile):
                here = slice(j * tile, (j + 1) * tile)
                out_ref[0, here, h * HEAD : (h + 1) * HEAD] = ref[k, :, here].T.astype(dtype)

    return pl.pallas_call(
        kernel,
        out_shape=jax.ShapeDtypeStruct((1, tokens, heads * HEAD), dtype),
        in_specs=[VMEM] * len(parts),
        out_specs=VMEM,
        compiler_params=pltpu.CompilerParams(vmem_limit_bytes=16 * MIB),
        name="turned_back",
    )(*parts)


def dot(a, b, contract=((1,), (0,))):
    return lax.dot_general(a, b, (contract, ((), ())), preferred_element_type=jnp.float32)


def shuffle(rows, join):
    to = lax.broadcasted_iota(jnp.int32, (2 * rows, 2 * rows), 1 if join else 0)
    source = lax.broadcasted_iota(jnp.int32, (2 * rows, 2 * rows), 0 if join else 1)
    wanted = jnp.where(to < rows, 2 * to, 2 * (to - rows) + 1)
    return jnp.where(source == wanted, 1.0, 0.0).astype(jnp.bfloat16)


def reordered(parts, join, apart=False):
    pair_rows = parts[0][0].shape[1]
    heads = sum(b.shape[0] for b in parts[0])
    sizes = [1] * heads if apart else [heads]

    def kernel(*refs):
        order = shuffle(pair_rows // 2, join)
        ins, outs = refs[: sum(map(len, parts))], refs[sum(map(len, parts)) :]
        for part in parts:
            sources = [(ref, h) for ref in ins[: len(part)] for h in range(ref.shape[0])]
            targets = [(ref, h) for ref in outs[: len(sizes)] for h in range(ref.shape[0])]
            for (source, h), (target, k) in zip(sources, targets):
                target[k] = dot(order, source[h]).astype(target.dtype)
            ins, outs = ins[len(part) :], outs[len(sizes) :]

    return pl.pallas_call(
        kernel,
        out_shape=[
            jax.ShapeDtypeStruct((size, pair_rows, HEAD), part[0].dtype)
            for part in parts
            for size in sizes
        ],
        in_specs=[VMEM] * sum(map(len, parts)),
        out_specs=[VMEM] * (len(parts) * len(sizes)),
        compiler_params=pltpu.CompilerParams(vmem_limit_bytes=24 * MIB),
        name="reordered",
    )(*sum(parts, []))


def split_chunks(chunks, h, rows, refs, done):
    k_ref, v_ref, kt_ref, vt_ref = refs
    split = None if done else shuffle(rows, False)
    for i, chunk in enumerate(chunks):
        both = chunk[h].astype(jnp.float32) if done else dot(split, chunk[h])
        here = slice(i * rows, (i + 1) * rows)
        keys, values = both[:rows], both[rows:]
        k_ref[h, here, :] = keys.astype(jnp.bfloat16)
        v_ref[h, here, :] = values.astype(jnp.bfloat16)
        kt_ref[h, :, here] = keys.T.astype(jnp.bfloat16)
        vt_ref[h, :HEAD, here] = values.T.astype(jnp.bfloat16)
    tail = (vt_ref.shape[1] - HEAD, vt_ref.shape[2])
    vt_ref[h, HEAD:, :] = jnp.ones(tail, jnp.bfloat16)


def store_chunks(outs, h, rows, gk_ref, gv_ref, join):
    order = shuffle(rows, True) if join else None
    for i, out in enumerate(outs):
        here = slice(i * rows, (i + 1) * rows)
        both = jnp.concatenate([gk_ref[h, here, :] * FACTOR, gv_ref[h, here, :]], axis=0)
        both = both.astype(jnp.bfloat16)
        out[h] = dot(order, both).astype(jnp.bfloat16) if join else both


def raise_scores(keys, qt, values_t, before):
    scores = dot(keys, qt)
    top = jnp.max(scores, axis=0, keepdims=True)
    if before is not None:
        top = jnp.maximum(top, before[0])
    raised = jnp.exp2((scores - top) * EXPONENT)
    low = raised.astype(jnp.bfloat16)
    summed = dot(values_t, low)
    total, context = summed[HEAD : HEAD + 1], summed[:HEAD]
    if before is not None:
        shrink = jnp.exp2((before[0] - top) * EXPONENT)
        total = total + before[1] * shrink
        context = context + before[2] * shrink
    return raised, low, top, total, context


def forward_kernel(count, first, tile, *refs):
    chunks, refs = refs[:count], refs[count:]
    qt_ref, refs = refs[0], refs[1:]
    if not first:
        stats_in, context_in, refs = refs[0], refs[1], refs[2:]
    stats_ref, context_ref, low_ref, v_ref, kt_ref, k_ref, vt_ref = refs
    heads, pair_rows, _ = chunks[0].shape
    for h in range(heads):
        split_chunks(chunks, h, pair_rows // 2, (k_ref, v_ref, kt_ref, vt_ref), False)

    @tiles(qt_ref.shape[2] // tile)
    def _(j):
        here = tokens_of(j, tile)
        for h in range(heads):
            before = None
            if not first:
                before = (stats_in[h, 0:1, here], stats_in[h, 1:2, here], context_in[h, :, here])
            _, low, top, total, context = raise_scores(
                k_ref[h], qt_ref[h, :, here], vt_ref[h], before
            )
            low_ref[h, :, here] = low
            stats_ref[h, 0:1, here] = top
            stats_ref[h, 1:2, here] = total
            context_ref[h, :, here] = context


def gradients(raised, scale, row_dot, rows, gt, refs, h):
    v_ref, kt_ref, gk_ref, gv_ref = refs
    query_rows, grad_rows = rows
    weights = raised * scale
    grad_weights = dot(v_ref[h], gt)
    grad_scores = (weights * (grad_weights - row_dot)).astype(jnp.bfloat16)
    gv_ref[h] += dot(weights.astype(jnp.bfloat16), grad_rows)
    gk_ref[h] += dot(grad_scores, query_rows)
    return dot(kt_ref[h], grad_scores) * FACTOR


def turn_kernel(count, head, tile, *refs):
    chunks, refs = refs[:count], refs[count:]
    q_ref, g_ref, qt_ref, gt_ref, stats_in, context_in = refs[:6]
    stats_ref, context_ref, grad_q_ref = refs[6:9]
    outs, refs = refs[9 : 9 + count], refs[9 + count :]
    k_ref, vt_ref, v_ref, kt_ref, gk_ref, gv_ref = refs
    rows = chunks[0].shape[1] // 2
    columns = slice(head * HEAD, (head + 1) * HEAD)
    split_chunks(chunks, 0, rows, (k_ref, v_ref, kt_ref, vt_ref), True)
    gk_ref[...] = jnp.zeros_like(gk_ref)
    gv_ref[...] = jnp.zeros_like(gv_ref)

    @tiles(qt_ref.shape[2] // tile)
    def _(j):
        here = tokens_of(j, tile)
        qt, gt = qt_ref[head, :, here], gt_ref[head, :, here]
        before = (
            stats_in[head, 0:1, here],
            stats_in[head, 1:2, here],
            context_in[head, :, here],
        )
        raised, _, top, total, context = raise_scores(k_ref[0], qt, vt_ref[0], before)
        rows_here = q_ref[0, here, columns], g_ref[0, here, columns]
        scale = 1.0 / total
        context = context * scale
        row_dot = jnp.sum(gt.astype(jnp.float32) * context, axis=0, keepdims=True)
        context_ref[0, :, here] = context
        stats_ref[0, 0:1, here] = top
        stats_ref[0, 1:2, here] = scale
        stats_ref[0, 2:3, here] = row_dot
        grad_q_ref[0, :, here] = gradients(
            raised, scale, row_dot, rows_here, gt, (v_ref, kt_ref, gk_ref, gv_ref), 0
        )

    store_chunks(outs, 0, rows, gk_ref, gv_ref, False)


def backward_kernel(back, counts, heads, joined, join, tile, *refs):
    refs = refs[back:]
    groups = [refs[4 * i : 4 * i + 4] for i in range(len(counts))]
    refs = refs[4 * len(counts) :]
    q_ref, g_ref, gt_ref, refs = refs[0], refs[1], refs[2], refs[3:]
    stats, refs = refs[:heads], refs[heads:]
    if joined:
        grads_in, refs = [refs[0].at[h : h + 1] for h in range(heads)], refs[1:]
    else:
        grads_in, refs = refs[:heads], refs[heads:]
    grad_q_ref, refs = refs[0], refs[1:]
    outs, refs = refs[: sum(counts)], refs[sum(counts) :]
    sums = [refs[i : i + 2] for i in range(0, len(refs), 2)]
    pair_rows = outs[0].shape[1]
    for ref in refs:
        ref[...] = jnp.zeros_like(ref)

    @tiles(gt_ref.shape[2] // tile)
    def _(j):
        here = tokens_of(j, tile)
        for h in range(heads):
            columns = slice(h * HEAD, (h + 1) * HEAD)
            rows_here = q_ref[0, here, columns], g_ref[0, here, columns]
            gt = gt_ref[h, :, here]
            top, scale, row_dot = (stats[h][0, i : i + 1, here] for i in range(3))
            grad_q = grads_in[h][0, :, here]
            for (low_ref, then_ref, v_ref, kt_ref), own in zip(groups, sums):
                shrunk = jnp.exp2((then_ref[h, 0:1, here] - top) * EXPONENT)
                raised = low_ref[h, :, here].astype(jnp.float32)
                grad_q = grad_q + gradients(
                    raised, scale * shrunk, row_dot, rows_here, gt, (v_ref, kt_ref, *own), h
                )
            grad_q_ref[h, :, here] = grad_q

    for count, (gk_ref, gv_ref) in zip(counts, sums):
        for h in range(heads):
            store_chunks(outs[:count], h, pair_rows // 2, gk_ref, gv_ref, join)
        outs = outs[count:]


def cost(heads, rows, tokens, matmuls):
    return pl.CostEstimate(
        flops=2 * matmuls * heads * rows * tokens * HEAD,
        bytes_accessed=heads * (rows + tokens) * HEAD * 8,
        transcendentals=heads * rows * tokens,
    )


def attend(groups, final_blocks, queries, upstream, send_back):
    heads, pair_rows, _ = groups[0][0].shape
    rows = pair_rows // 2
    enc_len = (sum(len(g) for g in groups) + len(final_blocks[0])) * rows
    tokens = queries.shape[1]
    qt, gt = turned(queries), turned(upstream)
    stats_shape = jax.ShapeDtypeStruct((heads, 8, tokens), jnp.float32)
    wide_shape = jax.ShapeDtypeStruct((heads, HEAD, tokens), jnp.float32)
    compiler_params = params(enc_len)

    def natural(count):
        return pltpu.VMEM((heads, count * rows, HEAD), jnp.bfloat16)

    def across(count, extra=0):
        return pltpu.VMEM((heads, HEAD + extra, count * rows), jnp.bfloat16)

    def sums(count):
        return pltpu.VMEM((heads, count * rows, HEAD), jnp.float32)

    def shapes_of(group):
        return [jax.ShapeDtypeStruct(c.shape, c.dtype) for c in group]

    state, kept = [], []
    for group in groups:
        count = len(group)
        low_shape = jax.ShapeDtypeStruct((heads, count * rows, tokens), jnp.bfloat16)
        v_shape = jax.ShapeDtypeStruct((heads, count * rows, HEAD), jnp.bfloat16)
        kt_shape = jax.ShapeDtypeStruct((heads, HEAD, count * rows), jnp.bfloat16)
        stats, context, *saved = pl.pallas_call(
            functools.partial(forward_kernel, count, not state, tile_of(count * rows, tokens)),
            out_shape=[stats_shape, wide_shape, low_shape, v_shape, kt_shape],
            in_specs=[VMEM] * (count + 1 + len(state)),
            out_specs=[VMEM] * 5,
            scratch_shapes=[natural(count), across(count, 16)],
            compiler_params=compiler_params,
            cost_estimate=cost(heads, count * rows, tokens, 2),
            name="forward",
        )(*group, qt, *state)
        state = [stats, context]
        kept.append((saved[0], stats, *saved[1:]))

    stats_one = jax.ShapeDtypeStruct((1, 8, tokens), jnp.float32)
    wide_one = jax.ShapeDtypeStruct((1, HEAD, tokens), jnp.float32)
    final, contexts, grads_q, back = [], [], [], []
    for h, group in enumerate(final_blocks):
        count = len(group)
        stats, context, grad_q, *grads = pl.pallas_call(
            functools.partial(turn_kernel, count, h, tile_of(count * rows, tokens)),
            out_shape=[stats_one, wide_one, wide_one] + shapes_of(group),
            in_specs=[VMEM] * (count + 6),
            out_specs=[VMEM] * (count + 3),
            scratch_shapes=[
                pltpu.VMEM((1, count * rows, HEAD), jnp.bfloat16),
                pltpu.VMEM((1, HEAD + 16, count * rows), jnp.bfloat16),
                pltpu.VMEM((1, count * rows, HEAD), jnp.bfloat16),
                pltpu.VMEM((1, HEAD, count * rows), jnp.bfloat16),
                pltpu.VMEM((1, count * rows, HEAD), jnp.float32),
                pltpu.VMEM((1, count * rows, HEAD), jnp.float32),
            ],
            compiler_params=compiler_params,
            cost_estimate=cost(1, count * rows, tokens, 6),
            name="turn",
        )(*group, queries, upstream, qt, gt, *state)
        final.append(stats)
        contexts.append(context)
        grads_q.append(grad_q)
        back += send_back(len(groups), grads)

    for part in (list(range(len(groups) - 1, 0, -1)), [0]):
        first = part != [0]
        counts = [len(groups[i]) for i in part]
        waits = [] if first else back
        operands = []
        for i in part:
            operands += kept[i]
        operands += [queries, upstream, gt, *final, *grads_q]
        outs = pl.pallas_call(
            functools.partial(
                backward_kernel,
                len(waits),
                counts,
                heads,
                not first,
                not first,
                tile_of(max(counts) * rows, tokens),
            ),
            out_shape=[wide_shape] + shapes_of(sum((groups[i] for i in part), [])),
            in_specs=[ANY] * len(waits) + [VMEM] * len(operands),
            out_specs=[VMEM] * (1 + sum(counts)),
            scratch_shapes=[sums(count) for count in counts for _ in range(2)],
            compiler_params=compiler_params,
            cost_estimate=cost(heads, sum(counts) * rows, tokens, 4),
            name="backward",
        )(*waits, *operands)
        grads_q, blocks = [outs[0]], list(outs[1:])
        for i in part:
            send_back(i, blocks[: len(groups[i])])
            blocks = blocks[len(groups[i]) :]
    return turned_back(contexts, queries.dtype), turned_back(grads_q, queries.dtype)


def shards(pairs, queries, upstream):
    _, rows, _, width = pairs.shape
    heads = queries.shape[2] // HEAD
    offsets = offset_groups()
    order = sum(offsets, [])
    first, final = len(offsets[0]), len(offsets[-1])
    packed = pack(pairs, order[:first], heads) + pack(pairs, order[first:], heads)
    packed = [block.reshape(heads, 2 * rows, HEAD) for block in packed]

    def send(block, offset, back):
        return lax.ppermute(block, AXES, route(offset, back))

    blocks = [send(b, o, False) for b, o in zip(packed[:-final], order)]
    groups = []
    for group in offsets[:-1]:
        groups.append(blocks[: len(group)])
        blocks = blocks[len(group) :]
    apart = reordered([[b] for b in packed[-final:]], False, apart=True)
    final_blocks = [
        [send(b, o, False) for b, o in zip(apart[h::heads], offsets[-1])] for h in range(heads)
    ]
    homes, returned = [], [[] for _ in offsets]

    def send_back(i, grads):
        sent = sorted(zip(offsets[i], grads), key=lambda s: (s[0][0] > 0) == (i == 1))
        back = [send(g, o, True) for o, g in sent]
        returned[i].append(back)
        if len(returned[i]) == 1:
            homes.extend(o for o, _ in sent)
        return back

    context, grad_query = attend(groups, final_blocks, queries, upstream, send_back)
    parts = [list(by_head) for by_head in zip(*returned[-1])]
    parts += [[b] for i in range(len(groups) - 1, 0, -1) for b in returned[i][0]]
    joined = reordered(parts, True)
    joined = [b.reshape(heads, rows, 2, HEAD) for b in list(joined) + returned[0][0]]
    return context, grad_query, unpack(joined, homes, width)


def solution(mesh):
    return jax.shard_map(
        shards,
        mesh=mesh,
        in_specs=(
            P("segment", ("seq", "tp"), None, None),
            P("segment", None, ("seq", "tp")),
            P("segment", None, ("seq", "tp")),
        ),
        out_specs=(
            P("segment", None, ("seq", "tp")),
            P("segment", None, ("seq", "tp")),
            P("segment", ("seq", "tp"), None, None),
        ),
        check_vma=False,
    )
```

```python
import functools

import jax
import jax.numpy as jnp
from jax import lax
from jax.experimental import pallas as pl
from jax.experimental.pallas import tpu as pltpu
from jax.sharding import PartitionSpec as P

HEAD = 128
AXES = ("segment", "seq", "tp")
FACTOR = HEAD**-0.5
EXPONENT = FACTOR * 1.4426950408889634
MIB = 1 << 20
ANY = pl.BlockSpec(memory_space=pl.ANY)
HBM = pl.BlockSpec(memory_space=pltpu.HBM)
VMEM = pl.BlockSpec(memory_space=pltpu.VMEM)


def offset_groups():
    seq_count = lax.axis_size("seq")
    tp_count = lax.axis_size("tp")
    near = [(0, dy) for dy in reversed(range(tp_count))]
    far = [(dz, dy) for dy in reversed(range(tp_count)) for dz in range(1, seq_count)]
    far.sort(key=lambda o: -abs(o[0] - seq_count / 2))
    eighth = max(1, (len(near) + len(far)) // 8)
    short, long = far[: -2 * eighth], far[-2 * eighth :]
    short = [((d, d), dy) for d, dy in sorted(short, key=lambda o: -o[1]) if d != 1]
    long = [((d, d), dy) for d, dy in long]
    half = len(short) // 2
    mixed = []
    for part, (_, dy) in zip((short[:half], short[half:]), near):
        mixed.append(part[:1] + [((1, 0), dy)] + part[1:] + [((0, 1), dy)])
    return [mixed[0], mixed[1], long[:eighth], long[eighth:]]


def group_at(offset):
    seq_count = lax.axis_size("seq")
    tp_count = lax.axis_size("tp")
    even, odd = offset[0]
    dz = even + (odd - even) * lax.rem(lax.axis_index("segment"), 2)
    z = lax.rem(lax.axis_index("seq") + dz, seq_count)
    y = lax.rem(lax.axis_index("tp") + offset[1], tp_count)
    return z * tp_count + y


def route(offset, back):
    segments, seq_count, tp_count = (lax.axis_size(a) for a in AXES)
    hops = []
    for s in range(segments):
        for z in range(seq_count):
            for y in range(tp_count):
                source = (s * seq_count + z) * tp_count + y
                s_to = (s + 1) % segments
                z_to = (z + offset[0][s % 2]) % seq_count
                y_to = (y + offset[1]) % tp_count
                target = (s_to * seq_count + z_to) * tp_count + y_to
                hops.append((target, source) if back else (source, target))
    return hops


def params(enc_len):
    return pltpu.CompilerParams(vmem_limit_bytes=(12 + enc_len * 36 // 4096) * MIB)


def pack(pairs, order, heads):
    _, rows, _, width = pairs.shape
    local = heads * HEAD

    def kernel(pairs_ref, *outs):
        @pl.loop(0, rows // 16)
        def _(r):
            here = pl.ds(pl.multiple_of(r * 16, 16), 16)
            for out, offset in zip(outs, order):
                base = group_at(offset) * local
                for h in range(heads):
                    column = pl.multiple_of(base + h * HEAD, HEAD)
                    out[h, here] = pairs_ref[0, here, :, pl.ds(column, HEAD)]

    return pl.pallas_call(
        kernel,
        out_shape=[jax.ShapeDtypeStruct((heads, rows, 2, HEAD), pairs.dtype)] * len(order),
        in_specs=[VMEM],
        out_specs=[VMEM] * len(order),
        compiler_params=pltpu.CompilerParams(vmem_limit_bytes=24 * MIB),
        name="pack",
    )(pairs)


def unpack(blocks, order, width):
    heads, rows, _, _ = blocks[0].shape
    local = heads * HEAD
    parts = 4 if rows % 64 == 0 else 1
    size = rows // parts

    def kernel(*refs):
        ins, out, held, sem = refs[: len(order)], refs[len(order)], refs[-2], refs[-1]

        def store(r):
            here = pl.ds(pl.multiple_of(r * size, size), size)
            return pltpu.make_async_copy(held.at[here], out.at[0, here], sem.at[r])

        @pl.loop(0, parts)
        def _(r):
            here = pl.ds(pl.multiple_of(r * size, size), size)
            for block, offset in zip(ins, order):
                base = group_at(offset) * local
                for h in range(heads):
                    column = pl.multiple_of(base + h * HEAD, HEAD)
                    held[here, :, pl.ds(column, HEAD)] = block[h, here]
            store(r).start()

        for r in range(parts):
            store(r).wait()

    return pl.pallas_call(
        kernel,
        out_shape=jax.ShapeDtypeStruct((1, rows, 2, width), blocks[0].dtype),
        in_specs=[VMEM] * len(order),
        out_specs=HBM,
        scratch_shapes=[
            pltpu.VMEM((rows, 2, width), blocks[0].dtype),
            pltpu.SemaphoreType.DMA((parts,)),
        ],
        compiler_params=pltpu.CompilerParams(vmem_limit_bytes=24 * MIB),
        name="unpack",
    )(*blocks)


def turned(rows):
    _, tokens, local = rows.shape
    heads = local // HEAD
    tile = 256 if tokens % 256 == 0 else tokens

    def kernel(rows_ref, out_ref):
        for h in range(heads):
            for j in range(tokens // tile):
                here = slice(j * tile, (j + 1) * tile)
                block = rows_ref[0, here, h * HEAD : (h + 1) * HEAD]
                out_ref[h, :, here] = block.astype(jnp.float32).T.astype(rows.dtype)

    return pl.pallas_call(
        kernel,
        out_shape=jax.ShapeDtypeStruct((heads, HEAD, tokens), rows.dtype),
        in_specs=[VMEM],
        out_specs=VMEM,
        compiler_params=pltpu.CompilerParams(vmem_limit_bytes=16 * MIB),
        name="turned",
    )(rows)


def tiles(count):
    def run(body):
        if count <= 2:
            for j in range(count):
                body(j)
        else:
            pl.loop(0, count)(body)

    return run


def tokens_of(j, tile):
    return pl.ds(j * tile if isinstance(j, int) else pl.multiple_of(j * tile, tile), tile)


def tile_of(rows, tokens):
    for parts in range(1, tokens // 256 + 1):
        if tokens % (256 * parts) == 0 and rows * (tokens // parts) * 4 <= 5 * MIB // 4:
            return tokens // parts
    return 256 if tokens % 256 == 0 else tokens


def turned_back(columns, dtype):
    heads, _, tokens = columns.shape
    tile = 256 if tokens % 256 == 0 else tokens

    def kernel(columns_ref, out_ref):
        for h in range(heads):
            for j in range(tokens // tile):
                here = slice(j * tile, (j + 1) * tile)
                block = columns_ref[h, :, here].T.astype(dtype)
                out_ref[0, here, h * HEAD : (h + 1) * HEAD] = block

    return pl.pallas_call(
        kernel,
        out_shape=jax.ShapeDtypeStruct((1, tokens, heads * HEAD), dtype),
        in_specs=[VMEM],
        out_specs=VMEM,
        compiler_params=pltpu.CompilerParams(vmem_limit_bytes=16 * MIB),
        name="turned_back",
    )(columns)


def dot(a, b, contract=((1,), (0,))):
    return lax.dot_general(a, b, (contract, ((), ())), preferred_element_type=jnp.float32)


def shuffle(rows, join):
    to = lax.broadcasted_iota(jnp.int32, (2 * rows, 2 * rows), 1 if join else 0)
    source = lax.broadcasted_iota(jnp.int32, (2 * rows, 2 * rows), 0 if join else 1)
    wanted = jnp.where(to < rows, 2 * to, 2 * (to - rows) + 1)
    return jnp.where(source == wanted, 1.0, 0.0).astype(jnp.bfloat16)


def reordered(blocks, join):
    heads, pair_rows, _ = blocks[0].shape

    def kernel(*refs):
        order = shuffle(pair_rows // 2, join)
        for block, out in zip(refs[: len(blocks)], refs[len(blocks) :]):
            for h in range(heads):
                out[h] = dot(order, block[h]).astype(out.dtype)

    return pl.pallas_call(
        kernel,
        out_shape=[jax.ShapeDtypeStruct(b.shape, b.dtype) for b in blocks],
        in_specs=[VMEM] * len(blocks),
        out_specs=[VMEM] * len(blocks),
        compiler_params=pltpu.CompilerParams(vmem_limit_bytes=24 * MIB),
        name="reordered",
    )(*blocks)


def split_chunks(chunks, h, rows, refs, done):
    k_ref, v_ref, kt_ref, vt_ref = refs
    split = None if done else shuffle(rows, False)
    for i, chunk in enumerate(chunks):
        both = chunk[h].astype(jnp.float32) if done else dot(split, chunk[h])
        here = slice(i * rows, (i + 1) * rows)
        keys, values = both[:rows], both[rows:]
        k_ref[h, here, :] = keys.astype(jnp.bfloat16)
        v_ref[h, here, :] = values.astype(jnp.bfloat16)
        kt_ref[h, :, here] = keys.T.astype(jnp.bfloat16)
        vt_ref[h, :HEAD, here] = values.T.astype(jnp.bfloat16)
    tail = (vt_ref.shape[1] - HEAD, vt_ref.shape[2])
    vt_ref[h, HEAD:, :] = jnp.ones(tail, jnp.bfloat16)


def store_chunks(outs, h, rows, gk_ref, gv_ref, join):
    order = shuffle(rows, True) if join else None
    for i, out in enumerate(outs):
        here = slice(i * rows, (i + 1) * rows)
        both = jnp.concatenate([gk_ref[h, here, :] * FACTOR, gv_ref[h, here, :]], axis=0)
        both = both.astype(jnp.bfloat16)
        out[h] = dot(order, both).astype(jnp.bfloat16) if join else both


def raise_scores(keys, qt, values_t, before):
    scores = dot(keys, qt)
    top = jnp.max(scores, axis=0, keepdims=True)
    if before is not None:
        top = jnp.maximum(top, before[0])
    raised = jnp.exp2((scores - top) * EXPONENT)
    low = raised.astype(jnp.bfloat16)
    summed = dot(values_t, low)
    total, context = summed[HEAD : HEAD + 1], summed[:HEAD]
    if before is not None:
        shrink = jnp.exp2((before[0] - top) * EXPONENT)
        total = total + before[1] * shrink
        context = context + before[2] * shrink
    return raised, low, top, total, context


def forward_kernel(count, first, tile, *refs):
    chunks, refs = refs[:count], refs[count:]
    qt_ref, refs = refs[0], refs[1:]
    if not first:
        stats_in, context_in, refs = refs[0], refs[1], refs[2:]
    stats_ref, context_ref, low_ref, v_ref, kt_ref, k_ref, vt_ref = refs
    heads, pair_rows, _ = chunks[0].shape
    for h in range(heads):
        split_chunks(chunks, h, pair_rows // 2, (k_ref, v_ref, kt_ref, vt_ref), False)

    @tiles(qt_ref.shape[2] // tile)
    def _(j):
        here = tokens_of(j, tile)
        for h in range(heads):
            before = None
            if not first:
                before = (stats_in[h, 0:1, here], stats_in[h, 1:2, here], context_in[h, :, here])
            _, low, top, total, context = raise_scores(
                k_ref[h], qt_ref[h, :, here], vt_ref[h], before
            )
            low_ref[h, :, here] = low
            stats_ref[h, 0:1, here] = top
            stats_ref[h, 1:2, here] = total
            context_ref[h, :, here] = context


def gradients(raised, scale, row_dot, rows, gt, refs, h):
    v_ref, kt_ref, gk_ref, gv_ref = refs
    query_rows, grad_rows = rows
    weights = raised * scale
    grad_weights = dot(v_ref[h], gt)
    grad_scores = (weights * (grad_weights - row_dot)).astype(jnp.bfloat16)
    gv_ref[h] += dot(weights.astype(jnp.bfloat16), grad_rows)
    gk_ref[h] += dot(grad_scores, query_rows)
    return dot(kt_ref[h], grad_scores) * FACTOR


def turn_kernel(count, tile, *refs):
    chunks, refs = refs[:count], refs[count:]
    q_ref, g_ref, qt_ref, gt_ref, stats_in, context_in = refs[:6]
    stats_ref, context_ref, grad_q_ref = refs[6:9]
    outs, refs = refs[9 : 9 + count], refs[9 + count :]
    k_ref, vt_ref, v_ref, kt_ref, gk_ref, gv_ref = refs
    heads, pair_rows, _ = chunks[0].shape
    rows = pair_rows // 2
    for h in range(heads):
        split_chunks(chunks, h, rows, (k_ref, v_ref, kt_ref, vt_ref), True)
    gk_ref[...] = jnp.zeros_like(gk_ref)
    gv_ref[...] = jnp.zeros_like(gv_ref)

    @tiles(qt_ref.shape[2] // tile)
    def _(j):
        here = tokens_of(j, tile)
        for h in range(heads):
            qt, gt = qt_ref[h, :, here], gt_ref[h, :, here]
            before = (stats_in[h, 0:1, here], stats_in[h, 1:2, here], context_in[h, :, here])
            raised, _, top, total, context = raise_scores(k_ref[h], qt, vt_ref[h], before)
            columns = slice(h * HEAD, (h + 1) * HEAD)
            rows_here = q_ref[0, here, columns], g_ref[0, here, columns]
            scale = 1.0 / total
            context = context * scale
            row_dot = jnp.sum(gt.astype(jnp.float32) * context, axis=0, keepdims=True)
            context_ref[h, :, here] = context
            stats_ref[h, 0:1, here] = top
            stats_ref[h, 1:2, here] = scale
            stats_ref[h, 2:3, here] = row_dot
            grad_q_ref[h, :, here] = gradients(
                raised, scale, row_dot, rows_here, gt, (v_ref, kt_ref, gk_ref, gv_ref), h
            )

    for h in range(heads):
        store_chunks(outs, h, rows, gk_ref, gv_ref, False)


def backward_kernel(back, counts, join, tile, *refs):
    refs = refs[back:]
    groups = [refs[4 * i : 4 * i + 4] for i in range(len(counts))]
    refs = refs[4 * len(counts) :]
    q_ref, g_ref, gt_ref, stats_ref, grad_q_in, grad_q_ref = refs[:6]
    outs, refs = refs[6 : 6 + sum(counts)], refs[6 + sum(counts) :]
    sums = [refs[i : i + 2] for i in range(0, len(refs), 2)]
    heads, pair_rows, _ = outs[0].shape
    for ref in refs:
        ref[...] = jnp.zeros_like(ref)

    @tiles(gt_ref.shape[2] // tile)
    def _(j):
        here = tokens_of(j, tile)
        for h in range(heads):
            columns = slice(h * HEAD, (h + 1) * HEAD)
            rows_here = q_ref[0, here, columns], g_ref[0, here, columns]
            gt = gt_ref[h, :, here]
            top, scale, row_dot = (stats_ref[h, i : i + 1, here] for i in range(3))
            grad_q = grad_q_in[h, :, here]
            for (low_ref, then_ref, v_ref, kt_ref), own in zip(groups, sums):
                shrunk = jnp.exp2((then_ref[h, 0:1, here] - top) * EXPONENT)
                raised = low_ref[h, :, here].astype(jnp.float32)
                grad_q = grad_q + gradients(
                    raised, scale * shrunk, row_dot, rows_here, gt, (v_ref, kt_ref, *own), h
                )
            grad_q_ref[h, :, here] = grad_q

    for count, (gk_ref, gv_ref) in zip(counts, sums):
        for h in range(heads):
            store_chunks(outs[:count], h, pair_rows // 2, gk_ref, gv_ref, join)
        outs = outs[count:]


def cost(heads, rows, tokens, matmuls):
    return pl.CostEstimate(
        flops=2 * matmuls * heads * rows * tokens * HEAD,
        bytes_accessed=heads * (rows + tokens) * HEAD * 8,
        transcendentals=heads * rows * tokens,
    )


def attend(groups, queries, upstream, send_back):
    heads, pair_rows, _ = groups[0][0].shape
    rows = pair_rows // 2
    enc_len = sum(len(g) for g in groups) * rows
    tokens = queries.shape[1]
    qt, gt = turned(queries), turned(upstream)
    stats_shape = jax.ShapeDtypeStruct((heads, 8, tokens), jnp.float32)
    wide_shape = jax.ShapeDtypeStruct((heads, HEAD, tokens), jnp.float32)
    compiler_params = params(enc_len)

    def natural(count):
        return pltpu.VMEM((heads, count * rows, HEAD), jnp.bfloat16)

    def across(count, extra=0):
        return pltpu.VMEM((heads, HEAD + extra, count * rows), jnp.bfloat16)

    def sums(count):
        return pltpu.VMEM((heads, count * rows, HEAD), jnp.float32)

    def shapes_of(group):
        return [jax.ShapeDtypeStruct(c.shape, c.dtype) for c in group]

    state, kept = [], []
    for group in groups[:-1]:
        count = len(group)
        low_shape = jax.ShapeDtypeStruct((heads, count * rows, tokens), jnp.bfloat16)
        v_shape = jax.ShapeDtypeStruct((heads, count * rows, HEAD), jnp.bfloat16)
        kt_shape = jax.ShapeDtypeStruct((heads, HEAD, count * rows), jnp.bfloat16)
        stats, context, *saved = pl.pallas_call(
            functools.partial(forward_kernel, count, not state, tile_of(count * rows, tokens)),
            out_shape=[stats_shape, wide_shape, low_shape, v_shape, kt_shape],
            in_specs=[VMEM] * (count + 1 + len(state)),
            out_specs=[VMEM] * 5,
            scratch_shapes=[natural(count), across(count, 16)],
            compiler_params=compiler_params,
            cost_estimate=cost(heads, count * rows, tokens, 2),
            name="forward",
        )(*group, qt, *state)
        state = [stats, context]
        kept.append((saved[0], stats, *saved[1:]))

    group, count = groups[-1], len(groups[-1])
    final, context, grad_q, *grads = pl.pallas_call(
        functools.partial(turn_kernel, count, tile_of(count * rows, tokens)),
        out_shape=[stats_shape, wide_shape, wide_shape] + shapes_of(group),
        in_specs=[VMEM] * (count + 6),
        out_specs=[VMEM] * (count + 3),
        scratch_shapes=[natural(count), across(count, 16), natural(count), across(count)]
        + [sums(count)] * 2,
        compiler_params=compiler_params,
        cost_estimate=cost(heads, count * rows, tokens, 6),
        name="turn",
    )(*group, queries, upstream, qt, gt, *state)
    returned = [send_back(len(groups) - 1, grads)]

    for part in (list(range(len(groups) - 2, 0, -1)), [0]):
        first = part != [0]
        counts = [len(groups[i]) for i in part]
        back = [] if first else returned[0]
        operands = []
        for i in part:
            operands += kept[i]
        operands += [queries, upstream, gt, final, grad_q]
        outs = pl.pallas_call(
            functools.partial(
                backward_kernel, len(back), counts, not first, tile_of(max(counts) * rows, tokens)
            ),
            out_shape=[wide_shape] + shapes_of(sum((groups[i] for i in part), [])),
            in_specs=[ANY] * len(back) + [VMEM] * len(operands),
            out_specs=[VMEM] * (1 + sum(counts)),
            scratch_shapes=[sums(count) for count in counts for _ in range(2)],
            compiler_params=compiler_params,
            cost_estimate=cost(heads, sum(counts) * rows, tokens, 4),
            name="backward",
        )(*back, *operands)
        grad_q, blocks = outs[0], list(outs[1:])
        for i in part:
            returned.append(send_back(i, blocks[: len(groups[i])]))
            blocks = blocks[len(groups[i]) :]
    return turned_back(context, queries.dtype), turned_back(grad_q, queries.dtype)


def shards(pairs, queries, upstream):
    _, rows, _, width = pairs.shape
    heads = queries.shape[2] // HEAD
    offsets = offset_groups()
    order = sum(offsets, [])
    blocks = []
    first = len(offsets[0])
    packed = pack(pairs, order[:first], heads) + pack(pairs, order[first:], heads)
    packed = [block.reshape(heads, 2 * rows, HEAD) for block in packed]
    final = len(offsets[-1])
    packed[-final:] = reordered(packed[-final:], False)
    for offset, block in zip(order, packed):
        blocks.append(lax.ppermute(block, AXES, route(offset, False)))
    groups = []
    for group in offsets:
        groups.append(blocks[: len(group)])
        blocks = blocks[len(group) :]
    homes, returned = [], []

    def send_back(i, grads):
        back = [lax.ppermute(g, AXES, route(o, True)) for o, g in zip(offsets[i], grads)]
        homes.extend(offsets[i])
        returned.append(back)
        return back

    context, grad_query = attend(groups, queries, upstream, send_back)
    early = reordered(sum(returned[:-1], []), True)
    returned = [b.reshape(heads, rows, 2, HEAD) for b in list(early) + returned[-1]]
    return context, grad_query, unpack(returned, homes, width)


def solution(mesh):
    return jax.shard_map(
        shards,
        mesh=mesh,
        in_specs=(
            P("segment", ("seq", "tp"), None, None),
            P("segment", None, ("seq", "tp")),
            P("segment", None, ("seq", "tp")),
        ),
        out_specs=(
            P("segment", None, ("seq", "tp")),
            P("segment", None, ("seq", "tp")),
            P("segment", ("seq", "tp"), None, None),
        ),
        check_vma=False,
    )
```

```python
import functools

import jax
import jax.numpy as jnp
from jax import lax
from jax.experimental import pallas as pl
from jax.experimental.pallas import tpu as pltpu
from jax.sharding import PartitionSpec as P

HEAD = 128
AXES = ("segment", "seq", "tp")
FACTOR = HEAD**-0.5
EXPONENT = FACTOR * 1.4426950408889634
MIB = 1 << 20
ANY = pl.BlockSpec(memory_space=pl.ANY)
HBM = pl.BlockSpec(memory_space=pltpu.HBM)
VMEM = pl.BlockSpec(memory_space=pltpu.VMEM)


def offset_groups():
    seq_count = lax.axis_size("seq")
    tp_count = lax.axis_size("tp")
    near = [(0, dy) for dy in reversed(range(tp_count))]
    far = [(dz, dy) for dy in reversed(range(tp_count)) for dz in range(1, seq_count)]
    far.sort(key=lambda o: -abs(o[0] - seq_count / 2))
    eighth = max(1, (len(near) + len(far)) // 8)
    short, long = far[: -2 * eighth], far[-2 * eighth :]
    short.sort(key=lambda o: -o[1])
    half = len(short) // 2
    return [
        short[1:half] + short[:1] + near[:1],
        short[half:] + near[1:],
        long[:eighth],
        long[eighth:],
    ]


def group_at(offset):
    seq_count = lax.axis_size("seq")
    tp_count = lax.axis_size("tp")
    z = lax.rem(lax.axis_index("seq") + offset[0], seq_count)
    y = lax.rem(lax.axis_index("tp") + offset[1], tp_count)
    return z * tp_count + y


def route(offset, back):
    segments, seq_count, tp_count = (lax.axis_size(a) for a in AXES)
    hops = []
    for s in range(segments):
        for z in range(seq_count):
            for y in range(tp_count):
                source = (s * seq_count + z) * tp_count + y
                s_to = (s + 1) % segments
                z_to = (z + offset[0]) % seq_count
                y_to = (y + offset[1]) % tp_count
                target = (s_to * seq_count + z_to) * tp_count + y_to
                hops.append((target, source) if back else (source, target))
    return hops


def params(enc_len):
    return pltpu.CompilerParams(vmem_limit_bytes=(12 + enc_len * 36 // 4096) * MIB)


def pack(pairs, order, heads):
    _, rows, _, width = pairs.shape
    local = heads * HEAD

    def kernel(pairs_ref, *outs):
        @pl.loop(0, rows // 16)
        def _(r):
            here = pl.ds(pl.multiple_of(r * 16, 16), 16)
            for out, offset in zip(outs, order):
                base = group_at(offset) * local
                for h in range(heads):
                    column = pl.multiple_of(base + h * HEAD, HEAD)
                    out[h, here] = pairs_ref[0, here, :, pl.ds(column, HEAD)]

    return pl.pallas_call(
        kernel,
        out_shape=[jax.ShapeDtypeStruct((heads, rows, 2, HEAD), pairs.dtype)] * len(order),
        in_specs=[VMEM],
        out_specs=[VMEM] * len(order),
        compiler_params=pltpu.CompilerParams(vmem_limit_bytes=24 * MIB),
        name="pack",
    )(pairs)


def unpack(blocks, order, width):
    heads, rows, _, _ = blocks[0].shape
    local = heads * HEAD
    parts = 4 if rows % 64 == 0 else 1
    size = rows // parts

    def kernel(*refs):
        ins, out, held, sem = refs[: len(order)], refs[len(order)], refs[-2], refs[-1]

        def store(r):
            here = pl.ds(pl.multiple_of(r * size, size), size)
            return pltpu.make_async_copy(held.at[here], out.at[0, here], sem.at[r])

        @pl.loop(0, parts)
        def _(r):
            here = pl.ds(pl.multiple_of(r * size, size), size)
            for block, offset in zip(ins, order):
                base = group_at(offset) * local
                for h in range(heads):
                    column = pl.multiple_of(base + h * HEAD, HEAD)
                    held[here, :, pl.ds(column, HEAD)] = block[h, here]
            store(r).start()

        for r in range(parts):
            store(r).wait()

    return pl.pallas_call(
        kernel,
        out_shape=jax.ShapeDtypeStruct((1, rows, 2, width), blocks[0].dtype),
        in_specs=[VMEM] * len(order),
        out_specs=HBM,
        scratch_shapes=[
            pltpu.VMEM((rows, 2, width), blocks[0].dtype),
            pltpu.SemaphoreType.DMA((parts,)),
        ],
        compiler_params=pltpu.CompilerParams(vmem_limit_bytes=24 * MIB),
        name="unpack",
    )(*blocks)


def turned(rows):
    _, tokens, local = rows.shape
    heads = local // HEAD
    tile = 256 if tokens % 256 == 0 else tokens

    def kernel(rows_ref, out_ref):
        for h in range(heads):
            for j in range(tokens // tile):
                here = slice(j * tile, (j + 1) * tile)
                block = rows_ref[0, here, h * HEAD : (h + 1) * HEAD]
                out_ref[h, :, here] = block.astype(jnp.float32).T.astype(rows.dtype)

    return pl.pallas_call(
        kernel,
        out_shape=jax.ShapeDtypeStruct((heads, HEAD, tokens), rows.dtype),
        in_specs=[VMEM],
        out_specs=VMEM,
        compiler_params=pltpu.CompilerParams(vmem_limit_bytes=16 * MIB),
        name="turned",
    )(rows)


def tiles(count):
    def run(body):
        if count <= 2:
            for j in range(count):
                body(j)
        else:
            pl.loop(0, count)(body)

    return run


def tokens_of(j, tile):
    return pl.ds(j * tile if isinstance(j, int) else pl.multiple_of(j * tile, tile), tile)


def tile_of(rows, tokens):
    for parts in range(1, tokens // 256 + 1):
        if tokens % (256 * parts) == 0 and rows * (tokens // parts) * 4 <= 5 * MIB // 4:
            return tokens // parts
    return 256 if tokens % 256 == 0 else tokens


def turned_back(columns, dtype):
    heads, _, tokens = columns.shape
    tile = 256 if tokens % 256 == 0 else tokens

    def kernel(columns_ref, out_ref):
        for h in range(heads):
            for j in range(tokens // tile):
                here = slice(j * tile, (j + 1) * tile)
                block = columns_ref[h, :, here].T.astype(dtype)
                out_ref[0, here, h * HEAD : (h + 1) * HEAD] = block

    return pl.pallas_call(
        kernel,
        out_shape=jax.ShapeDtypeStruct((1, tokens, heads * HEAD), dtype),
        in_specs=[VMEM],
        out_specs=VMEM,
        compiler_params=pltpu.CompilerParams(vmem_limit_bytes=16 * MIB),
        name="turned_back",
    )(columns)


def dot(a, b, contract=((1,), (0,))):
    return lax.dot_general(a, b, (contract, ((), ())), preferred_element_type=jnp.float32)


def shuffle(rows, join):
    to = lax.broadcasted_iota(jnp.int32, (2 * rows, 2 * rows), 1 if join else 0)
    source = lax.broadcasted_iota(jnp.int32, (2 * rows, 2 * rows), 0 if join else 1)
    wanted = jnp.where(to < rows, 2 * to, 2 * (to - rows) + 1)
    return jnp.where(source == wanted, 1.0, 0.0).astype(jnp.bfloat16)


def reordered(blocks, join):
    heads, pair_rows, _ = blocks[0].shape

    def kernel(*refs):
        order = shuffle(pair_rows // 2, join)
        for block, out in zip(refs[: len(blocks)], refs[len(blocks) :]):
            for h in range(heads):
                out[h] = dot(order, block[h]).astype(out.dtype)

    return pl.pallas_call(
        kernel,
        out_shape=[jax.ShapeDtypeStruct(b.shape, b.dtype) for b in blocks],
        in_specs=[VMEM] * len(blocks),
        out_specs=[VMEM] * len(blocks),
        compiler_params=pltpu.CompilerParams(vmem_limit_bytes=24 * MIB),
        name="reordered",
    )(*blocks)


def split_chunks(chunks, h, rows, refs, done):
    k_ref, v_ref, kt_ref, vt_ref = refs
    split = None if done else shuffle(rows, False)
    for i, chunk in enumerate(chunks):
        both = chunk[h].astype(jnp.float32) if done else dot(split, chunk[h])
        here = slice(i * rows, (i + 1) * rows)
        keys, values = both[:rows], both[rows:]
        k_ref[h, here, :] = keys.astype(jnp.bfloat16)
        v_ref[h, here, :] = values.astype(jnp.bfloat16)
        kt_ref[h, :, here] = keys.T.astype(jnp.bfloat16)
        vt_ref[h, :HEAD, here] = values.T.astype(jnp.bfloat16)
    tail = (vt_ref.shape[1] - HEAD, vt_ref.shape[2])
    vt_ref[h, HEAD:, :] = jnp.ones(tail, jnp.bfloat16)


def store_chunks(outs, h, rows, gk_ref, gv_ref, join):
    order = shuffle(rows, True) if join else None
    for i, out in enumerate(outs):
        here = slice(i * rows, (i + 1) * rows)
        both = jnp.concatenate([gk_ref[h, here, :] * FACTOR, gv_ref[h, here, :]], axis=0)
        both = both.astype(jnp.bfloat16)
        out[h] = dot(order, both).astype(jnp.bfloat16) if join else both


def raise_scores(keys, qt, values_t, before):
    scores = dot(keys, qt)
    top = jnp.max(scores, axis=0, keepdims=True)
    if before is not None:
        top = jnp.maximum(top, before[0])
    raised = jnp.exp2((scores - top) * EXPONENT)
    low = raised.astype(jnp.bfloat16)
    summed = dot(values_t, low)
    total, context = summed[HEAD : HEAD + 1], summed[:HEAD]
    if before is not None:
        shrink = jnp.exp2((before[0] - top) * EXPONENT)
        total = total + before[1] * shrink
        context = context + before[2] * shrink
    return raised, low, top, total, context


def forward_kernel(count, first, tile, *refs):
    chunks, refs = refs[:count], refs[count:]
    qt_ref, refs = refs[0], refs[1:]
    if not first:
        stats_in, context_in, refs = refs[0], refs[1], refs[2:]
    stats_ref, context_ref, low_ref, v_ref, kt_ref, k_ref, vt_ref = refs
    heads, pair_rows, _ = chunks[0].shape
    for h in range(heads):
        split_chunks(chunks, h, pair_rows // 2, (k_ref, v_ref, kt_ref, vt_ref), False)

    @tiles(qt_ref.shape[2] // tile)
    def _(j):
        here = tokens_of(j, tile)
        for h in range(heads):
            before = None
            if not first:
                before = (stats_in[h, 0:1, here], stats_in[h, 1:2, here], context_in[h, :, here])
            _, low, top, total, context = raise_scores(
                k_ref[h], qt_ref[h, :, here], vt_ref[h], before
            )
            low_ref[h, :, here] = low
            stats_ref[h, 0:1, here] = top
            stats_ref[h, 1:2, here] = total
            context_ref[h, :, here] = context


def gradients(raised, scale, row_dot, rows, gt, refs, h):
    v_ref, kt_ref, gk_ref, gv_ref = refs
    query_rows, grad_rows = rows
    weights = raised * scale
    grad_weights = dot(v_ref[h], gt)
    grad_scores = (weights * (grad_weights - row_dot)).astype(jnp.bfloat16)
    gv_ref[h] += dot(weights.astype(jnp.bfloat16), grad_rows)
    gk_ref[h] += dot(grad_scores, query_rows)
    return dot(kt_ref[h], grad_scores) * FACTOR


def turn_kernel(count, tile, *refs):
    chunks, refs = refs[:count], refs[count:]
    q_ref, g_ref, qt_ref, gt_ref, stats_in, context_in = refs[:6]
    stats_ref, context_ref, grad_q_ref = refs[6:9]
    outs, refs = refs[9 : 9 + count], refs[9 + count :]
    k_ref, vt_ref, v_ref, kt_ref, gk_ref, gv_ref = refs
    heads, pair_rows, _ = chunks[0].shape
    rows = pair_rows // 2
    for h in range(heads):
        split_chunks(chunks, h, rows, (k_ref, v_ref, kt_ref, vt_ref), True)
    gk_ref[...] = jnp.zeros_like(gk_ref)
    gv_ref[...] = jnp.zeros_like(gv_ref)

    @tiles(qt_ref.shape[2] // tile)
    def _(j):
        here = tokens_of(j, tile)
        for h in range(heads):
            qt, gt = qt_ref[h, :, here], gt_ref[h, :, here]
            before = (stats_in[h, 0:1, here], stats_in[h, 1:2, here], context_in[h, :, here])
            raised, _, top, total, context = raise_scores(k_ref[h], qt, vt_ref[h], before)
            columns = slice(h * HEAD, (h + 1) * HEAD)
            rows_here = q_ref[0, here, columns], g_ref[0, here, columns]
            scale = 1.0 / total
            context = context * scale
            row_dot = jnp.sum(gt.astype(jnp.float32) * context, axis=0, keepdims=True)
            context_ref[h, :, here] = context
            stats_ref[h, 0:1, here] = top
            stats_ref[h, 1:2, here] = scale
            stats_ref[h, 2:3, here] = row_dot
            grad_q_ref[h, :, here] = gradients(
                raised, scale, row_dot, rows_here, gt, (v_ref, kt_ref, gk_ref, gv_ref), h
            )

    for h in range(heads):
        store_chunks(outs, h, rows, gk_ref, gv_ref, False)


def backward_kernel(back, counts, join, tile, *refs):
    refs = refs[back:]
    groups = [refs[4 * i : 4 * i + 4] for i in range(len(counts))]
    refs = refs[4 * len(counts) :]
    q_ref, g_ref, gt_ref, stats_ref, grad_q_in, grad_q_ref = refs[:6]
    outs, refs = refs[6 : 6 + sum(counts)], refs[6 + sum(counts) :]
    sums = [refs[i : i + 2] for i in range(0, len(refs), 2)]
    heads, pair_rows, _ = outs[0].shape
    for ref in refs:
        ref[...] = jnp.zeros_like(ref)

    @tiles(gt_ref.shape[2] // tile)
    def _(j):
        here = tokens_of(j, tile)
        for h in range(heads):
            columns = slice(h * HEAD, (h + 1) * HEAD)
            rows_here = q_ref[0, here, columns], g_ref[0, here, columns]
            gt = gt_ref[h, :, here]
            top, scale, row_dot = (stats_ref[h, i : i + 1, here] for i in range(3))
            grad_q = grad_q_in[h, :, here]
            for (low_ref, then_ref, v_ref, kt_ref), own in zip(groups, sums):
                shrunk = jnp.exp2((then_ref[h, 0:1, here] - top) * EXPONENT)
                raised = low_ref[h, :, here].astype(jnp.float32)
                grad_q = grad_q + gradients(
                    raised, scale * shrunk, row_dot, rows_here, gt, (v_ref, kt_ref, *own), h
                )
            grad_q_ref[h, :, here] = grad_q

    for count, (gk_ref, gv_ref) in zip(counts, sums):
        for h in range(heads):
            store_chunks(outs[:count], h, pair_rows // 2, gk_ref, gv_ref, join)
        outs = outs[count:]


def cost(heads, rows, tokens, matmuls):
    return pl.CostEstimate(
        flops=2 * matmuls * heads * rows * tokens * HEAD,
        bytes_accessed=heads * (rows + tokens) * HEAD * 8,
        transcendentals=heads * rows * tokens,
    )


def attend(groups, queries, upstream, send_back):
    heads, pair_rows, _ = groups[0][0].shape
    rows = pair_rows // 2
    enc_len = sum(len(g) for g in groups) * rows
    tokens = queries.shape[1]
    qt, gt = turned(queries), turned(upstream)
    stats_shape = jax.ShapeDtypeStruct((heads, 8, tokens), jnp.float32)
    wide_shape = jax.ShapeDtypeStruct((heads, HEAD, tokens), jnp.float32)
    compiler_params = params(enc_len)

    def natural(count):
        return pltpu.VMEM((heads, count * rows, HEAD), jnp.bfloat16)

    def across(count, extra=0):
        return pltpu.VMEM((heads, HEAD + extra, count * rows), jnp.bfloat16)

    def sums(count):
        return pltpu.VMEM((heads, count * rows, HEAD), jnp.float32)

    def shapes_of(group):
        return [jax.ShapeDtypeStruct(c.shape, c.dtype) for c in group]

    state, kept = [], []
    for group in groups[:-1]:
        count = len(group)
        low_shape = jax.ShapeDtypeStruct((heads, count * rows, tokens), jnp.bfloat16)
        v_shape = jax.ShapeDtypeStruct((heads, count * rows, HEAD), jnp.bfloat16)
        kt_shape = jax.ShapeDtypeStruct((heads, HEAD, count * rows), jnp.bfloat16)
        stats, context, *saved = pl.pallas_call(
            functools.partial(forward_kernel, count, not state, tile_of(count * rows, tokens)),
            out_shape=[stats_shape, wide_shape, low_shape, v_shape, kt_shape],
            in_specs=[VMEM] * (count + 1 + len(state)),
            out_specs=[VMEM] * 5,
            scratch_shapes=[natural(count), across(count, 16)],
            compiler_params=compiler_params,
            cost_estimate=cost(heads, count * rows, tokens, 2),
            name="forward",
        )(*group, qt, *state)
        state = [stats, context]
        kept.append((saved[0], stats, *saved[1:]))

    group, count = groups[-1], len(groups[-1])
    final, context, grad_q, *grads = pl.pallas_call(
        functools.partial(turn_kernel, count, tile_of(count * rows, tokens)),
        out_shape=[stats_shape, wide_shape, wide_shape] + shapes_of(group),
        in_specs=[VMEM] * (count + 6),
        out_specs=[VMEM] * (count + 3),
        scratch_shapes=[natural(count), across(count, 16), natural(count), across(count)]
        + [sums(count)] * 2,
        compiler_params=compiler_params,
        cost_estimate=cost(heads, count * rows, tokens, 6),
        name="turn",
    )(*group, queries, upstream, qt, gt, *state)
    returned = [send_back(len(groups) - 1, grads)]

    for part in (list(range(len(groups) - 2, 0, -1)), [0]):
        first = part != [0]
        counts = [len(groups[i]) for i in part]
        back = [] if first else returned[0]
        operands = []
        for i in part:
            operands += kept[i]
        operands += [queries, upstream, gt, final, grad_q]
        outs = pl.pallas_call(
            functools.partial(
                backward_kernel, len(back), counts, not first, tile_of(max(counts) * rows, tokens)
            ),
            out_shape=[wide_shape] + shapes_of(sum((groups[i] for i in part), [])),
            in_specs=[ANY] * len(back) + [VMEM] * len(operands),
            out_specs=[VMEM] * (1 + sum(counts)),
            scratch_shapes=[sums(count) for count in counts for _ in range(2)],
            compiler_params=compiler_params,
            cost_estimate=cost(heads, sum(counts) * rows, tokens, 4),
            name="backward",
        )(*back, *operands)
        grad_q, blocks = outs[0], list(outs[1:])
        for i in part:
            returned.append(send_back(i, blocks[: len(groups[i])]))
            blocks = blocks[len(groups[i]) :]
    return turned_back(context, queries.dtype), turned_back(grad_q, queries.dtype)


def shards(pairs, queries, upstream):
    _, rows, _, width = pairs.shape
    heads = queries.shape[2] // HEAD
    offsets = offset_groups()
    order = sum(offsets, [])
    blocks = []
    first = len(offsets[0])
    packed = pack(pairs, order[:first], heads) + pack(pairs, order[first:], heads)
    packed = [block.reshape(heads, 2 * rows, HEAD) for block in packed]
    final = len(offsets[-1])
    packed[-final:] = reordered(packed[-final:], False)
    for offset, block in zip(order, packed):
        blocks.append(lax.ppermute(block, AXES, route(offset, False)))
    groups = []
    for group in offsets:
        groups.append(blocks[: len(group)])
        blocks = blocks[len(group) :]
    homes, returned = [], []

    def send_back(i, grads):
        sent = sorted(zip(offsets[i], grads), key=lambda s: s[0][0] > 0)
        back = [lax.ppermute(g, AXES, route(o, True)) for o, g in sent]
        homes.extend(o for o, _ in sent)
        returned.append(back)
        return back

    context, grad_query = attend(groups, queries, upstream, send_back)
    early = reordered(sum(returned[:-1], []), True)
    returned = [b.reshape(heads, rows, 2, HEAD) for b in list(early) + returned[-1]]
    return context, grad_query, unpack(returned, homes, width)


def solution(mesh):
    return jax.shard_map(
        shards,
        mesh=mesh,
        in_specs=(
            P("segment", ("seq", "tp"), None, None),
            P("segment", None, ("seq", "tp")),
            P("segment", None, ("seq", "tp")),
        ),
        out_specs=(
            P("segment", None, ("seq", "tp")),
            P("segment", None, ("seq", "tp")),
            P("segment", ("seq", "tp"), None, None),
        ),
        check_vma=False,
    )
```
